32 devices in a mesh: dp: 8 (over y, x, core), kern: 4 (over z).
Axes of the slice: x: 2, y: 2, z: 4, core: 2. Of those that a mesh axis runs over, the one named last changes fastest.
Arguments:
- tokens: bfloat16 [16, 2048, 768], P('dp', 'kern'), may hold values from -6 to 6
- cotangent: bfloat16 [16, 2048, 768], P('dp', 'kern'), may hold values from -6 to 6
- in_weight: bfloat16 [768, 1536], replicated, may hold values from -0.21875 to 0.21875
- out_weight: bfloat16 [768, 768], replicated, may hold values from -0.4375 to 0.4375
- up_weight: bfloat16 [768, 3072], replicated, may hold values from -0.21875 to 0.21875
- down_weight: bfloat16 [3072, 768], replicated, may hold values from -0.15625 to 0.15625
- first_gain: float32 [768], replicated, may hold values from 0.1 to 1.9
- second_gain: float32 [768], replicated, may hold values from 0.1 to 1.9
- raw_taps: float32 [2048, 768], P('kern'), may hold values from -0.125 to 0.125
- pad_lengths: int32 [768], replicated, may hold values from 0 to 1023
Outputs:
- out_tokens: bfloat16 [16, 2048, 768], P('dp', 'kern')
- grad_tokens: bfloat16 [16, 2048, 768], P('dp', 'kern')
- grad_in: float32 [768, 1536], P('kern', 'dp')
- grad_out: float32 [768, 768], P('kern', 'dp')
- grad_up: float32 [768, 3072], P('kern', 'dp')
- grad_down: float32 [3072, 768], P('kern', 'dp')
- grad_first_gain: float32 [768], P('kern')
- grad_second_gain: float32 [768], P('kern')
- grad_raw: float32 [2048, 768], P('kern')
The draws below stay inside these ranges and needn't reach their ends.
Inputs may be any that keep to these rules, and one draw needn't show every extreme that they name: Channel c keeps its first 2048 - pad_lengths[c] taps.
All inputs are finite; a program needn't handle non-finite values.
Results may differ from the reference program's by a relative error of at most 0.02.
Values may be sent and summed in bfloat16 or wider, within the bound.
No kernel may reach another device: no remote copies, remote signals or barrier semaphores. Data moves between devices by JAX's collectives and lax.ppermute only.
A program may use at most 320 MiB of HBM per device.

```python
import jax
import jax.numpy as jnp
from jax import lax

D = 768
FF = 3072
TAPS = 2048
LEN = 2048
SEQS = 16


def place_ends(drawn, key, low, largest):
    dims = drawn.shape
    spot = [jax.random.randint(jax.random.fold_in(key, axis), (), 0, dims[axis]) for axis in range(len(dims))]
    drawn = drawn.at[tuple(spot)].set(low)
    longest = dims.index(max(dims))
    spot[longest] = (spot[longest] + 1) % dims[longest]
    return drawn.at[tuple(spot)].set(largest)


def shard_levels(rng, extent, pieces, smallest, largest):
    def one(position, blocks):
        heights = jax.random.uniform(jax.random.fold_in(jax.random.fold_in(rng, 6), position), (blocks,), jnp.float32, smallest / len(pieces), largest / len(pieces))
        return jnp.repeat(jnp.exp(heights), extent[position] // blocks).reshape((-1,) + (1,) * (len(extent) - position - 1))

    factor_of = one(*pieces[0])
    for cut in pieces[1:]:
        factor_of = factor_of * one(*cut)
    return factor_of


def noise(key, dims, scale, reach, cuts=(), kind=jnp.bfloat16):
    drawn = jax.random.normal(key, dims, jnp.float32) * scale
    if len(cuts) > 0:
        drawn = shard_levels(key, dims, cuts, -0.22, 0.18) * drawn
    return jnp.clip(drawn, min=-reach, max=reach).astype(kind)


def setup_inputs(seed: int = 0) -> dict:
    seeds = jax.random.split(jax.random.key(seed), 11)
    return {
        "tokens": noise(seeds[0], (SEQS, LEN, D), 1.0, 6.0, ((0, 8), (1, 4))),
        "cotangent": noise(seeds[1], (SEQS, LEN, D), 1.0, 6.0, ((0, 8), (1, 4))),
        "in_weight": noise(seeds[2], (D, 2 * D), D ** -0.5, 0.21875),
        "out_weight": noise(seeds[3], (D, D), (D // 4) ** -0.5, 0.4375),
        "up_weight": noise(seeds[4], (D, FF), D ** -0.5, 0.21875),
        "down_weight": noise(seeds[5], (FF, D), (FF // 2) ** -0.5, 0.15625),
        "first_gain": jnp.clip(1.0 + 0.18 * jax.random.normal(seeds[6], (D,), jnp.float32), 0.1, 1.9),
        "second_gain": jnp.clip(1.0 + 0.18 * jax.random.normal(seeds[7], (D,), jnp.float32), 0.1, 1.9),
        "raw_taps": noise(seeds[8], (TAPS, D), TAPS ** -0.5, 0.125, ((0, 4),), jnp.float32),
        "pad_lengths": place_ends(jax.random.randint(seeds[9], (D,), 0, TAPS // 2), jax.random.fold_in(seeds[9], 1), 0, (TAPS // 2) - 1).astype(jnp.int32),
    }


shrink_level = 0.003
norm_eps = 1e-05
highest = lax.Precision.HIGHEST

@jax.custom_vjp
def low(v):
    return lax.optimization_barrier(v.astype(jnp.bfloat16)).astype(jnp.float32)

@jax.custom_vjp
def low_back(v):
    return v

def low_keep(v):
    return (low(v), None)

def low_pass(kept, grad):
    return (grad,)

def back_keep(v):
    return (v, None)

def back_low(kept, grad):
    return (low(grad),)
low.defvjp(low_keep, low_pass)
low_back.defvjp(back_keep, back_low)

def layer_norm(values, norm_gain):
    center = values - lax.optimization_barrier(jnp.mean(values, axis=-1, keepdims=True))
    spread = lax.optimization_barrier(jnp.mean(center * center, axis=-1, keepdims=True))
    return center * lax.rsqrt(spread + norm_eps) * norm_gain

def causal_conv(signal, kernel):
    full_size = 2 * signal.shape[1]
    spectrum = jnp.fft.rfft(signal, n=full_size, axis=1) * jnp.fft.rfft(kernel, n=full_size, axis=0)[None]
    return jnp.fft.irfft(spectrum, n=full_size, axis=1)[:, :signal.shape[1]]

def forward(inputs, in_weight, out_weight, up_weight, down_weight, first_gain, second_gain, raw_taps, pad_lengths):
    tap_index = jnp.arange(TAPS, dtype=jnp.int32)
    mask = (tap_index[:, None] < (TAPS - pad_lengths.astype(jnp.int32))[None, :]).astype(jnp.float32)
    shrunk = raw_taps - shrink_level * raw_taps / jnp.sqrt(raw_taps * raw_taps + shrink_level * shrink_level)
    padded = jnp.pad(shrunk, ((1, 1), (0, 0)))
    kernel = low(mask * (padded[:-2] + padded[1:-1] + padded[2:]) / 3.0)
    norm1 = low(layer_norm(inputs, first_gain))
    projected = low_back(jnp.einsum('bld,de->ble', norm1, in_weight, precision=highest))
    signal = low(projected[..., :D])
    gate_part = projected[..., D:]
    convolved = low_back(causal_conv(signal, kernel))
    mixed_out = low(gate_part * convolved)
    branch = low_back(jnp.einsum('bld,de->ble', mixed_out, out_weight, precision=highest))
    middle = inputs + branch
    norm2 = low(layer_norm(middle, second_gain))
    raised = low_back(jnp.einsum('bld,df->blf', norm2, up_weight, precision=highest))
    hidden = low(jax.nn.gelu(raised))
    return middle + jnp.einsum('blf,fd->bld', hidden, down_weight, precision=highest)

def reference(tokens, cotangent, in_weight, out_weight, up_weight, down_weight, first_gain, second_gain, raw_taps, pad_lengths):
    group_size = 1
    weights = (in_weight.astype(jnp.float32), out_weight.astype(jnp.float32), up_weight.astype(jnp.float32), down_weight.astype(jnp.float32), first_gain.astype(jnp.float32), second_gain.astype(jnp.float32), raw_taps.astype(jnp.float32))
    token_groups = tokens.reshape(SEQS // group_size, group_size, LEN, D)
    cotangent_groups = cotangent.reshape(SEQS // group_size, group_size, LEN, D)

    def layer_fn(inputs, w_a, w_b, w_c, w_d, gain_a, gain_b, taps_a):
        return forward(inputs, w_a, w_b, w_c, w_d, gain_a, gain_b, taps_a, pad_lengths)

    def one_group(totals, batch_pair):
        group_tokens, group_cotangent = batch_pair
        output, pullback = jax.vjp(layer_fn, group_tokens.astype(jnp.float32), *weights)
        gradients = pullback(group_cotangent.astype(jnp.float32))
        new_totals = jax.tree.map(jnp.add, totals, tuple(gradients[1:]))
        return (new_totals, (output.astype(jnp.bfloat16), gradients[0].astype(jnp.bfloat16)))
    initial = tuple((jnp.zeros(weight.shape, jnp.float32) for weight in weights))
    totals, stacked = lax.scan(one_group, initial, (token_groups, cotangent_groups))
    out_tokens = stacked[0].reshape(SEQS, LEN, D)
    grad_tokens = stacked[1].reshape(SEQS, LEN, D)
    return (out_tokens, grad_tokens, totals[0], totals[1], totals[2], totals[3], totals[4], totals[5], totals[6])
```

```python
import math

import jax
import jax.numpy as jnp
import ml_dtypes
import numpy as np
from jax import lax
from jax.experimental import pallas as pl
from jax.experimental.pallas import tpu as pltpu
from jax.sharding import PartitionSpec as P

shrink_level = 0.003
norm_eps = 1e-05
bf16 = jnp.bfloat16
f32 = jnp.float32
inner = 128
group = 16
wide = 4


def inner_tables(outer):
    length = outer * inner
    k1 = np.arange(outer)[:, None, None]
    k2 = np.arange(inner)[None, :, None]
    n2 = np.arange(inner)[None, None, :]
    turns = (n2 * (4 * (outer * k2 + k1) + 1)) % (4 * length)
    angle = turns * (2 * math.pi / (4 * length))
    c, s = np.cos(angle), np.sin(angle)
    table = np.concatenate([np.concatenate([c, s], 2), np.concatenate([-s, c], 2)], 1)
    back = table.transpose(0, 2, 1) / length
    return table.astype(ml_dtypes.bfloat16), back.astype(ml_dtypes.bfloat16)


def outer_tables(outer):
    k1 = np.arange(outer)[:, None]
    n1 = np.arange(outer)[None, :]
    angle = (n1 * (4 * k1 + 1)) % (4 * outer) * (2 * math.pi / (4 * outer))
    parts = np.stack([np.cos(angle), -np.sin(angle)], 1)
    table = np.einsum("kcn,ij->kcinj", parts, np.eye(group))
    table = table.reshape(outer * 2 * group, outer * group)
    return table.astype(ml_dtypes.bfloat16), table.T.astype(ml_dtypes.bfloat16)


def all_tables(outer):
    table, back = inner_tables(outer)
    first, last = outer_tables(outer)
    tabs = {"inner": table, "inner_back": back, "first": first, "last": last}
    return {key: jnp.asarray(value) for key, value in tabs.items()}


def outer_forward(x_ref, table_ref, y_ref):
    outer, _, ch = x_ref.shape

    def step(j, carry):
        rows = pl.ds(pl.multiple_of(j * group, group), group)
        x = x_ref[:, rows, :].reshape(outer * group, ch)
        y = jnp.dot(table_ref[...], x, preferred_element_type=f32).astype(bf16)
        y = y.reshape(outer, 2, group, ch)
        y_ref[:, 0, rows, :] = y[:, 0]
        y_ref[:, 1, rows, :] = y[:, 1]
        return carry

    lax.fori_loop(0, inner // group, step, 0, unroll=4)


def outer_back(w_ref, table_ref, x_ref):
    outer, _, _, ch = w_ref.shape

    def step(j, carry):
        rows = pl.ds(pl.multiple_of(j * group, group), group)
        w = w_ref[:, :, rows, :].reshape(outer * 2 * group, ch)
        x = jnp.dot(table_ref[...], w, preferred_element_type=f32)
        x_ref[:, rows, :] = x.astype(x_ref.dtype).reshape(outer, group, ch)
        return carry

    lax.fori_loop(0, inner // group, step, 0, unroll=4)


def whole(shape):
    return pl.BlockSpec(shape, lambda i: (0,) * len(shape))


def slab(*shape):
    return pl.BlockSpec((wide,) + shape, lambda i: (i,) + (0,) * len(shape))


def smem():
    return pl.BlockSpec(memory_space=pltpu.SMEM)


def params(mib):
    return pltpu.CompilerParams(
        vmem_limit_bytes=mib * 2**20, dimension_semantics=("arbitrary",)
    )


def cost(micros):
    return pl.CostEstimate(
        flops=int(micros * 8e8), bytes_accessed=int(micros * 1e6), transcendentals=0
    )


def tap_spectrum(words, taps, limits, tabs):
    groups, kern, share, ch = taps.shape
    length = groups * kern * share
    outer = length // inner

    def kernel(_, taps_ref, limit_ref, table_ref, first_ref, out_ref, x_ref, y_ref, flat_ref):
        @pl.when(pl.program_id(0) == 0)
        def _():
            for z in range(kern):
                for p in range(groups):
                    at = (z * groups + p) * share
                    flat_ref[at : at + share] = taps_ref[p, z].astype(f32)
            values = flat_ref[...]
            edge = jnp.zeros((1, ch), f32)
            below = jnp.concatenate([edge, values[:-1]], 0)
            above = jnp.concatenate([values[1:], edge], 0)
            index = lax.broadcasted_iota(jnp.int32, (length, ch), 0)
            values = jnp.where(index < limit_ref[...], (below + values + above) / 3.0, 0.0)
            x_ref[...] = values.astype(bf16).reshape(outer, inner, ch)
            outer_forward(x_ref, first_ref, y_ref)

        for i in range(wide):
            y = y_ref[pl.program_id(0) * wide + i].reshape(2 * inner, ch)
            s = jnp.dot(table_ref[i], y, preferred_element_type=f32)
            out_ref[i] = s.astype(bf16)

    return pl.pallas_call(
        kernel,
        grid=(outer // wide,),
        in_specs=[
            smem(),
            whole(taps.shape),
            whole((1, ch)),
            slab(2 * inner, 2 * inner),
            whole(tabs["first"].shape),
        ],
        out_specs=slab(2 * inner, ch),
        out_shape=jax.ShapeDtypeStruct((outer, 2 * inner, ch), bf16),
        scratch_shapes=[
            pltpu.VMEM((outer, inner, ch), bf16),
            pltpu.VMEM((outer, 2, inner, ch), bf16),
            pltpu.VMEM((length, ch), f32),
        ],
        compiler_params=params(56),
        cost_estimate=cost(6),
        name="tap_spectrum",
    )(words, taps, limits, tabs["inner"], tabs["first"])


def packed(rows, ch):
    if ch % 128 == 64 and rows % (2 * inner) == 0:
        return (rows // inner * (2 * ch // 128) // 2, inner, 128)
    return (rows // inner, inner, ch)


def pack(ref, lead, values, part, parts):
    rows, ch = values.shape
    blocks = rows // inner
    if ref.shape[-1] == ch:
        ref[(*lead, pl.ds(part * blocks, blocks))] = values.reshape(blocks, inner, ch)
        return
    full = ch // 128
    for j in range(full):
        at = (j * parts + part) * blocks
        lanes = values[:, j * 128 : (j + 1) * 128]
        ref[(*lead, pl.ds(at, blocks))] = lanes.reshape(blocks, inner, 128)
    rest = values[:, full * 128 :]
    half = parts * blocks // 2
    for t in range(blocks):
        at = part * blocks + t
        side, row = at // half, at % half
        ref[(*lead, full * parts * blocks + row, slice(None), slice(side * 64, side * 64 + 64))] = (
            rest[t * inner : (t + 1) * inner]
        )


def unpack(ref, lead, part, parts, ch, blocks):
    if ref.shape[-1] == ch:
        return [(0, ref[(*lead, pl.ds(part * blocks, blocks))])]
    full = ch // 128
    out = []
    for j in range(full):
        at = (j * parts + part) * blocks
        out.append((j * 128, ref[(*lead, pl.ds(at, blocks))]))
    half = parts * blocks // 2
    rest = []
    for t in range(blocks):
        at = part * blocks + t
        side, row = at // half, at % half
        rest.append(
            ref[(*lead, full * parts * blocks + row, slice(None), slice(side * 64, side * 64 + 64))]
        )
    out.append((full * 128, jnp.stack(rest)))
    return out


def owners(me_ref, refs, kern, sign):
    if len(refs) == 1 and kern > 1:
        return [(refs[0], (k,), k) for k in range(kern)]
    return [
        (ref, (), lax.rem(me_ref[0] + (k if sign > 0 else kern - k), kern))
        for k, ref in enumerate(refs)
    ]


def piece_shapes(kern, rows, ch, stacked):
    shape = packed(rows, ch)
    return [(kern, *shape)] if stacked else [shape] * kern


def place_pieces(me_ref, piece_refs, x_ref, kern):
    outer, _, ch = x_ref.shape
    blocks = outer // kern
    for ref, lead, owner in owners(me_ref, piece_refs, kern, 1):
        for at, block in unpack(ref, lead, 0, 1, ch, blocks):
            x_ref[pl.ds(owner * blocks, blocks), :, at : at + block.shape[2]] = block


def take_pieces(me_ref, x_ref, piece_refs, kern):
    outer, _, ch = x_ref.shape
    blocks = outer // kern
    for ref, lead, owner in owners(me_ref, piece_refs, kern, 1):
        pack(ref, lead, x_ref[pl.ds(owner * blocks, blocks)].reshape(blocks * inner, ch), 0, 1)


def convolve(me, pieces, kern, kernel_spec, tabs, flip, other_spec=None, stacked=False):
    count = len(pieces)
    outer, _, ch = kernel_spec.shape
    shapes = piece_shapes(kern, outer * inner // kern, ch, stacked)

    def kernel(me_ref, *refs):
        piece_refs, refs = refs[:count], refs[count:]
        spec_ref, table_ref, back_ref, first_ref, last_ref = refs[:5]
        refs = refs[5:]
        if flip:
            other_ref, refs = refs[0], refs[1:]
        out_refs, refs = refs[: len(shapes)], refs[len(shapes) :]
        save_ref, x_ref, y_ref, w_ref = refs
        step = pl.program_id(0)

        @pl.when(step == 0)
        def _():
            place_pieces(me_ref, piece_refs, x_ref, kern)
            outer_forward(x_ref, first_ref, y_ref)

        for i in range(wide):
            at = step * wide + i
            y = y_ref[at].reshape(2 * inner, ch)
            s = jnp.dot(table_ref[i], y, preferred_element_type=f32)
            sr, si = s[:inner], s[inner:]
            kr = spec_ref[i, :inner].astype(f32)
            ki = spec_ref[i, inner:].astype(f32)
            if flip:
                orr = other_ref[i, :inner].astype(f32)
                oi = other_ref[i, inner:].astype(f32)
                save_ref[i, :inner] = (sr * orr + si * oi).astype(bf16)
                save_ref[i, inner:] = (si * orr - sr * oi).astype(bf16)
                zr, zi = sr * kr + si * ki, si * kr - sr * ki
            else:
                save_ref[i] = s.astype(bf16)
                zr, zi = sr * kr - si * ki, sr * ki + si * kr
            z = jnp.concatenate([zr, zi], 0).astype(bf16)
            w = jnp.dot(back_ref[i], z, preferred_element_type=f32)
            w_ref[at] = w.astype(bf16).reshape(2, inner, ch)

        @pl.when(step == pl.num_programs(0) - 1)
        def _():
            outer_back(w_ref, last_ref, x_ref)
            take_pieces(me_ref, x_ref, out_refs, kern)

    args = [me, *pieces, kernel_spec, tabs["inner"], tabs["inner_back"], tabs["first"], tabs["last"]]
    in_specs = [smem()] + [whole(piece.shape) for piece in pieces] + [
        slab(2 * inner, ch),
        slab(2 * inner, 2 * inner),
        slab(2 * inner, 2 * inner),
        whole(tabs["first"].shape),
        whole(tabs["last"].shape),
    ]
    if flip:
        args.append(other_spec)
        in_specs.append(slab(2 * inner, ch))
    outs = pl.pallas_call(
        kernel,
        grid=(outer // wide,),
        in_specs=in_specs,
        out_specs=[whole(shape) for shape in shapes] + [slab(2 * inner, ch)],
        out_shape=[jax.ShapeDtypeStruct(shape, bf16) for shape in shapes]
        + [jax.ShapeDtypeStruct((outer, 2 * inner, ch), bf16)],
        scratch_shapes=[
            pltpu.VMEM((outer, inner, ch), bf16),
            pltpu.VMEM((outer, 2, inner, ch), bf16),
            pltpu.VMEM((outer, 2, inner, ch), bf16),
        ],
        compiler_params=params(56),
        cost_estimate=cost(8),
        name="correlate" if flip else "convolve",
    )(*args)
    return list(outs[:-1]), outs[-1]


def tap_gradient(words, products, limits, tabs, kern, groups):
    outer, _, ch = products[0].shape
    length = outer * inner
    share = length // (kern * groups)

    def kernel(_, limit_ref, *refs):
        spec_refs, refs = refs[: len(products)], refs[len(products) :]
        back_ref, last_ref, out_ref, w_ref, x_ref = refs
        step = pl.program_id(0)
        for i in range(wide):
            z = spec_refs[0][i].astype(f32)
            for spec_ref in spec_refs[1:]:
                z = z + spec_ref[i].astype(f32)
            w = jnp.dot(back_ref[i], z.astype(bf16), preferred_element_type=f32)
            w_ref[step * wide + i] = w.astype(bf16).reshape(2, inner, ch)

        @pl.when(step == pl.num_programs(0) - 1)
        def _():
            outer_back(w_ref, last_ref, x_ref)
            taps = x_ref[...].reshape(length, ch)
            index = lax.broadcasted_iota(jnp.int32, (length, ch), 0)
            taps = jnp.where(index < limit_ref[...], taps, 0.0)
            edge = jnp.zeros((1, ch), f32)
            below = jnp.concatenate([edge, taps[:-1]], 0)
            above = jnp.concatenate([taps[1:], edge], 0)
            taps = ((below + taps + above) / 3.0).astype(bf16)
            for z in range(kern):
                for p in range(groups):
                    at = (z * groups + p) * share
                    out_ref[p, z] = taps[at : at + share]

    return pl.pallas_call(
        kernel,
        grid=(outer // wide,),
        in_specs=[smem(), whole((1, ch))]
        + [slab(2 * inner, ch)] * len(products)
        + [slab(2 * inner, 2 * inner), whole(tabs["last"].shape)],
        out_specs=whole((groups, kern, share, ch)),
        out_shape=jax.ShapeDtypeStruct((groups, kern, share, ch), bf16),
        scratch_shapes=[
            pltpu.VMEM((outer, 2, inner, ch), bf16),
            pltpu.VMEM((outer, inner, ch), f32),
        ],
        compiler_params=params(56),
        cost_estimate=cost(5),
        name="tap_gradient",
    )(words, limits, *products, tabs["inner_back"], tabs["last"])


def exchange(pieces, sign):
    count = len(pieces)
    moved = [pieces[0]]
    for k in range(1, count):
        route = [(i, (i + sign * k) % count) for i in range(count)]
        moved.append(lax.ppermute(pieces[k], "kern", route))
    return moved


def spread_out(block, axis_name, groups=None):
    return lax.all_to_all(
        block, axis_name, split_axis=0, concat_axis=0, tiled=True, axis_index_groups=groups
    )


def sum_all(row):
    for axis_name in ("dp", "kern"):
        count = lax.axis_size(axis_name)
        for bit in range(count.bit_length() - 1):
            route = [(i, i ^ (1 << bit)) for i in range(count)]
            row = row + lax.ppermute(row, axis_name, route)
    return row


def padded_rows(block):
    count = lax.axis_size("kern")
    forward = [(i, i + 1) for i in range(count - 1)]
    backward = [(target, source) for source, target in forward]
    low = lax.ppermute(block[-1:], "kern", forward)
    high = lax.ppermute(block[:1], "kern", backward)
    return jnp.concatenate([low, block, high], axis=0)


def layer_norm(values, norm_gain):
    center = values - jnp.mean(values, axis=-1, keepdims=True)
    spread = jnp.mean(center * center, axis=-1, keepdims=True)
    return center * lax.rsqrt(spread + norm_eps) * norm_gain


def shrink(tap_values):
    return tap_values - shrink_level * tap_values / jnp.sqrt(
        tap_values * tap_values + shrink_level * shrink_level
    )


def shrink_slope(tap_values):
    return 1.0 - shrink_level**3 / (tap_values * tap_values + shrink_level * shrink_level) ** 1.5


def pool_three(padded):
    return (padded[:-2] + padded[1:-1] + padded[2:]) / 3.0


def dot(left, right, dims):
    return lax.dot_general(left, right, (dims, ((), ())), preferred_element_type=f32)


def shards_general(
    tokens,
    cotangent,
    in_weight,
    out_weight,
    up_weight,
    down_weight,
    first_gain,
    second_gain,
    raw_taps,
    pad_lengths,
):
    seq_count, row_count, feat = tokens.shape
    kern = lax.axis_size("kern")
    me = lax.axis_index("kern")
    me_word = me.astype(jnp.int32).reshape(1)
    groups = lax.axis_size("dp")
    local_taps = raw_taps.shape[0]
    total_taps = local_taps * kern
    chan = feat // kern
    outer = row_count * kern // inner
    blocks = row_count // inner
    tabs = all_tables(outer)

    limits = total_taps - lax.dynamic_slice_in_dim(pad_lengths, me * chan, chan, 0)[None]
    my_raw = lax.all_to_all(raw_taps, "kern", split_axis=1, concat_axis=0, tiled=True)
    kernel_spec = tap_spectrum(me_word, shrink(my_raw)[None, None], limits, tabs)

    def apart(values):
        values = values.reshape(blocks, inner, kern, chan).transpose(2, 0, 1, 3)
        return [values[(me - k) % kern] for k in range(kern)]

    def joined(pieces):
        stack = jnp.stack(pieces)
        stack = jnp.stack([stack[(me - k) % kern] for k in range(kern)])
        return stack.transpose(1, 2, 0, 3).reshape(row_count, feat)

    def one(x, cot):
        inputs = x.astype(f32)
        first_norm, first_pull = jax.vjp(layer_norm, inputs, first_gain)
        normed = first_norm.astype(bf16)
        projected = dot(normed, in_weight, ((1,), (0,)))
        gate = projected[:, feat:]
        pieces = exchange(apart(projected[:, :feat].astype(bf16)), -1)
        pieces, spectrum = convolve(me_word, pieces, kern, kernel_spec, tabs, False)
        convolved = joined(exchange(pieces, 1)).astype(f32)
        mixed = (gate * convolved).astype(bf16)
        middle = inputs + dot(mixed, out_weight, ((1,), (0,)))
        second_norm, second_pull = jax.vjp(layer_norm, middle, second_gain)
        normed_two = second_norm.astype(bf16)
        raised = dot(normed_two, up_weight, ((1,), (0,)))
        activated, gelu_pull = jax.vjp(jax.nn.gelu, raised)
        hidden = activated.astype(bf16)
        out = (middle + dot(hidden, down_weight, ((1,), (0,)))).astype(bf16)
        grad_raised = gelu_pull(dot(cot, down_weight, ((1,), (1,))))[0].astype(bf16)
        grad_mid, second_row = second_pull(dot(grad_raised, up_weight, ((1,), (1,))))
        grad_mid = cot.astype(f32) + grad_mid
        branch = grad_mid.astype(bf16)
        grad_mixed = dot(branch, out_weight, ((1,), (1,)))
        grad_gate = (grad_mixed * convolved).astype(bf16)
        pieces = exchange(apart((grad_mixed * gate).astype(bf16)), -1)
        pieces, product = convolve(me_word, pieces, kern, kernel_spec, tabs, True, spectrum)
        grad_signal = joined(exchange(pieces, 1))
        grad_projected = jnp.concatenate([grad_signal, grad_gate], axis=-1)
        grad_first, first_row = first_pull(dot(grad_projected, in_weight, ((1,), (1,))))
        weights = (
            dot(normed, grad_projected, ((0,), (0,))),
            dot(mixed, branch, ((0,), (0,))),
            dot(normed_two, grad_raised, ((0,), (0,))),
            dot(hidden, cot, ((0,), (0,))),
        )
        return out, (grad_mid + grad_first).astype(bf16), product, (first_row, second_row), weights

    ones = [one(tokens[b], cotangent[b]) for b in range(seq_count)]
    rows, weights = ones[0][3:]
    for other in ones[1:]:
        rows, weights = jax.tree.map(jnp.add, (rows, weights), other[3:])
    grad_taps = tap_gradient(me_word, [item[2] for item in ones], limits, tabs, kern, 1)[0]
    grad_taps = spread_out(grad_taps, "kern").transpose(1, 0, 2).reshape(local_taps, feat)
    grad_raw = lax.psum(grad_taps, "dp").astype(f32) * shrink_slope(raw_taps)
    sums = []
    for weight in weights:
        weight = lax.psum_scatter(weight.astype(bf16), "dp", scatter_dimension=1, tiled=True)
        weight = lax.psum_scatter(weight, "kern", scatter_dimension=0, tiled=True)
        sums.append(weight.astype(f32))
    gains = sum_all(jnp.stack(rows))
    gains = lax.dynamic_slice_in_dim(gains, me * chan, chan, 1)
    return (
        jnp.stack([item[0] for item in ones]),
        jnp.stack([item[1] for item in ones]),
        *sums,
        gains[0],
        gains[1],
        grad_raw,
    )


def row_mean(values):
    return jnp.mean(values, axis=-1, keepdims=True)


def centered(values):
    center = values - row_mean(values)
    inverse = lax.rsqrt(row_mean(center * center) + norm_eps)
    return center * inverse, inverse


def norm_back(grad, normed, inverse, gain):
    scaled = grad * gain
    return inverse * (scaled - row_mean(scaled) - normed * row_mean(scaled * normed))


def mm(left, right):
    return jnp.dot(left, right, preferred_element_type=f32)


def mm_nt(left, right):
    return lax.dot_general(left, right, (((1,), (1,)), ((), ())), preferred_element_type=f32)


def mm_tn(left, right):
    return lax.dot_general(left, right, (((0,), (0,)), ((), ())), preferred_element_type=f32)


def fixed(shape):
    return pl.BlockSpec(shape, lambda *_: (0,) * len(shape))


def once(shape):
    return pl.BlockSpec(
        shape, lambda *_: (0,) * len(shape), pipeline_mode=pl.Buffered(1)
    )


def along(seq, rows, feat):
    return pl.BlockSpec((1, rows, feat), lambda i: (seq, i, 0))


def cut(me_ref, values, piece_refs, stack_ref, part=0, parts=1):
    kern, rows, ch = stack_ref.shape
    if len(piece_refs) > 1:
        for k in range(kern):
            stack_ref[k] = values[:, k * ch : (k + 1) * ch]
    for ref, lead, owner in owners(me_ref, piece_refs, kern, -1):
        block = stack_ref[owner] if len(piece_refs) > 1 else values[:, owner * ch : (owner + 1) * ch]
        pack(ref, lead, block, part, parts)


def join(me_ref, piece_refs, stack_ref, out_ref, part=0, parts=1):
    kern, rows, ch = stack_ref.shape
    blocks = rows // inner
    for ref, lead, owner in owners(me_ref, piece_refs, kern, -1):
        for at, block in unpack(ref, lead, part, parts, ch, blocks):
            width = block.shape[2]
            block = block.reshape(rows, width)
            if len(piece_refs) > 1:
                stack_ref[owner, :, at : at + width] = block
            else:
                out_ref[:, owner * ch + at : owner * ch + at + width] = block
    if len(piece_refs) > 1:
        for k in range(kern):
            out_ref[:, k * ch : (k + 1) * ch] = stack_ref[k]


def project(me, seq, tokens, gain, weight, kern, stacked):
    _, rows, feat = tokens.shape
    chan = feat // kern
    tile = rows // 2
    shapes = piece_shapes(kern, rows, chan, stacked)

    def kernel(me_ref, x_ref, gain_ref, weight_ref, *refs):
        normed_ref, gate_ref = refs[:2]
        piece_refs, stack_ref = refs[2:-1], refs[-1]
        hat, _ = centered(x_ref[0].astype(f32))
        normed = (hat * gain_ref[...]).astype(bf16)
        normed_ref[...] = normed
        projected = mm(normed, weight_ref[...])
        gate_ref[...] = projected[:, feat:]
        signal = projected[:, :feat].astype(bf16)
        for part in range(2):
            pl.when(pl.program_id(0) == part)(
                lambda: cut(me_ref, signal, piece_refs, stack_ref, part, 2)
            )

    outs = pl.pallas_call(
        kernel,
        grid=(2,),
        in_specs=[smem(), along(seq, tile, feat), fixed((1, feat)), fixed(weight.shape)],
        out_specs=[
            pl.BlockSpec((tile, feat), lambda i: (i, 0)),
            pl.BlockSpec((tile, feat), lambda i: (i, 0)),
        ]
        + [fixed(shape) for shape in shapes],
        out_shape=[
            jax.ShapeDtypeStruct((rows, feat), bf16),
            jax.ShapeDtypeStruct((rows, feat), f32),
        ]
        + [jax.ShapeDtypeStruct(shape, bf16) for shape in shapes],
        scratch_shapes=[pltpu.VMEM((kern, tile, chan), bf16)],
        compiler_params=params(56),
        cost_estimate=cost(4),
        name="project",
    )(me, tokens, gain.reshape(1, feat), weight)
    return outs[0], outs[1], list(outs[2:])


def gelu_pair(raised):
    root = math.sqrt(2.0 / math.pi)
    square = raised * raised
    t = jnp.tanh(raised * (root + (root * 0.044715) * square))
    half = 0.5 + 0.5 * t
    slope = half + (0.5 * raised) * (1.0 - t * t) * (root + (3.0 * root * 0.044715) * square)
    return raised * half, slope


def feed_forward(words, seq, tokens, cots, gate, conv, normed, out_weight, up_weight, down_weight, gain, kern, groups, stacked, earlier, out_before):
    seqs, rows, feat = tokens.shape
    width = up_weight.shape[1]
    count = len(conv)
    shapes = piece_shapes(kern, rows, feat // kern, stacked)
    chan = feat // kern
    pairs = groups // 2
    chunk = width // pairs
    deep = feat // groups
    half = chunk // 2
    add = earlier is not None

    def kernel(word_ref, x_ref, cot_ref, gate_ref, normed_ref, ow_ref, up_ref, down_ref, gain_ref, *refs):
        conv_refs, refs = refs[:count], refs[count:]
        if add:
            old, refs = refs[:7], refs[8:]
        out_ref, mid_ref, ggate_ref, ggain_ref = refs[:4]
        u_keep, u_give, d_keep, d_give, o_ref, g_ref = refs[4:10]
        piece_refs, refs = refs[10 : 10 + len(shapes)], refs[10 + len(shapes) :]
        stack_s, cv, mixed_s, middle_s, n2_s, acc_s, back_s = refs
        f = pl.program_id(0)
        cot = cot_ref.at[0]

        @pl.when(f == 0)
        def _():
            join(word_ref, conv_refs, stack_s, cv)
            mixed = (gate_ref[...] * cv[...].astype(f32)).astype(bf16)
            mixed_s[...] = mixed
            middle = x_ref[0].astype(f32) + mm(mixed, ow_ref[...])
            middle_s[...] = middle
            hat, _ = centered(middle)
            n2_s[...] = (hat * gain_ref[...]).astype(bf16)
            acc_s[...] = middle
            back_s[...] = jnp.zeros_like(back_s)

        raised = mm(n2_s[...], up_ref[...])
        act, slope = gelu_pair(raised)
        hidden = act.astype(bf16)
        grad_raised = (mm_nt(cot[...], down_ref[...]) * slope).astype(bf16)
        acc_s[...] += mm(hidden, down_ref[...])
        back_s[...] += mm_nt(grad_raised, up_ref[...])
        u = mm_tn(n2_s[...], grad_raised)
        d = mm_tn(cot[...], hidden).reshape(pairs, 2, 1, deep, chunk)

        def put(side):
            for to, u_ref, d_ref, u_old, d_old in (
                (side, u_keep, d_keep, 0, 2),
                (1 - side, u_give, d_give, 1, 3),
            ):
                dd = d[:, to]
                if add:
                    dd = dd + old[d_old][...].astype(f32)
                d_ref[...] = dd.astype(bf16)
                uu = u[:, to * half : (to + 1) * half].reshape(kern, 2, deep, half)
                for h in range(2):
                    lanes = slice(h * half, (h + 1) * half)
                    part = uu[:, h]
                    if add:
                        part = part + old[u_old][0, :, :, lanes].astype(f32)
                    u_ref[0, :, :, lanes] = part.astype(bf16)

        pl.when(word_ref[1] == 0)(lambda: put(0))
        pl.when(word_ref[1] != 0)(lambda: put(1))

        @pl.when(f == pairs - 1)
        def _():
            out_ref[0] = acc_s[...].astype(bf16)
            hat, inverse = centered(middle_s[...])
            back = back_s[...]
            ggain = jnp.sum(back * hat, axis=0, keepdims=True)
            grad_mid = cot[...].astype(f32) + norm_back(back, hat, inverse, gain_ref[...])
            mid_ref[...] = grad_mid
            branch = grad_mid.astype(bf16)
            grad_mixed = mm_nt(branch, ow_ref[...])
            ggate = (grad_mixed * cv[...].astype(f32)).astype(bf16)
            ggate_ref[...] = ggate
            cut(word_ref, (grad_mixed * gate_ref[...]).astype(bf16), piece_refs, stack_s)
            o = mm_tn(branch, mixed_s[...])
            g = mm_tn(ggate, normed_ref[...])
            if add:
                ggain = ggain + old[6][...]
                o = o + old[4][...].astype(f32)
                g = g + old[5][...].astype(f32)
            ggain_ref[...] = ggain
            o_ref[...] = o.astype(bf16)
            g_ref[...] = g.astype(bf16)

    u_spec = pl.BlockSpec((1, kern, deep, chunk), lambda f: (f, 0, 0, 0))
    d_spec = pl.BlockSpec((pairs, 1, deep, chunk), lambda f: (0, f, 0, 0))
    square = fixed((feat, feat))
    flat = fixed((rows, feat))
    one = pl.BlockSpec((1, rows, feat), lambda f: (seq, 0, 0))
    args = [words, tokens, cots, gate, normed, out_weight, up_weight, down_weight, gain.reshape(1, feat), *conv]
    in_specs = [
        smem(),
        one,
        one,
        once((rows, feat)),
        once((rows, feat)),
        once(out_weight.shape),
        pl.BlockSpec((feat, chunk), lambda f: (0, f)),
        pl.BlockSpec((chunk, feat), lambda f: (f, 0)),
        fixed((1, feat)),
    ] + [fixed(piece.shape) for piece in conv]
    grad_specs = [u_spec, u_spec, d_spec, d_spec, square, square]
    aliases = {}
    if add:
        args += [*earlier, out_before]
        in_specs += [*grad_specs, fixed((1, feat)), pl.BlockSpec(memory_space=pl.ANY)]
        aliases = {len(args) - 1: 0}
    big = jax.ShapeDtypeStruct((pairs, kern, deep, chunk), bf16)
    outs = pl.pallas_call(
        kernel,
        grid=(pairs,),
        in_specs=in_specs,
        out_specs=[one, flat, flat, fixed((1, feat)), *grad_specs]
        + [fixed(shape) for shape in shapes],
        out_shape=[
            jax.ShapeDtypeStruct(tokens.shape, bf16),
            jax.ShapeDtypeStruct((rows, feat), f32),
            jax.ShapeDtypeStruct((rows, feat), bf16),
            jax.ShapeDtypeStruct((1, feat), f32),
            big,
            big,
            big,
            big,
            jax.ShapeDtypeStruct((feat, feat), bf16),
            jax.ShapeDtypeStruct((feat, feat), bf16),
        ]
        + [jax.ShapeDtypeStruct(shape, bf16) for shape in shapes],
        scratch_shapes=[
            pltpu.VMEM((kern, rows, chan), bf16),
            pltpu.VMEM((rows, feat), bf16),
            pltpu.VMEM((rows, feat), bf16),
            pltpu.VMEM((rows, feat), f32),
            pltpu.VMEM((rows, feat), bf16),
            pltpu.VMEM((rows, feat), f32),
            pltpu.VMEM((rows, feat), f32),
        ],
        input_output_aliases=aliases,
        compiler_params=params(56),
        cost_estimate=cost(24),
        name="feed_forward",
    )(*args)
    return outs[:4], list(outs[4:10]), list(outs[10:])


late_rows = 160


def finish(words, seq, tokens, normed, grad_mid, grad_gate, signal, weight, gain, kern, groups, earlier, out_before, others):
    seqs, rows, feat = tokens.shape
    count = len(signal)
    chan = feat // kern
    part = rows // 2
    add = earlier is not None
    last = others is not None
    pairs = groups // 2
    in_rows, out_rows = 2 * feat // groups, feat // groups

    def kernel(word_ref, x_ref, normed_ref, mid_ref, gate_ref, weight_ref, gain_ref, *refs):
        signal_refs, refs = refs[:count], refs[count:]
        if add:
            old_s, old_gain, refs = refs[0], refs[1], refs[3:]
        if last:
            gt_ref, ot_ref, row_ref, refs = refs[0], refs[1], refs[2], refs[3:]
            out_ref, refs = refs[0], refs[1:]
            late_refs, refs = (refs[:2], refs[2:4]), refs[4:]
            ggain_ref, s_ref, stack_s, gs = refs
        else:
            out_ref, ggain_ref, s_ref, stack_s, gs = refs
        i = pl.program_id(0)
        for p in range(2):
            pl.when(i == p)(lambda: join(word_ref, signal_refs, stack_s, gs, p, 2))
        back = mm_nt(gs[...], weight_ref[:, :feat]) + mm_nt(gate_ref[...], weight_ref[:, feat:])
        hat, inverse = centered(x_ref[0].astype(f32))
        grad = mid_ref[...] + norm_back(back, hat, inverse, gain_ref[...])
        out_ref[0] = grad.astype(bf16)
        ggain = jnp.sum(back * hat, axis=0, keepdims=True)
        s = mm_tn(gs[...], normed_ref[...])

        @pl.when(i == 0)
        def _():
            ggain_ref[...] = ggain + old_gain[...] if add else ggain
            s_ref[...] = s + old_s[...] if add else s

        @pl.when(i != 0)
        def _():
            ggain_ref[...] += ggain
            s_ref[...] += s

        if last:

            @pl.when(i == 1)
            def _():
                zero = jnp.zeros((2 * late_rows - in_rows - out_rows - 2, feat), f32)
                gains = jnp.concatenate([ggain_ref[...], row_ref[...], zero], 0)
                for to, side in ((0, word_ref[1]), (1, 1 - word_ref[1])):
                    for pair in range(pairs):
                        from_ref = s_ref if pair < pairs // 2 else gt_ref
                        at_in = (2 * (pair % (pairs // 2)) + side) * in_rows
                        at_in = pl.multiple_of(at_in, in_rows)
                        at_out = pl.multiple_of((2 * pair + side) * out_rows, out_rows)
                        block = jnp.concatenate(
                            [
                                from_ref[pl.ds(at_in, in_rows), :].astype(f32),
                                ot_ref[pl.ds(at_out, out_rows), :].astype(f32),
                                gains,
                            ],
                            0,
                        )
                        for h in range(2):
                            values = block[h * late_rows : (h + 1) * late_rows].astype(bf16)
                            for z in range(kern):
                                late_pack(late_refs[h][to], (pair, z), values[:, z * chan : (z + 1) * chan])

    tiled = pl.BlockSpec((part, feat), lambda i: (i, 0))
    args = [words, tokens, normed, grad_mid, grad_gate, weight, gain.reshape(1, feat), *signal]
    in_specs = [
        smem(),
        along(seq, part, feat),
        tiled,
        tiled,
        tiled,
        fixed(weight.shape),
        fixed((1, feat)),
    ] + [fixed(piece.shape) for piece in signal]
    aliases = {}
    if add:
        args += [*earlier, out_before]
        in_specs += [fixed((feat, feat)), fixed((1, feat)), pl.BlockSpec(memory_space=pl.ANY)]
        aliases = {len(args) - 1: 0}
    out_specs = [along(seq, part, feat)]
    out_shape = [jax.ShapeDtypeStruct(tokens.shape, bf16)]
    scratch = [
        pltpu.VMEM((kern, part, chan), bf16),
        pltpu.VMEM((part, feat), bf16),
    ]
    if last:
        args += others
        in_specs += [fixed((feat, feat)), fixed((feat, feat)), fixed((1, feat))]
        late = (pairs, kern, late_rows // 2 * 3, 128)
        out_specs += [fixed(late)] * 4
        out_shape += [jax.ShapeDtypeStruct(late, bf16)] * 4
        scratch = [pltpu.VMEM((1, feat), f32), pltpu.VMEM((feat, feat), f32)] + scratch
    else:
        out_specs += [fixed((1, feat)), fixed((feat, feat))]
        out_shape += [
            jax.ShapeDtypeStruct((1, feat), f32),
            jax.ShapeDtypeStruct((feat, feat), f32),
        ]
    return pl.pallas_call(
        kernel,
        grid=(2,),
        in_specs=in_specs,
        out_specs=out_specs,
        out_shape=out_shape,
        scratch_shapes=scratch,
        input_output_aliases=aliases,
        compiler_params=params(56),
        cost_estimate=cost(6),
        name="finish",
    )(*args)


def late_pack(ref, lead, values):
    half = late_rows // 2
    ref[(*lead, slice(0, late_rows))] = values[:, :128]
    ref[(*lead, slice(late_rows, late_rows + half), slice(0, 64))] = values[:half, 128:]
    ref[(*lead, slice(late_rows, late_rows + half), slice(64, 128))] = values[half:, 128:]


def late_unpack(block):
    half = late_rows // 2
    rest = block[late_rows:]
    rest = jnp.concatenate([rest[:, :64], rest[:, 64:]], axis=0)
    return jnp.concatenate([block[:late_rows], rest], axis=1)


def swap(block, axis_name, bit):
    route = [(i, i ^ (1 << bit)) for i in range(lax.axis_size(axis_name))]
    return lax.ppermute(block, axis_name, route)


def added(block):
    return jnp.sum(block.astype(f32), axis=0)


def fold(words, stage, plane_x, plane_y, finals=None):
    pairs, kern = plane_x[0].shape[:2]
    shape = plane_x[0].shape[2:]
    zero = (0,) * len(shape)
    half = kern // 2

    def place(w, kind):
        return (w[2], w[3]) if kind == 0 else (w[3], w[2])

    def pair(kind, first, second):
        return 2 * second + first if kind == 0 else 2 * first + second

    def z_of(g, w):
        if stage == 3:
            return 2 * g + 1 - w[0] % 2
        if stage == 4:
            return 2 * (1 - w[0] // 2) + w[0] % 2
        return w[0]

    def own(w, kind, g):
        first, second = place(w, kind)
        if stage == 1:
            return 1 - first, g
        return first, 1 - second if stage == 2 else second

    if stage == 1:
        grid, blocks = 2, (kern,)
        maps = [lambda g, w, k: (pair(k, *own(w, k, g)), 0)]
        out_block, out_map, out_lead = (None, kern), lambda g, w: (g, 0), (2, kern)
        blocks = [(None, kern)]
    elif stage == 2:
        grid = 2
        maps = [
            lambda g, w, k: (pair(k, *own(w, k, g)), g),
            lambda g, w, k: (own(w, k, g)[1], g),
        ]
        blocks = [(None, half), (None, half)]
        out_block, out_map, out_lead = (half,), lambda g, w: (g,), (kern,)
    else:
        grid = 2 if stage == 3 else 1
        maps = [
            lambda g, w, k: (pair(k, *own(w, k, g)), z_of(g, w)),
            lambda g, w, k: (own(w, k, g)[1], z_of(g, w)),
            lambda g, w, k: (z_of(g, w),),
            lambda g, w, k: (z_of(g, w) // 2,),
            lambda g, w, k: (),
        ]
        blocks = [(None, None), (None, None), (None,), (None,), ()]
        if stage == 3:
            out_block, out_map, out_lead = (None,), lambda g, w: (g,), (2,)
        else:
            out_block, out_map, out_lead = (), lambda g, w: (), ()

    def spec(index, kind):
        which = max(0, index - 1)
        return pl.BlockSpec(
            blocks[which] + shape, lambda g, w: tuple(maps[which](g, w, kind)) + zero
        )

    counts = len(plane_x)

    def kernel(word_ref, *refs):
        for kind in range(2):
            terms = refs[kind * counts : (kind + 1) * counts]
            out = terms[0][...].astype(f32)
            for term in terms[1:]:
                out = out + term[...].astype(f32)
            if finals is None:
                refs[2 * counts + kind][...] = out.astype(bf16)
            else:
                finals[2 * kind](out, *refs[2 * counts :])

    if finals is None:
        out_shape = [jax.ShapeDtypeStruct(out_lead + shape, bf16)] * 2
        out_specs = [
            pl.BlockSpec(out_block + shape, lambda g, w: tuple(out_map(g, w)) + zero)
        ] * 2
    else:
        out_shape = [jax.ShapeDtypeStruct(dims, f32) for dims in finals[1]]
        out_specs = [pl.BlockSpec(dims, lambda g, w, n=len(dims): (0,) * n) for dims in finals[1]]
    return pl.pallas_call(
        kernel,
        grid_spec=pltpu.PrefetchScalarGridSpec(
            num_scalar_prefetch=1,
            grid=(grid,),
            in_specs=[spec(i, kind) for kind in range(2) for i in range(counts)],
            out_specs=out_specs,
        ),
        out_shape=out_shape,
        compiler_params=params(56),
        cost_estimate=cost(2),
        name=f"fold_{stage}",
    )(words, *plane_x, *plane_y)


class Folding:
    steps = (("dp", 1, 2), ("dp", 2, 1), ("kern", 0, 0), ("kern", 1, 1))

    def __init__(self, keep_x, give_x, keep_y, give_y):
        self.terms = [
            [keep_x, swap(give_x, "dp", 0)],
            [keep_y, swap(give_y, "dp", 0)],
        ]

    def step(self, words, stage):
        axis_name, bit_x, bit_y = self.steps[stage - 1]
        out = fold(words, stage, *self.terms)
        for terms, block, bit in zip(self.terms, out, (bit_x, bit_y)):
            terms.append(swap(block, axis_name, bit))
        return out[0]

    def finish(self, words, finals):
        return fold(words, 5, *self.terms, finals)


def after(anchor, values):
    return lax.optimization_barrier((anchor, values))[1]


def shards(
    tokens,
    cotangent,
    in_weight,
    out_weight,
    up_weight,
    down_weight,
    first_gain,
    second_gain,
    raw_taps,
    pad_lengths,
):
    seq_count, row_count, feat = tokens.shape
    width = up_weight.shape[1]
    kern = lax.axis_size("kern")
    groups = lax.axis_size("dp")
    me = lax.axis_index("kern").astype(jnp.int32)
    my_group = lax.axis_index("dp").astype(jnp.int32)
    words = jnp.stack([me, my_group % 2, my_group // 2 % 2, my_group // 4])
    local_taps = raw_taps.shape[0]
    total_taps = local_taps * kern
    chan = feat // kern
    outer = row_count * kern // inner
    share = local_taps // groups
    deep = feat // groups
    in_rows = 2 * deep
    tabs = all_tables(outer)
    seqs = range(seq_count)

    moved = []

    def across(pieces, sign):
        if moved:
            pieces = after(moved[-1], pieces)
        if len(pieces) == 1:
            moved.append([spread_out(pieces[0], "kern")])
        else:
            moved.append(exchange(pieces, sign))
        return moved[-1]

    def to_all(block):
        return spread_out(jnp.broadcast_to(block[None], (groups, *block.shape)), "dp")

    my_taps = lax.dynamic_slice_in_dim(raw_taps, my_group * share, share, 0)
    my_taps = shrink(my_taps).astype(bf16).reshape(share, kern, chan).transpose(1, 0, 2)
    my_taps = spread_out(my_taps, "kern")
    limits = total_taps - lax.dynamic_slice_in_dim(pad_lengths, me * chan, chan, 0)[None]

    heads, arrived = [], []
    for b in seqs:
        head = project(words, b, tokens, first_gain, in_weight, kern, b > 0)
        words = after(head[0], words)
        heads.append(head)
        if b == 0:
            moved.append(my_taps)
        arrived.append(across(head[2], -1))
        if b == 0:
            all_taps = to_all(my_taps)
            moved.append([*arrived[0], all_taps])

    kernel_spec = tap_spectrum(words, all_taps, limits, tabs)
    words = after(kernel_spec, words)

    convs, returned = [], []
    for b in seqs:
        conv = convolve(words, arrived[b], kern, kernel_spec, tabs, False, None, True)
        words = after(conv[1], words)
        convs.append(conv)
        returned.append(across(conv[0], 1))

    mids, arrived_back = [], []
    earlier, out_tokens = None, None
    for b in seqs:
        mid, grads, pieces = feed_forward(
            words,
            b,
            tokens,
            cotangent,
            heads[b][1],
            returned[b],
            heads[b][0],
            out_weight,
            up_weight,
            down_weight,
            second_gain,
            kern,
            groups,
            True,
            earlier,
            out_tokens,
        )
        words = after(mid[3], words)
        out_tokens, second_row = mid[0], mid[3]
        earlier = [*grads, second_row]
        mids.append(mid)
        arrived_back.append(across(pieces, -1))
        if b == seq_count - 1:
            grads = after(moved[-2], grads)
    u_keep, u_give, d_keep, d_give, out_t, gate_t = grads
    wide_sums = Folding(u_keep, u_give, d_keep, d_give)

    corrs, signal_back = [], []
    for b in seqs:
        last = b == seq_count - 1
        corr = convolve(
            words, arrived_back[b], kern, kernel_spec, tabs, True, convs[b][1], not last
        )
        words = after(corr[1], words)
        corrs.append(corr)
        signal_back.append(across(corr[0], 1))
        if b == 0:
            words = after(wide_sums.step(words, 1), words)

    grad_taps = tap_gradient(words, [corr[1] for corr in corrs], limits, tabs, kern, groups)
    words = after(grad_taps, words)
    grad_taps = added(spread_out(grad_taps, "dp")).astype(bf16)
    grad_taps = spread_out(grad_taps, "kern").transpose(1, 0, 2).reshape(share, feat)
    grad_taps = to_all(grad_taps).reshape(local_taps, feat).astype(f32)
    grad_raw = grad_taps * shrink_slope(raw_taps)

    earlier, grad_tokens = None, None
    for b in seqs:
        last = b == seq_count - 1
        tail = finish(
            words,
            b,
            tokens,
            heads[b][0],
            mids[b][1],
            mids[b][2],
            signal_back[b],
            in_weight,
            first_gain,
            kern,
            groups,
            earlier,
            grad_tokens,
            [gate_t, out_t, second_row] if last else None,
        )
        words = after(tail[1], words)
        grad_tokens = tail[0]
        if not last:
            earlier = [tail[2], tail[1]]
            if b == 0:
                words = after(wide_sums.step(words, 2), words)

    late = Folding(*tail[1:])
    words = after(wide_sums.step(words, 3), words)
    words = after(late.step(words, 1), words)
    words = after(wide_sums.step(words, 4), words)
    words = after(late.step(words, 2), words)

    def up_out(block, up_ref, down_ref):
        up_ref[:deep] = block[:, : block.shape[1] // 2]
        up_ref[deep:] = block[:, block.shape[1] // 2 :]

    def down_out(block, up_ref, down_ref):
        down_ref[...] = block.T

    up_shape = (2 * deep, width // groups)
    down_shape = (width // kern, deep)
    sum_up, sum_down = wide_sums.finish(
        words, (up_out, (up_shape, down_shape), down_out)
    )
    words = after(sum_up, words)
    words = after(late.step(words, 3), words)
    words = after(late.step(words, 4), words)

    def late_first(block, in_ref, out_ref, one_ref, two_ref):
        in_ref[:, :late_rows] = late_unpack(block).T

    def late_second(block, in_ref, out_ref, one_ref, two_ref):
        block = late_unpack(block)
        left = in_rows - late_rows
        in_ref[:, late_rows:] = block[:left].T
        out_ref[...] = block[left : left + deep].T
        one_ref[...] = block[left + deep : left + deep + 1]
        two_ref[...] = block[left + deep + 1 : left + deep + 2]

    sum_in, sum_out, first_row, second_row = late.finish(
        words,
        (late_first, ((chan, in_rows), (chan, deep), (1, chan), (1, chan)), late_second),
    )

    return (
        out_tokens,
        grad_tokens,
        sum_in,
        sum_out,
        sum_up,
        sum_down,
        first_row[0],
        second_row[0],
        grad_raw,
    )


def solution(mesh):
    placed = (
        P("dp", "kern", None),
        P("dp", "kern", None),
        P(),
        P(),
        P(),
        P(),
        P(),
        P(),
        P("kern", None),
        P(),
    )
    placed_out = (
        P("dp", "kern", None),
        P("dp", "kern", None),
        P("kern", "dp"),
        P("kern", "dp"),
        P("kern", "dp"),
        P("kern", "dp"),
        P("kern"),
        P("kern"),
        P("kern", None),
    )
    groups, kern = mesh.shape["dp"], mesh.shape["kern"]

    def layer(*arrays):
        seq_count, length, feat = arrays[0].shape
        width = arrays[4].shape[1]
        rows = length // kern
        tiles = (
            feat % (16 * groups) == 0
            and width % (128 * groups) == 0
            and width == groups // 2 * feat
            and groups == 8
            and kern == 4
            and rows % (2 * inner) == 0
            and 3 * feat // groups + 2 <= 2 * late_rows
            and feat // kern == 192
        )
        return run(shards if tiles else shards_general)(*arrays)

    def run(body):
        return jax.shard_map(
            body,
            mesh=mesh,
            in_specs=placed,
            out_specs=placed_out,
            check_vma=False,
        )

    return layer
```

```python
import math

import jax
import jax.numpy as jnp
import ml_dtypes
import numpy as np
from jax import lax
from jax.experimental import pallas as pl
from jax.experimental.pallas import tpu as pltpu
from jax.sharding import PartitionSpec as P

shrink_level = 0.003
norm_eps = 1e-05
bf16 = jnp.bfloat16
f32 = jnp.float32
inner = 128
group = 16
wide = 8


def inner_tables(outer):
    length = outer * inner
    k1 = np.arange(outer)[:, None, None]
    k2 = np.arange(inner)[None, :, None]
    n2 = np.arange(inner)[None, None, :]
    turns = (n2 * (4 * (outer * k2 + k1) + 1)) % (4 * length)
    angle = turns * (2 * math.pi / (4 * length))
    c, s = np.cos(angle), np.sin(angle)
    table = np.concatenate([np.concatenate([c, s], 2), np.concatenate([-s, c], 2)], 1)
    return table.astype(ml_dtypes.bfloat16)


def outer_tables(outer):
    k1 = np.arange(outer)[:, None]
    n1 = np.arange(outer)[None, :]
    angle = (n1 * (4 * k1 + 1)) % (4 * outer) * (2 * math.pi / (4 * outer))
    parts = np.stack([np.cos(angle), -np.sin(angle)], 1)
    table = np.einsum("kcn,ij->kcinj", parts, np.eye(group))
    table = table.reshape(outer * 2 * group, outer * group)
    return table.astype(ml_dtypes.bfloat16), table.T.astype(ml_dtypes.bfloat16)


def all_tables(outer):
    first, last = outer_tables(outer)
    tabs = {"inner": inner_tables(outer), "first": first, "last": last}
    return {key: jnp.asarray(value) for key, value in tabs.items()}


def outer_forward(x_ref, table_ref, y_ref):
    outer, _, ch = x_ref.shape

    def step(j, carry):
        rows = pl.ds(pl.multiple_of(j * group, group), group)
        x = x_ref[:, rows, :].reshape(outer * group, ch)
        y = jnp.dot(table_ref[...], x, preferred_element_type=f32).astype(bf16)
        y = y.reshape(outer, 2, group, ch)
        y_ref[:, 0, rows, :] = y[:, 0]
        y_ref[:, 1, rows, :] = y[:, 1]
        return carry

    lax.fori_loop(0, inner // group, step, 0, unroll=8)


def outer_back(w_ref, table_ref, x_ref):
    outer, _, _, ch = w_ref.shape

    def step(j, carry):
        rows = pl.ds(pl.multiple_of(j * group, group), group)
        w = w_ref[:, :, rows, :].reshape(outer * 2 * group, ch)
        x = jnp.dot(table_ref[...], w, preferred_element_type=f32)
        x_ref[:, rows, :] = x.astype(x_ref.dtype).reshape(outer, group, ch)
        return carry

    lax.fori_loop(0, inner // group, step, 0, unroll=8)


def whole(shape):
    return pl.BlockSpec(shape, lambda i: (0,) * len(shape))


def slab(*shape):
    return pl.BlockSpec((wide,) + shape, lambda i: (i,) + (0,) * len(shape))


def smem():
    return pl.BlockSpec(memory_space=pltpu.SMEM)


def params(mib):
    return pltpu.CompilerParams(
        vmem_limit_bytes=mib * 2**20, dimension_semantics=("arbitrary",)
    )


def cost(micros):
    return pl.CostEstimate(
        flops=int(micros * 8e8), bytes_accessed=int(micros * 1e6), transcendentals=0
    )


def tap_spectrum(words, taps, limits, tabs):
    groups, kern, share, ch = taps.shape
    length = groups * kern * share
    outer = length // inner

    def kernel(_, taps_ref, limit_ref, table_ref, first_ref, out_ref, x_ref, y_ref, flat_ref):
        @pl.when(pl.program_id(0) == 0)
        def _():
            for z in range(kern):
                for p in range(groups):
                    at = (z * groups + p) * share
                    flat_ref[at : at + share] = taps_ref[p, z].astype(f32)
            values = flat_ref[...]
            edge = jnp.zeros((1, ch), f32)
            below = jnp.concatenate([edge, values[:-1]], 0)
            above = jnp.concatenate([values[1:], edge], 0)
            index = lax.broadcasted_iota(jnp.int32, (length, ch), 0)
            values = jnp.where(index < limit_ref[...], (below + values + above) / 3.0, 0.0)
            x_ref[...] = values.astype(bf16).reshape(outer, inner, ch)
            outer_forward(x_ref, first_ref, y_ref)

        for i in range(wide):
            y = y_ref[pl.program_id(0) * wide + i].reshape(2 * inner, ch)
            s = jnp.dot(table_ref[i], y, preferred_element_type=f32)
            out_ref[i] = (s * (1.0 / length)).astype(bf16)

    return pl.pallas_call(
        kernel,
        grid=(outer // wide,),
        in_specs=[
            smem(),
            whole(taps.shape),
            whole((1, ch)),
            slab(2 * inner, 2 * inner),
            whole(tabs["first"].shape),
        ],
        out_specs=slab(2 * inner, ch),
        out_shape=jax.ShapeDtypeStruct((outer, 2 * inner, ch), bf16),
        scratch_shapes=[
            pltpu.VMEM((outer, inner, ch), bf16),
            pltpu.VMEM((outer, 2, inner, ch), bf16),
            pltpu.VMEM((length, ch), f32),
        ],
        compiler_params=params(56),
        cost_estimate=cost(6),
        name="tap_spectrum",
    )(words, taps, limits, tabs["inner"], tabs["first"])


def packed(rows, ch):
    if ch % 128 == 64 and rows % (2 * inner) == 0:
        return (rows // inner * (2 * ch // 128) // 2, inner, 128)
    return (rows // inner, inner, ch)


def pack(ref, lead, values, part, parts):
    rows, ch = values.shape
    blocks = rows // inner
    if ref.shape[-1] == ch:
        ref[(*lead, pl.ds(part * blocks, blocks))] = values.reshape(blocks, inner, ch)
        return
    full = ch // 128
    for j in range(full):
        at = (j * parts + part) * blocks
        lanes = values[:, j * 128 : (j + 1) * 128]
        ref[(*lead, pl.ds(at, blocks))] = lanes.reshape(blocks, inner, 128)
    rest = values[:, full * 128 :]
    half = parts * blocks // 2
    for t in range(blocks):
        at = part * blocks + t
        side, row = at // half, at % half
        ref[(*lead, full * parts * blocks + row, slice(None), slice(side * 64, side * 64 + 64))] = (
            rest[t * inner : (t + 1) * inner]
        )


def unpack(ref, lead, part, parts, ch, blocks):
    if ref.shape[-1] == ch:
        return [(0, ref[(*lead, pl.ds(part * blocks, blocks))])]
    full = ch // 128
    out = []
    for j in range(full):
        at = (j * parts + part) * blocks
        out.append((j * 128, ref[(*lead, pl.ds(at, blocks))]))
    half = parts * blocks // 2
    rest = []
    for t in range(blocks):
        at = part * blocks + t
        side, row = at // half, at % half
        rest.append(
            ref[(*lead, full * parts * blocks + row, slice(None), slice(side * 64, side * 64 + 64))]
        )
    out.append((full * 128, jnp.stack(rest)))
    return out


def owners(me_ref, refs, kern, sign):
    if len(refs) == 1 and kern > 1:
        return [(refs[0], (k,), k) for k in range(kern)]
    return [
        (ref, (), lax.rem(me_ref[0] + (k if sign > 0 else kern - k), kern))
        for k, ref in enumerate(refs)
    ]


def piece_shapes(kern, rows, ch, stacked):
    shape = packed(rows, ch)
    return [(kern, *shape)] if stacked else [shape] * kern


def place_pieces(me_ref, piece_refs, x_ref, kern):
    outer, _, ch = x_ref.shape
    blocks = outer // kern
    for ref, lead, owner in owners(me_ref, piece_refs, kern, 1):
        for at, block in unpack(ref, lead, 0, 1, ch, blocks):
            x_ref[pl.ds(owner * blocks, blocks), :, at : at + block.shape[2]] = block


def take_pieces(me_ref, x_ref, piece_refs, kern):
    outer, _, ch = x_ref.shape
    blocks = outer // kern
    for ref, lead, owner in owners(me_ref, piece_refs, kern, 1):
        pack(ref, lead, x_ref[pl.ds(owner * blocks, blocks)].reshape(blocks * inner, ch), 0, 1)


def convolve(me, pieces, kern, kernel_spec, tabs, flip, other_spec=None, stacked=False):
    count = len(pieces)
    outer, _, ch = kernel_spec.shape
    shapes = piece_shapes(kern, outer * inner // kern, ch, stacked)

    def kernel(me_ref, *refs):
        piece_refs, refs = refs[:count], refs[count:]
        spec_ref, table_ref, first_ref, last_ref = refs[:4]
        refs = refs[4:]
        if flip:
            other_ref, refs = refs[0], refs[1:]
        out_refs, refs = refs[: len(shapes)], refs[len(shapes) :]
        save_ref, x_ref, y_ref, w_ref = refs
        step = pl.program_id(0)

        @pl.when(step == 0)
        def _():
            place_pieces(me_ref, piece_refs, x_ref, kern)
            outer_forward(x_ref, first_ref, y_ref)

        for i in range(wide):
            at = step * wide + i
            y = y_ref[at].reshape(2 * inner, ch)
            s = jnp.dot(table_ref[i], y, preferred_element_type=f32)
            sr, si = s[:inner], s[inner:]
            kr = spec_ref[i, :inner].astype(f32)
            ki = spec_ref[i, inner:].astype(f32)
            if flip:
                orr = other_ref[i, :inner].astype(f32)
                oi = other_ref[i, inner:].astype(f32)
                save_ref[i, :inner] = (sr * orr + si * oi).astype(bf16)
                save_ref[i, inner:] = (si * orr - sr * oi).astype(bf16)
                zr, zi = sr * kr + si * ki, si * kr - sr * ki
            else:
                save_ref[i] = s.astype(bf16)
                zr, zi = sr * kr - si * ki, sr * ki + si * kr
            z = jnp.concatenate([zr, zi], 0).astype(bf16)
            w = mm_tn(table_ref[i], z)
            w_ref[at] = w.astype(bf16).reshape(2, inner, ch)

        @pl.when(step == pl.num_programs(0) - 1)
        def _():
            outer_back(w_ref, last_ref, x_ref)
            take_pieces(me_ref, x_ref, out_refs, kern)

    args = [me, *pieces, kernel_spec, tabs["inner"], tabs["first"], tabs["last"]]
    in_specs = [smem()] + [whole(piece.shape) for piece in pieces] + [
        slab(2 * inner, ch),
        slab(2 * inner, 2 * inner),
        whole(tabs["first"].shape),
        whole(tabs["last"].shape),
    ]
    if flip:
        args.append(other_spec)
        in_specs.append(slab(2 * inner, ch))
    outs = pl.pallas_call(
        kernel,
        grid=(outer // wide,),
        in_specs=in_specs,
        out_specs=[whole(shape) for shape in shapes] + [slab(2 * inner, ch)],
        out_shape=[jax.ShapeDtypeStruct(shape, bf16) for shape in shapes]
        + [jax.ShapeDtypeStruct((outer, 2 * inner, ch), bf16)],
        scratch_shapes=[
            pltpu.VMEM((outer, inner, ch), bf16),
            pltpu.VMEM((outer, 2, inner, ch), bf16),
            pltpu.VMEM((outer, 2, inner, ch), bf16),
        ],
        compiler_params=params(56),
        cost_estimate=cost(8),
        name="correlate" if flip else "convolve",
    )(*args)
    return list(outs[:-1]), outs[-1]


def tap_gradient(words, products, limits, tabs, out_shapes, write):
    outer, _, ch = products[0].shape
    length = outer * inner

    def kernel(word_ref, limit_ref, *refs):
        spec_refs, refs = refs[: len(products)], refs[len(products) :]
        table_ref, last_ref, refs = refs[0], refs[1], refs[2:]
        out_refs, (w_ref, x_ref, t_ref) = refs[: len(out_shapes)], refs[len(out_shapes) :]
        step = pl.program_id(0)
        for i in range(wide):
            z = spec_refs[0][i].astype(f32)
            for spec_ref in spec_refs[1:]:
                z = z + spec_ref[i].astype(f32)
            w = mm_tn(table_ref[i], (z * (1.0 / length)).astype(bf16))
            w_ref[step * wide + i] = w.astype(bf16).reshape(2, inner, ch)

        @pl.when(step == pl.num_programs(0) - 1)
        def _():
            outer_back(w_ref, last_ref, x_ref)
            taps = x_ref[...].reshape(length, ch)
            index = lax.broadcasted_iota(jnp.int32, (length, ch), 0)
            taps = jnp.where(index < limit_ref[...], taps, 0.0)
            edge = jnp.zeros((1, ch), f32)
            below = jnp.concatenate([edge, taps[:-1]], 0)
            above = jnp.concatenate([taps[1:], edge], 0)
            t_ref[...] = ((below + taps + above) / 3.0).astype(bf16)
            write(word_ref, t_ref, out_refs)

    return pl.pallas_call(
        kernel,
        grid=(outer // wide,),
        in_specs=[smem(), whole((1, ch))]
        + [slab(2 * inner, ch)] * len(products)
        + [slab(2 * inner, 2 * inner), whole(tabs["last"].shape)],
        out_specs=[whole(shape) for shape in out_shapes],
        out_shape=[jax.ShapeDtypeStruct(shape, bf16) for shape in out_shapes],
        scratch_shapes=[
            pltpu.VMEM((outer, 2, inner, ch), bf16),
            pltpu.VMEM((outer, inner, ch), f32),
            pltpu.VMEM((length, ch), bf16),
        ],
        compiler_params=params(56),
        cost_estimate=cost(5),
        name="tap_gradient",
    )(words, limits, *products, tabs["inner"], tabs["last"])


def exchange(pieces, sign):
    count = len(pieces)
    moved = [pieces[0]]
    for k in range(1, count):
        route = [(i, (i + sign * k) % count) for i in range(count)]
        moved.append(lax.ppermute(pieces[k], "kern", route))
    return moved


def spread_out(block, axis_name, groups=None):
    return lax.all_to_all(
        block, axis_name, split_axis=0, concat_axis=0, tiled=True, axis_index_groups=groups
    )


def sum_all(row):
    for axis_name in ("dp", "kern"):
        count = lax.axis_size(axis_name)
        for bit in range(count.bit_length() - 1):
            route = [(i, i ^ (1 << bit)) for i in range(count)]
            row = row + lax.ppermute(row, axis_name, route)
    return row


def padded_rows(block):
    count = lax.axis_size("kern")
    forward = [(i, i + 1) for i in range(count - 1)]
    backward = [(target, source) for source, target in forward]
    low = lax.ppermute(block[-1:], "kern", forward)
    high = lax.ppermute(block[:1], "kern", backward)
    return jnp.concatenate([low, block, high], axis=0)


def layer_norm(values, norm_gain):
    center = values - jnp.mean(values, axis=-1, keepdims=True)
    spread = jnp.mean(center * center, axis=-1, keepdims=True)
    return center * lax.rsqrt(spread + norm_eps) * norm_gain


def shrink(tap_values):
    return tap_values - shrink_level * tap_values / jnp.sqrt(
        tap_values * tap_values + shrink_level * shrink_level
    )


def shrink_slope(tap_values):
    return 1.0 - shrink_level**3 / (tap_values * tap_values + shrink_level * shrink_level) ** 1.5


def pool_three(padded):
    return (padded[:-2] + padded[1:-1] + padded[2:]) / 3.0


def dot(left, right, dims):
    return lax.dot_general(left, right, (dims, ((), ())), preferred_element_type=f32)


def shards_general(
    tokens,
    cotangent,
    in_weight,
    out_weight,
    up_weight,
    down_weight,
    first_gain,
    second_gain,
    raw_taps,
    pad_lengths,
):
    seq_count, row_count, feat = tokens.shape
    kern = lax.axis_size("kern")
    me = lax.axis_index("kern")
    me_word = me.astype(jnp.int32).reshape(1)
    groups = lax.axis_size("dp")
    local_taps = raw_taps.shape[0]
    total_taps = local_taps * kern
    chan = feat // kern
    outer = row_count * kern // inner
    blocks = row_count // inner
    tabs = all_tables(outer)

    limits = total_taps - lax.dynamic_slice_in_dim(pad_lengths, me * chan, chan, 0)[None]
    my_raw = lax.all_to_all(raw_taps, "kern", split_axis=1, concat_axis=0, tiled=True)
    kernel_spec = tap_spectrum(me_word, shrink(my_raw)[None, None], limits, tabs)

    def apart(values):
        values = values.reshape(blocks, inner, kern, chan).transpose(2, 0, 1, 3)
        return [values[(me - k) % kern] for k in range(kern)]

    def joined(pieces):
        stack = jnp.stack(pieces)
        stack = jnp.stack([stack[(me - k) % kern] for k in range(kern)])
        return stack.transpose(1, 2, 0, 3).reshape(row_count, feat)

    def one(x, cot):
        inputs = x.astype(f32)
        first_norm, first_pull = jax.vjp(layer_norm, inputs, first_gain)
        normed = first_norm.astype(bf16)
        projected = dot(normed, in_weight, ((1,), (0,)))
        gate = projected[:, feat:]
        pieces = exchange(apart(projected[:, :feat].astype(bf16)), -1)
        pieces, spectrum = convolve(me_word, pieces, kern, kernel_spec, tabs, False)
        convolved = joined(exchange(pieces, 1)).astype(f32)
        mixed = (gate * convolved).astype(bf16)
        middle = inputs + dot(mixed, out_weight, ((1,), (0,)))
        second_norm, second_pull = jax.vjp(layer_norm, middle, second_gain)
        normed_two = second_norm.astype(bf16)
        raised = dot(normed_two, up_weight, ((1,), (0,)))
        activated, gelu_pull = jax.vjp(jax.nn.gelu, raised)
        hidden = activated.astype(bf16)
        out = (middle + dot(hidden, down_weight, ((1,), (0,)))).astype(bf16)
        grad_raised = gelu_pull(dot(cot, down_weight, ((1,), (1,))))[0].astype(bf16)
        grad_mid, second_row = second_pull(dot(grad_raised, up_weight, ((1,), (1,))))
        grad_mid = cot.astype(f32) + grad_mid
        branch = grad_mid.astype(bf16)
        grad_mixed = dot(branch, out_weight, ((1,), (1,)))
        grad_gate = (grad_mixed * convolved).astype(bf16)
        pieces = exchange(apart((grad_mixed * gate).astype(bf16)), -1)
        pieces, product = convolve(me_word, pieces, kern, kernel_spec, tabs, True, spectrum)
        grad_signal = joined(exchange(pieces, 1))
        grad_projected = jnp.concatenate([grad_signal, grad_gate], axis=-1)
        grad_first, first_row = first_pull(dot(grad_projected, in_weight, ((1,), (1,))))
        weights = (
            dot(normed, grad_projected, ((0,), (0,))),
            dot(mixed, branch, ((0,), (0,))),
            dot(normed_two, grad_raised, ((0,), (0,))),
            dot(hidden, cot, ((0,), (0,))),
        )
        return out, (grad_mid + grad_first).astype(bf16), product, (first_row, second_row), weights

    ones = [one(tokens[b], cotangent[b]) for b in range(seq_count)]
    rows, weights = ones[0][3:]
    for other in ones[1:]:
        rows, weights = jax.tree.map(jnp.add, (rows, weights), other[3:])
    def write(_, taps_ref, out_refs):
        out_refs[0][...] = taps_ref[...]

    products = [item[2] for item in ones]
    shapes = [(total_taps, chan)]
    grad_taps = tap_gradient(me_word, products, limits, tabs, shapes, write)[0]
    grad_taps = lax.all_to_all(grad_taps, "kern", split_axis=0, concat_axis=1, tiled=True)
    grad_raw = lax.psum(grad_taps, "dp").astype(f32) * shrink_slope(raw_taps)
    sums = []
    for weight in weights:
        weight = lax.psum_scatter(weight.astype(bf16), "dp", scatter_dimension=1, tiled=True)
        weight = lax.psum_scatter(weight, "kern", scatter_dimension=0, tiled=True)
        sums.append(weight.astype(f32))
    gains = sum_all(jnp.stack(rows))
    gains = lax.dynamic_slice_in_dim(gains, me * chan, chan, 1)
    return (
        jnp.stack([item[0] for item in ones]),
        jnp.stack([item[1] for item in ones]),
        *sums,
        gains[0],
        gains[1],
        grad_raw,
    )


def row_mean(values):
    return jnp.mean(values, axis=-1, keepdims=True)


def centered(values):
    center = values - row_mean(values)
    inverse = lax.rsqrt(row_mean(center * center) + norm_eps)
    return center * inverse, inverse


def norm_back(grad, normed, inverse, gain):
    scaled = grad * gain
    return inverse * (scaled - row_mean(scaled) - normed * row_mean(scaled * normed))


def mm(left, right):
    return jnp.dot(left, right, preferred_element_type=f32)


def mm_nt(left, right):
    return lax.dot_general(left, right, (((1,), (1,)), ((), ())), preferred_element_type=f32)


def mm_tn(left, right):
    return lax.dot_general(left, right, (((0,), (0,)), ((), ())), preferred_element_type=f32)


def fixed(shape):
    return pl.BlockSpec(shape, lambda *_: (0,) * len(shape))


def once(shape):
    return pl.BlockSpec(
        shape, lambda *_: (0,) * len(shape), pipeline_mode=pl.Buffered(1)
    )


def along(seq, rows, feat):
    return pl.BlockSpec((1, rows, feat), lambda i: (seq, i, 0))


def cut(me_ref, values, piece_refs, stack_ref, part=0, parts=1):
    kern, rows, ch = stack_ref.shape
    if len(piece_refs) > 1:
        for k in range(kern):
            stack_ref[k] = values[:, k * ch : (k + 1) * ch]
    for ref, lead, owner in owners(me_ref, piece_refs, kern, -1):
        block = stack_ref[owner] if len(piece_refs) > 1 else values[:, owner * ch : (owner + 1) * ch]
        pack(ref, lead, block, part, parts)


def join(me_ref, piece_refs, stack_ref, out_ref, part=0, parts=1):
    kern, rows, ch = stack_ref.shape
    blocks = rows // inner
    for ref, lead, owner in owners(me_ref, piece_refs, kern, -1):
        for at, block in unpack(ref, lead, part, parts, ch, blocks):
            width = block.shape[2]
            block = block.reshape(rows, width)
            if len(piece_refs) > 1:
                stack_ref[owner, :, at : at + width] = block
            else:
                out_ref[:, owner * ch + at : owner * ch + at + width] = block
    if len(piece_refs) > 1:
        for k in range(kern):
            out_ref[:, k * ch : (k + 1) * ch] = stack_ref[k]


def project(me, seq, tokens, gain, weight, kern, stacked):
    _, rows, feat = tokens.shape
    chan = feat // kern
    tile = rows // 2
    shapes = piece_shapes(kern, rows, chan, stacked)

    def kernel(me_ref, x_ref, gain_ref, weight_ref, *refs):
        normed_ref, gate_ref = refs[:2]
        piece_refs, stack_ref = refs[2:-1], refs[-1]
        hat, _ = centered(x_ref[0].astype(f32))
        normed = (hat * gain_ref[...]).astype(bf16)
        normed_ref[...] = normed
        projected = mm(normed, weight_ref[...])
        gate_ref[...] = projected[:, feat:]
        signal = projected[:, :feat].astype(bf16)
        for part in range(2):
            pl.when(pl.program_id(0) == part)(
                lambda: cut(me_ref, signal, piece_refs, stack_ref, part, 2)
            )

    outs = pl.pallas_call(
        kernel,
        grid=(2,),
        in_specs=[smem(), along(seq, tile, feat), fixed((feat,)), fixed(weight.shape)],
        out_specs=[
            pl.BlockSpec((tile, feat), lambda i: (i, 0)),
            pl.BlockSpec((tile, feat), lambda i: (i, 0)),
        ]
        + [fixed(shape) for shape in shapes],
        out_shape=[
            jax.ShapeDtypeStruct((rows, feat), bf16),
            jax.ShapeDtypeStruct((rows, feat), f32),
        ]
        + [jax.ShapeDtypeStruct(shape, bf16) for shape in shapes],
        scratch_shapes=[pltpu.VMEM((kern, tile, chan), bf16)],
        compiler_params=params(56),
        cost_estimate=cost(4),
        name="project",
    )(me, tokens, gain, weight)
    return outs[0], outs[1], list(outs[2:])


def gelu_pair(raised):
    root = math.sqrt(2.0 / math.pi)
    square = raised * raised
    t = jnp.tanh(raised * (root + (root * 0.044715) * square))
    half = 0.5 + 0.5 * t
    slope = half + (0.5 * raised) * (1.0 - t * t) * (root + (3.0 * root * 0.044715) * square)
    return raised * half, slope


def own_pair(words):
    return 2 * words[3] + words[2]


def grad_hidden(words, cots, down_weight):
    seqs, rows, feat = cots.shape
    width = down_weight.shape[0]
    chunk = feat

    def kernel(_, cot_ref, down_ref, out_ref):
        out = mm_nt(cot_ref[...].reshape(seqs * rows, feat), down_ref[...])
        out_ref[...] = out.astype(bf16).reshape(seqs, rows, chunk)

    return pl.pallas_call(
        kernel,
        grid=(width // chunk,),
        in_specs=[smem(), fixed(cots.shape), pl.BlockSpec((chunk, feat), lambda i: (i, 0))],
        out_specs=pl.BlockSpec((seqs, rows, chunk), lambda i: (0, 0, i)),
        out_shape=jax.ShapeDtypeStruct((seqs, rows, width), bf16),
        compiler_params=params(56),
        cost_estimate=cost(6),
        name="grad_hidden",
    )(words, cots, down_weight)


def flipped(place):
    return 2 * (place & 1) + (place >> 1)


def feed_forward(words, seq, tokens, cots, grads, gate, conv, normed, out_weight, up_weight, down_weight, gain, kern, groups, stacked, earlier, out_before):
    seqs, rows, feat = tokens.shape
    width = up_weight.shape[1]
    count = len(conv)
    shapes = piece_shapes(kern, rows, feat // kern, stacked)
    chan = feat // kern
    pairs = groups // 2
    chunk = width // pairs
    deep = feat // groups
    half = chunk // 2
    add = earlier is not None

    def kernel(word_ref, x_ref, cot_ref, gh_ref, gate_ref, normed_ref, ow_ref, up_ref, down_ref, gain_ref, *refs):
        conv_refs, refs = refs[:count], refs[count:]
        if add:
            old, refs = refs[:7], refs[8:]
        out_ref, mid_ref, ggate_ref, ggain_ref = refs[:4]
        u_keep, u_give, d_keep, d_give, o_ref, g_ref = refs[4:10]
        piece_refs, refs = refs[10 : 10 + len(shapes)], refs[10 + len(shapes) :]
        stack_s, cv, mixed_s, middle_s, n2_s, acc_s, back_s = refs
        f = pl.program_id(0)
        cot = cot_ref.at[0]

        @pl.when(f == 0)
        def _():
            join(word_ref, conv_refs, stack_s, cv)
            mixed = (gate_ref[...] * cv[...].astype(f32)).astype(bf16)
            mixed_s[...] = mixed
            middle = x_ref[0].astype(f32) + mm(mixed, ow_ref[...])
            middle_s[...] = middle
            hat, _ = centered(middle)
            n2_s[...] = (hat * gain_ref[...]).astype(bf16)
            acc_s[...] = middle
            back_s[...] = jnp.zeros_like(back_s)

        hidden, grad_raised = [], []
        for at in range(0, rows, rows // 2):
            part = slice(at, at + rows // 2)
            act, slope = gelu_pair(mm(n2_s[part], up_ref[...]))
            hidden.append(act.astype(bf16))
            grad_raised.append((gh_ref[0, part].astype(f32) * slope).astype(bf16))
        hidden = jnp.concatenate(hidden, 0)
        grad_raised = jnp.concatenate(grad_raised, 0)
        acc_s[...] += mm(hidden, down_ref[...])
        back_s[...] += mm_nt(grad_raised, up_ref[...])
        u = mm_tn(n2_s[...], grad_raised).astype(bf16)
        d = mm_tn(cot[...], hidden).astype(bf16).reshape(pairs, 2, deep, chunk)
        even = word_ref[1] == 0
        for to, u_ref, d_ref, u_old, d_old in (
            (0, u_keep, d_keep, 0, 2),
            (1, u_give, d_give, 1, 3),
        ):
            for pair in range(pairs):
                at = pair ^ own_pair(word_ref)
                part = jnp.where(even, d[pair, to], d[pair, 1 - to])
                d_ref[at, 0] = part + old[d_old][at, 0] if add else part
            uu = jnp.where(
                even,
                u[:, to * half : (to + 1) * half],
                u[:, (1 - to) * half : (2 - to) * half],
            ).reshape(kern, 2, deep, half)
            for z in range(kern):
                at = flipped(z ^ word_ref[0])
                part = jnp.concatenate([uu[z, 0], uu[z, 1]], axis=1)
                u_ref[0, at] = part + old[u_old][0, at] if add else part

        @pl.when(f == pairs - 1)
        def _():
            out_ref[0] = acc_s[...].astype(bf16)
            hat, inverse = centered(middle_s[...])
            back = back_s[...]
            ggain = jnp.sum(back * hat, axis=0, keepdims=True)
            grad_mid = cot[...].astype(f32) + norm_back(back, hat, inverse, gain_ref[...])
            mid_ref[...] = grad_mid
            branch = grad_mid.astype(bf16)
            grad_mixed = mm_nt(branch, ow_ref[...])
            ggate = (grad_mixed * cv[...].astype(f32)).astype(bf16)
            ggate_ref[...] = ggate
            cut(word_ref, (grad_mixed * gate_ref[...]).astype(bf16), piece_refs, stack_s)
            o = mm_tn(branch, mixed_s[...])
            g = mm_tn(ggate, normed_ref[...])
            if add:
                ggain = ggain + old[6][...]
                o = o + old[4][...].astype(f32)
                g = g + old[5][...].astype(f32)
            ggain_ref[...] = ggain
            o_ref[...] = o.astype(bf16)
            g_ref[...] = g.astype(bf16)

    u_spec = pl.BlockSpec((1, kern, deep, chunk), lambda f, w: (flipped(f ^ own_pair(w)), 0, 0, 0))
    d_spec = pl.BlockSpec((pairs, 1, deep, chunk), lambda f, w: (0, flipped(f ^ w[0]), 0, 0))
    square = fixed((feat, feat))
    flat = fixed((rows, feat))
    one = pl.BlockSpec((1, rows, feat), lambda f, w: (seq, 0, 0))
    args = [words, tokens, cots, grads, gate, normed, out_weight, up_weight, down_weight, gain, *conv]
    in_specs = [
        one,
        one,
        pl.BlockSpec((1, rows, chunk), lambda f, w: (seq, 0, f)),
        once((rows, feat)),
        once((rows, feat)),
        once(out_weight.shape),
        pl.BlockSpec((feat, chunk), lambda f, w: (0, f)),
        pl.BlockSpec((chunk, feat), lambda f, w: (f, 0)),
        fixed((feat,)),
    ] + [fixed(piece.shape) for piece in conv]
    grad_specs = [u_spec, u_spec, d_spec, d_spec, square, square]
    aliases = {}
    if add:
        args += [*earlier, out_before]
        in_specs += [*grad_specs, fixed((1, feat)), pl.BlockSpec(memory_space=pl.ANY)]
        aliases = {len(args) - 1: 0}
    big = jax.ShapeDtypeStruct((pairs, kern, deep, chunk), bf16)
    outs = pl.pallas_call(
        kernel,
        grid_spec=pltpu.PrefetchScalarGridSpec(
            num_scalar_prefetch=1,
            grid=(pairs,),
            in_specs=in_specs,
            out_specs=[one, flat, flat, fixed((1, feat)), *grad_specs]
            + [fixed(shape) for shape in shapes],
            scratch_shapes=[
                pltpu.VMEM((kern, rows, feat // kern), bf16),
                pltpu.VMEM((rows, feat), bf16),
                pltpu.VMEM((rows, feat), bf16),
                pltpu.VMEM((rows, feat), f32),
                pltpu.VMEM((rows, feat), bf16),
                pltpu.VMEM((rows, feat), f32),
                pltpu.VMEM((rows, feat), f32),
            ],
        ),
        out_shape=[
            jax.ShapeDtypeStruct(tokens.shape, bf16),
            jax.ShapeDtypeStruct((rows, feat), f32),
            jax.ShapeDtypeStruct((rows, feat), bf16),
            jax.ShapeDtypeStruct((1, feat), f32),
            big,
            big,
            big,
            big,
            jax.ShapeDtypeStruct((feat, feat), bf16),
            jax.ShapeDtypeStruct((feat, feat), bf16),
        ]
        + [jax.ShapeDtypeStruct(shape, bf16) for shape in shapes],
        input_output_aliases=aliases,
        compiler_params=params(56),
        cost_estimate=cost(24),
        name="feed_forward",
    )(*args)
    return outs[:4], list(outs[4:10]), list(outs[10:])


late_rows = 160
late_packed = late_rows // 2 * 3


def finish(words, seq, tokens, normed, grad_mid, grad_gate, signal, weight, gain, kern, groups, earlier, out_before, others):
    seqs, rows, feat = tokens.shape
    count = len(signal)
    chan = feat // kern
    part = rows // 2
    add = earlier is not None
    last = others is not None
    pairs = groups // 2
    in_rows, out_rows = 2 * feat // groups, feat // groups

    def kernel(word_ref, x_ref, normed_ref, mid_ref, gate_ref, weight_ref, gain_ref, *refs):
        signal_refs, refs = refs[:count], refs[count:]
        if add:
            old_s, old_gain, refs = refs[0], refs[1], refs[3:]
        if last:
            gt_ref, ot_ref, row_ref, refs = refs[0], refs[1], refs[2], refs[3:]
            tap_refs, refs = refs[:4], refs[4:]
            out_ref, refs = refs[0], refs[1:]
            late_refs, refs = (refs[:2], refs[2:4]), refs[4:]
            ggain_ref, s_ref, stack_s, gs = refs
        else:
            out_ref, ggain_ref, s_ref, stack_s, gs = refs
        i = pl.program_id(0)
        for p in range(2):
            pl.when(i == p)(lambda: join(word_ref, signal_refs, stack_s, gs, p, 2))
        back = mm_nt(gs[...], weight_ref[:, :feat]) + mm_nt(gate_ref[...], weight_ref[:, feat:])
        hat, inverse = centered(x_ref[0].astype(f32))
        grad = mid_ref[...] + norm_back(back, hat, inverse, gain_ref[...])
        out_ref[0] = grad.astype(bf16)
        ggain = jnp.sum(back * hat, axis=0, keepdims=True)
        s = mm_tn(gs[...], normed_ref[...])

        @pl.when(i == 0)
        def _():
            ggain_ref[...] = ggain + old_gain[...] if add else ggain
            s_ref[...] = s + old_s[...] if add else s

        @pl.when(i != 0)
        def _():
            ggain_ref[...] += ggain
            s_ref[...] += s

        if last:

            @pl.when(i == 1)
            def _():
                for h in range(2):
                    for to in range(2):
                        late_refs[h][to][:, :, late_packed:] = tap_refs[2 * h + to][...]
                zero = jnp.zeros((2 * late_rows - in_rows - out_rows - 2, feat), f32)
                gains = jnp.concatenate([ggain_ref[...], row_ref[...], zero], 0).astype(bf16)
                for to, side in ((0, word_ref[1]), (1, 1 - word_ref[1])):
                    for pair in range(pairs):
                        from_ref = s_ref if pair < pairs // 2 else gt_ref
                        at_in = (2 * (pair % (pairs // 2)) + side) * in_rows
                        at_in = pl.multiple_of(at_in, in_rows)
                        at_out = pl.multiple_of((2 * pair + side) * out_rows, out_rows)
                        columns = from_ref[pl.ds(at_in, in_rows), :].astype(bf16)
                        values = [
                            columns[:late_rows],
                            jnp.concatenate(
                                [columns[late_rows:], ot_ref[pl.ds(at_out, out_rows), :], gains],
                                0,
                            ),
                        ]
                        at = pair ^ own_pair(word_ref)
                        for h in range(2):
                            place = flipped(at) if h == 0 else at
                            for z in range(kern):
                                late_pack(
                                    late_refs[h][to],
                                    (place, flipped(z ^ word_ref[0])),
                                    values[h][:, z * chan : (z + 1) * chan],
                                )

    tiled = pl.BlockSpec((part, feat), lambda i: (i, 0))
    args = [words, tokens, normed, grad_mid, grad_gate, weight, gain, *signal]
    in_specs = [
        smem(),
        along(seq, part, feat),
        tiled,
        tiled,
        tiled,
        fixed(weight.shape),
        fixed((feat,)),
    ] + [fixed(piece.shape) for piece in signal]
    aliases = {}
    if add:
        args += [*earlier, out_before]
        in_specs += [fixed((feat, feat)), fixed((1, feat)), pl.BlockSpec(memory_space=pl.ANY)]
        aliases = {len(args) - 1: 0}
    out_specs = [along(seq, part, feat)]
    out_shape = [jax.ShapeDtypeStruct(tokens.shape, bf16)]
    scratch = [
        pltpu.VMEM((kern, part, chan), bf16),
        pltpu.VMEM((part, feat), bf16),
    ]
    if last:
        args += others
        in_specs += [fixed((feat, feat)), fixed((feat, feat)), fixed((1, feat))]
        in_specs += [fixed(other.shape) for other in others[3:]]
        late = (pairs, kern, late_packed + others[3].shape[2], 128)
        out_specs += [fixed(late)] * 4
        out_shape += [jax.ShapeDtypeStruct(late, bf16)] * 4
        scratch = [pltpu.VMEM((1, feat), f32), pltpu.VMEM((feat, feat), f32)] + scratch
    else:
        out_specs += [fixed((1, feat)), fixed((feat, feat))]
        out_shape += [
            jax.ShapeDtypeStruct((1, feat), f32),
            jax.ShapeDtypeStruct((feat, feat), f32),
        ]
    return pl.pallas_call(
        kernel,
        grid=(2,),
        in_specs=in_specs,
        out_specs=out_specs,
        out_shape=out_shape,
        scratch_shapes=scratch,
        input_output_aliases=aliases,
        compiler_params=params(56),
        cost_estimate=cost(6),
        name="finish",
    )(*args)


def late_pack(ref, lead, values):
    rows = values.shape[0]
    half = rows // 2
    ref[(*lead, slice(0, rows))] = values[:, :128]
    ref[(*lead, slice(rows, rows + half), slice(0, 64))] = values[:half, 128:]
    ref[(*lead, slice(rows, rows + half), slice(64, 128))] = values[half:, 128:]


def late_unpack(block):
    rows = block.shape[-2] // 3 * 2
    half = rows // 2
    rest = block[..., rows:, :]
    rest = jnp.concatenate([rest[..., :64], rest[..., 64:]], axis=-2)
    return jnp.concatenate([block[..., :rows, :], rest], axis=-1)


def swap(block, axis_name, bit):
    route = [(i, i ^ (1 << bit)) for i in range(lax.axis_size(axis_name))]
    return lax.ppermute(block, axis_name, route)


def added(block):
    return jnp.sum(block.astype(f32), axis=0)


class Folding:
    bits = ((("dp", 1), ("dp", 2)), (("dp", 2), ("dp", 1)))

    def __init__(self, first, second):
        self.rows = first[0].shape[2]
        self.rest = first[0].shape[2:]
        self.mine = [first[0], second[0]]
        self.got = [swap(first[1], "dp", 0), swap(second[1], "dp", 0)]
        self.stage = 0

    def half(self, which, side):
        left = 3 - self.stage
        shape = (2, 2**left) + self.rest
        mine = self.mine[which].reshape(shape)
        got = self.got[which].reshape(shape)
        return mine[side].astype(f32) + got[side].astype(f32)

    def step(self):
        gives = [self.half(which, 1).astype(bf16) for which in range(len(self.mine))]
        self.mine = [self.half(which, 0).astype(bf16) for which in range(len(self.mine))]
        if self.stage < 2:
            self.got = [swap(give, *self.bits[which][self.stage]) for which, give in enumerate(gives)]
        else:
            if len(gives) > 1:
                gives = [jnp.concatenate(gives, axis=-2)]
                self.mine = [jnp.concatenate(self.mine, axis=-2)]
                self.rest = (2 * self.rows, self.rest[1])
            self.got = [swap(gives[0], "kern", self.stage - 2)]
        self.stage += 1
        return gives

    def take(self, rows):
        taken = []
        for which in range(2):
            shape = (2 ** (4 - self.stage),) + self.rest
            mine, got = self.mine[which].reshape(shape), self.got[which].reshape(shape)
            taken.append(mine[:, rows:].astype(f32) + got[:, rows:].astype(f32))
            self.mine[which], self.got[which] = mine[:, :rows], got[:, :rows]
        self.rows, self.rest = rows, (rows, self.rest[1])
        return [block.astype(bf16) for block in taken]

    def hold(self, anchor):
        self.mine = after(anchor, self.mine)

    def totals(self):
        block = self.mine[0].reshape(self.rest).astype(f32) + self.got[0].reshape(self.rest).astype(f32)
        return block[: self.rows], block[self.rows :]


def after(anchor, values):
    return lax.optimization_barrier((anchor, values))[1]


def shards(
    tokens,
    cotangent,
    in_weight,
    out_weight,
    up_weight,
    down_weight,
    first_gain,
    second_gain,
    raw_taps,
    pad_lengths,
):
    seq_count, row_count, feat = tokens.shape
    width = up_weight.shape[1]
    kern = lax.axis_size("kern")
    groups = lax.axis_size("dp")
    me = lax.axis_index("kern").astype(jnp.int32)
    my_group = lax.axis_index("dp").astype(jnp.int32)
    words = jnp.stack([me, my_group % 2, my_group // 2 % 2, my_group // 4])
    local_taps = raw_taps.shape[0]
    total_taps = local_taps * kern
    chan = feat // kern
    outer = row_count * kern // inner
    share = local_taps // groups
    deep = feat // groups
    in_rows = 2 * deep
    tabs = all_tables(outer)
    seqs = range(seq_count)

    def across(pieces, sign, *anchors):
        if anchors:
            pieces = after(anchors, pieces)
        if len(pieces) == 1:
            return [spread_out(pieces[0], "kern")]
        return exchange(pieces, sign)

    def copies(block):
        return jnp.broadcast_to(block[None], (groups, *block.shape))

    def to_all(block):
        return spread_out(copies(block), "dp")

    my_taps = lax.dynamic_slice_in_dim(raw_taps, my_group * share, share, 0)
    my_taps = shrink(my_taps).astype(bf16).reshape(share, kern, chan).transpose(1, 0, 2)
    limits = total_taps - lax.dynamic_slice_in_dim(pad_lengths, me * chan, chan, 0)[None]

    my_taps = spread_out(my_taps, "kern")

    heads, arrived = [], []
    for b in seqs:
        head = project(words, b, tokens, first_gain, in_weight, kern, False)
        words = after(head[0], words)
        heads.append(head)
        if b == 0:
            all_taps = to_all(after(head[0], my_taps))
            arrived.append(across(head[2], -1))
        else:
            arrived.append(across(head[2], -1, *arrived, all_taps))

    hidden_back = grad_hidden(words, cotangent, down_weight)
    words = after(hidden_back, words)
    kernel_spec = tap_spectrum(words, all_taps, limits, tabs)
    words = after(kernel_spec, words)

    convs, returned = [], []
    for b in seqs:
        conv = convolve(words, arrived[b], kern, kernel_spec, tabs, False, None, True)
        words = after(conv[1], words)
        convs.append(conv)
        returned.append(across(conv[0], 1, arrived[-1], *returned))

    mids, arrived_back = [], []
    earlier, out_tokens = None, None
    for b in seqs:
        mid, grads, pieces = feed_forward(
            words,
            b,
            tokens,
            cotangent,
            hidden_back,
            heads[b][1],
            returned[b],
            heads[b][0],
            out_weight,
            up_weight,
            down_weight,
            second_gain,
            kern,
            groups,
            True,
            earlier,
            out_tokens,
        )
        words = after(mid[3], words)
        out_tokens, second_row = mid[0], mid[3]
        earlier = [*grads, second_row]
        mids.append(mid)
        arrived_back.append(across(pieces, -1, returned[-1], *arrived_back))
    u_keep, u_give, d_keep, d_give, out_t, gate_t = grads
    u_give, d_give = after(arrived_back[:-1], (u_give, d_give))
    wide_sums = Folding((u_keep, u_give), (d_keep, d_give))

    corrs, signal_back = [], []
    for b in seqs:
        corr = convolve(
            words, arrived_back[b], kern, kernel_spec, tabs, True, convs[b][1], b > 0
        )
        words = after(corr[1], words)
        corrs.append(corr)
        if b == 0:
            steps = wide_sums.step()
            words = after(steps, words)
            signal_back.append(across(corr[0], 1, steps))
        else:
            signal_back.append(across(corr[0], 1, *signal_back))

    def finish_one(b, words, earlier, grad_tokens, others):
        return finish(
            words,
            b,
            tokens,
            heads[b][0],
            mids[b][1],
            mids[b][2],
            signal_back[b],
            in_weight,
            first_gain,
            kern,
            groups,
            earlier,
            grad_tokens,
            others,
        )

    earlier, grad_tokens = None, None
    for b in seqs[:-1]:
        tail = finish_one(b, words, earlier, grad_tokens, None)
        grad_tokens = tail[0]
        earlier = [tail[2], tail[1]]
        words = after(tail[1], words)

    words = after(wide_sums.step(), words)

    def write(word_ref, taps_ref, out_refs):
        for to, side in ((0, word_ref[1]), (1, 1 - word_ref[1])):
            for pair in range(groups // 2):
                for z in range(kern):
                    start = (z * groups + 2 * pair + side) * share
                    block = taps_ref[pl.ds(pl.multiple_of(start, share), share), :]
                    at = pair ^ own_pair(word_ref)
                    for h in range(2):
                        place = (flipped(at) if h == 0 else at, flipped(z ^ word_ref[0]))
                        half = block[h * share // 2 : (h + 1) * share // 2]
                        late_pack(out_refs[2 * h + to], place, half)

    shapes = [(groups // 2, kern, share // 4 * 3, 128)] * 4
    products = [corr[1] for corr in corrs]
    grad_taps = tap_gradient(words, products, limits, tabs, shapes, write)
    words = after((grad_taps, wide_sums.got), words)

    others = [gate_t, out_t, second_row, *grad_taps]
    tail = finish_one(seqs[-1], words, earlier, grad_tokens, others)
    grad_tokens = tail[0]

    late_sums = Folding(tail[1:3], tail[3:5])
    wide_sums.hold(grad_tokens)
    wide_sums.step()
    steps = late_sums.step()
    wide_sums.hold(steps)
    wide_sums.step()
    late_sums.step()
    taps = jnp.stack(late_sums.take(late_packed), axis=1)
    steps = late_sums.step()
    taps = [taps[flipped(r)] for r in range(kern)]
    for r in range(1, kern):
        taps[r] = lax.ppermute(taps[r], "kern", [(i, i ^ r) for i in range(kern)])
    taps = late_unpack(jnp.stack(taps)).reshape(kern, share, chan)
    taps = jnp.concatenate(
        [lax.dynamic_index_in_dim(taps, me ^ z, 0, keepdims=False) for z in range(kern)], axis=1
    )
    taps = copies(taps)
    late_sums.hold(taps)
    steps = late_sums.step()
    wide_sums.hold(steps)
    up, down = wide_sums.totals()
    grad_taps = spread_out(taps, "dp").reshape(local_taps, feat)
    grad_raw = grad_taps.astype(f32) * shrink_slope(raw_taps)

    sum_up = jnp.concatenate(jnp.split(up, 2, axis=1), axis=0)
    sum_down = down.T
    late = jnp.concatenate([late_unpack(block) for block in late_sums.totals()], axis=0)
    sum_in = late[:in_rows].T
    sum_out = late[in_rows : in_rows + deep].T
    first_row = late[in_rows + deep : in_rows + deep + 1]
    second_row = late[in_rows + deep + 1 : in_rows + deep + 2]

    return (
        out_tokens,
        grad_tokens,
        sum_in,
        sum_out,
        sum_up,
        sum_down,
        first_row[0],
        second_row[0],
        grad_raw,
    )


def solution(mesh):
    placed = (
        P("dp", "kern", None),
        P("dp", "kern", None),
        P(),
        P(),
        P(),
        P(),
        P(),
        P(),
        P("kern", None),
        P(),
    )
    placed_out = (
        P("dp", "kern", None),
        P("dp", "kern", None),
        P("kern", "dp"),
        P("kern", "dp"),
        P("kern", "dp"),
        P("kern", "dp"),
        P("kern"),
        P("kern"),
        P("kern", None),
    )
    groups, kern = mesh.shape["dp"], mesh.shape["kern"]

    def layer(*arrays):
        seq_count, length, feat = arrays[0].shape
        width = arrays[4].shape[1]
        rows = length // kern
        tiles = (
            feat % (16 * groups) == 0
            and width % (128 * groups) == 0
            and width == groups // 2 * feat
            and groups == 8
            and kern == 4
            and rows % (2 * inner) == 0
            and 3 * feat // groups + 2 <= 2 * late_rows
            and feat // kern == 192
            and arrays[8].shape[0] == 64 * groups * kern
        )
        return run(shards if tiles else shards_general)(*arrays)

    def run(body):
        return jax.shard_map(
            body,
            mesh=mesh,
            in_specs=placed,
            out_specs=placed_out,
            check_vma=False,
        )

    return layer
```

```python
import math

import jax
import jax.numpy as jnp
import ml_dtypes
import numpy as np
from jax import lax
from jax.experimental import pallas as pl
from jax.experimental.pallas import tpu as pltpu
from jax.sharding import PartitionSpec as P

shrink_level = 0.003
norm_eps = 1e-05
bf16 = jnp.bfloat16
f32 = jnp.float32
inner = 128
group = 16
wide = 8


def inner_tables(outer):
    length = outer * inner
    k1 = np.arange(outer)[:, None, None]
    k2 = np.arange(inner)[None, :, None]
    n2 = np.arange(inner)[None, None, :]
    turns = (n2 * (4 * (outer * k2 + k1) + 1)) % (4 * length)
    angle = turns * (2 * math.pi / (4 * length))
    c, s = np.cos(angle), np.sin(angle)
    table = np.concatenate([np.concatenate([c, s], 2), np.concatenate([-s, c], 2)], 1)
    return table.astype(ml_dtypes.bfloat16)


def outer_tables(outer):
    k1 = np.arange(outer)[:, None]
    n1 = np.arange(outer)[None, :]
    angle = (n1 * (4 * k1 + 1)) % (4 * outer) * (2 * math.pi / (4 * outer))
    parts = np.stack([np.cos(angle), -np.sin(angle)], 1)
    table = np.einsum("kcn,ij->kcinj", parts, np.eye(group))
    table = table.reshape(outer * 2 * group, outer * group)
    return table.astype(ml_dtypes.bfloat16), table.T.astype(ml_dtypes.bfloat16)


def all_tables(outer):
    first, last = outer_tables(outer)
    tabs = {"inner": inner_tables(outer), "first": first, "last": last}
    return {key: jnp.asarray(value) for key, value in tabs.items()}


def outer_forward(x_ref, table_ref, y_ref):
    outer, _, ch = x_ref.shape

    def step(j, carry):
        rows = pl.ds(pl.multiple_of(j * group, group), group)
        x = x_ref[:, rows, :].reshape(outer * group, ch)
        y = jnp.dot(table_ref[...], x, preferred_element_type=f32).astype(bf16)
        y = y.reshape(outer, 2, group, ch)
        y_ref[:, 0, rows, :] = y[:, 0]
        y_ref[:, 1, rows, :] = y[:, 1]
        return carry

    lax.fori_loop(0, inner // group, step, 0, unroll=8)


def outer_back(w_ref, table_ref, x_ref):
    outer, _, _, ch = w_ref.shape

    def step(j, carry):
        rows = pl.ds(pl.multiple_of(j * group, group), group)
        w = w_ref[:, :, rows, :].reshape(outer * 2 * group, ch)
        x = jnp.dot(table_ref[...], w, preferred_element_type=f32)
        x_ref[:, rows, :] = x.astype(x_ref.dtype).reshape(outer, group, ch)
        return carry

    lax.fori_loop(0, inner // group, step, 0, unroll=8)


def whole(shape):
    return pl.BlockSpec(shape, lambda i: (0,) * len(shape))


def slab(*shape):
    return pl.BlockSpec((wide,) + shape, lambda i: (i,) + (0,) * len(shape))


def smem():
    return pl.BlockSpec(memory_space=pltpu.SMEM)


def params(mib):
    return pltpu.CompilerParams(
        vmem_limit_bytes=mib * 2**20, dimension_semantics=("arbitrary",)
    )


def cost(micros):
    return pl.CostEstimate(
        flops=int(micros * 8e8), bytes_accessed=int(micros * 1e6), transcendentals=0
    )


def tap_spectrum(words, taps, limits, tabs):
    groups, kern, share, ch = taps.shape
    length = groups * kern * share
    outer = length // inner

    def kernel(_, taps_ref, limit_ref, table_ref, first_ref, out_ref, x_ref, y_ref, flat_ref):
        @pl.when(pl.program_id(0) == 0)
        def _():
            for z in range(kern):
                for p in range(groups):
                    at = (z * groups + p) * share
                    flat_ref[at : at + share] = taps_ref[p, z].astype(f32)
            values = flat_ref[...]
            edge = jnp.zeros((1, ch), f32)
            below = jnp.concatenate([edge, values[:-1]], 0)
            above = jnp.concatenate([values[1:], edge], 0)
            index = lax.broadcasted_iota(jnp.int32, (length, ch), 0)
            values = jnp.where(index < limit_ref[...], (below + values + above) / 3.0, 0.0)
            x_ref[...] = values.astype(bf16).reshape(outer, inner, ch)
            outer_forward(x_ref, first_ref, y_ref)

        for i in range(wide):
            y = y_ref[pl.program_id(0) * wide + i].reshape(2 * inner, ch)
            s = jnp.dot(table_ref[i], y, preferred_element_type=f32)
            out_ref[i] = (s * (1.0 / length)).astype(bf16)

    return pl.pallas_call(
        kernel,
        grid=(outer // wide,),
        in_specs=[
            smem(),
            whole(taps.shape),
            whole((1, ch)),
            slab(2 * inner, 2 * inner),
            whole(tabs["first"].shape),
        ],
        out_specs=slab(2 * inner, ch),
        out_shape=jax.ShapeDtypeStruct((outer, 2 * inner, ch), bf16),
        scratch_shapes=[
            pltpu.VMEM((outer, inner, ch), bf16),
            pltpu.VMEM((outer, 2, inner, ch), bf16),
            pltpu.VMEM((length, ch), f32),
        ],
        compiler_params=params(56),
        cost_estimate=cost(6),
        name="tap_spectrum",
    )(words, taps, limits, tabs["inner"], tabs["first"])


def packed(rows, ch):
    if ch % 128 == 64 and rows % (2 * inner) == 0:
        return (rows // inner * (2 * ch // 128) // 2, inner, 128)
    return (rows // inner, inner, ch)


def pack(ref, lead, values, part, parts):
    rows, ch = values.shape
    blocks = rows // inner
    if ref.shape[-1] == ch:
        ref[(*lead, pl.ds(part * blocks, blocks))] = values.reshape(blocks, inner, ch)
        return
    full = ch // 128
    for j in range(full):
        at = (j * parts + part) * blocks
        lanes = values[:, j * 128 : (j + 1) * 128]
        ref[(*lead, pl.ds(at, blocks))] = lanes.reshape(blocks, inner, 128)
    rest = values[:, full * 128 :]
    half = parts * blocks // 2
    for t in range(blocks):
        at = part * blocks + t
        side, row = at // half, at % half
        ref[(*lead, full * parts * blocks + row, slice(None), slice(side * 64, side * 64 + 64))] = (
            rest[t * inner : (t + 1) * inner]
        )


def unpack(ref, lead, part, parts, ch, blocks):
    if ref.shape[-1] == ch:
        return [(0, ref[(*lead, pl.ds(part * blocks, blocks))])]
    full = ch // 128
    out = []
    for j in range(full):
        at = (j * parts + part) * blocks
        out.append((j * 128, ref[(*lead, pl.ds(at, blocks))]))
    half = parts * blocks // 2
    rest = []
    for t in range(blocks):
        at = part * blocks + t
        side, row = at // half, at % half
        rest.append(
            ref[(*lead, full * parts * blocks + row, slice(None), slice(side * 64, side * 64 + 64))]
        )
    out.append((full * 128, jnp.stack(rest)))
    return out


def owners(me_ref, refs, kern, sign):
    if len(refs) == 1 and kern > 1:
        return [(refs[0], (k,), k) for k in range(kern)]
    return [
        (ref, (), lax.rem(me_ref[0] + (k if sign > 0 else kern - k), kern))
        for k, ref in enumerate(refs)
    ]


def piece_shapes(kern, rows, ch, stacked):
    shape = packed(rows, ch)
    return [(kern, *shape)] if stacked else [shape] * kern


def place_pieces(me_ref, piece_refs, x_ref, kern):
    outer, _, ch = x_ref.shape
    blocks = outer // kern
    for ref, lead, owner in owners(me_ref, piece_refs, kern, 1):
        for at, block in unpack(ref, lead, 0, 1, ch, blocks):
            x_ref[pl.ds(owner * blocks, blocks), :, at : at + block.shape[2]] = block


def take_pieces(me_ref, x_ref, piece_refs, kern):
    outer, _, ch = x_ref.shape
    blocks = outer // kern
    for ref, lead, owner in owners(me_ref, piece_refs, kern, 1):
        pack(ref, lead, x_ref[pl.ds(owner * blocks, blocks)].reshape(blocks * inner, ch), 0, 1)


def convolve(me, pieces, kern, kernel_spec, tabs, flip, other_spec=None, stacked=False):
    count = len(pieces)
    outer, _, ch = kernel_spec.shape
    shapes = piece_shapes(kern, outer * inner // kern, ch, stacked)

    def kernel(me_ref, *refs):
        piece_refs, refs = refs[:count], refs[count:]
        spec_ref, table_ref, first_ref, last_ref = refs[:4]
        refs = refs[4:]
        if flip:
            other_ref, refs = refs[0], refs[1:]
        out_refs, refs = refs[: len(shapes)], refs[len(shapes) :]
        save_ref, x_ref, y_ref, w_ref = refs
        step = pl.program_id(0)

        @pl.when(step == 0)
        def _():
            place_pieces(me_ref, piece_refs, x_ref, kern)
            outer_forward(x_ref, first_ref, y_ref)

        for i in range(wide):
            at = step * wide + i
            y = y_ref[at].reshape(2 * inner, ch)
            s = jnp.dot(table_ref[i], y, preferred_element_type=f32)
            sr, si = s[:inner], s[inner:]
            kr = spec_ref[i, :inner].astype(f32)
            ki = spec_ref[i, inner:].astype(f32)
            if flip:
                orr = other_ref[i, :inner].astype(f32)
                oi = other_ref[i, inner:].astype(f32)
                save_ref[i, :inner] = (sr * orr + si * oi).astype(bf16)
                save_ref[i, inner:] = (si * orr - sr * oi).astype(bf16)
                zr, zi = sr * kr + si * ki, si * kr - sr * ki
            else:
                save_ref[i] = s.astype(bf16)
                zr, zi = sr * kr - si * ki, sr * ki + si * kr
            z = jnp.concatenate([zr, zi], 0).astype(bf16)
            w = mm_tn(table_ref[i], z)
            w_ref[at] = w.astype(bf16).reshape(2, inner, ch)

        @pl.when(step == pl.num_programs(0) - 1)
        def _():
            outer_back(w_ref, last_ref, x_ref)
            take_pieces(me_ref, x_ref, out_refs, kern)

    args = [me, *pieces, kernel_spec, tabs["inner"], tabs["first"], tabs["last"]]
    in_specs = [smem()] + [whole(piece.shape) for piece in pieces] + [
        slab(2 * inner, ch),
        slab(2 * inner, 2 * inner),
        whole(tabs["first"].shape),
        whole(tabs["last"].shape),
    ]
    if flip:
        args.append(other_spec)
        in_specs.append(slab(2 * inner, ch))
    outs = pl.pallas_call(
        kernel,
        grid=(outer // wide,),
        in_specs=in_specs,
        out_specs=[whole(shape) for shape in shapes] + [slab(2 * inner, ch)],
        out_shape=[jax.ShapeDtypeStruct(shape, bf16) for shape in shapes]
        + [jax.ShapeDtypeStruct((outer, 2 * inner, ch), bf16)],
        scratch_shapes=[
            pltpu.VMEM((outer, inner, ch), bf16),
            pltpu.VMEM((outer, 2, inner, ch), bf16),
            pltpu.VMEM((outer, 2, inner, ch), bf16),
        ],
        compiler_params=params(56),
        cost_estimate=cost(8),
        name="correlate" if flip else "convolve",
    )(*args)
    return list(outs[:-1]), outs[-1]


def tap_gradient(words, products, limits, tabs, out_shapes, write):
    outer, _, ch = products[0].shape
    length = outer * inner

    def kernel(word_ref, limit_ref, *refs):
        spec_refs, refs = refs[: len(products)], refs[len(products) :]
        table_ref, last_ref, refs = refs[0], refs[1], refs[2:]
        out_refs, (w_ref, x_ref, t_ref) = refs[: len(out_shapes)], refs[len(out_shapes) :]
        step = pl.program_id(0)
        for i in range(wide):
            z = spec_refs[0][i].astype(f32)
            for spec_ref in spec_refs[1:]:
                z = z + spec_ref[i].astype(f32)
            w = mm_tn(table_ref[i], (z * (1.0 / length)).astype(bf16))
            w_ref[step * wide + i] = w.astype(bf16).reshape(2, inner, ch)

        @pl.when(step == pl.num_programs(0) - 1)
        def _():
            outer_back(w_ref, last_ref, x_ref)
            taps = x_ref[...].reshape(length, ch)
            index = lax.broadcasted_iota(jnp.int32, (length, ch), 0)
            taps = jnp.where(index < limit_ref[...], taps, 0.0)
            edge = jnp.zeros((1, ch), f32)
            below = jnp.concatenate([edge, taps[:-1]], 0)
            above = jnp.concatenate([taps[1:], edge], 0)
            t_ref[...] = ((below + taps + above) / 3.0).astype(bf16)
            write(word_ref, t_ref, out_refs)

    return pl.pallas_call(
        kernel,
        grid=(outer // wide,),
        in_specs=[smem(), whole((1, ch))]
        + [slab(2 * inner, ch)] * len(products)
        + [slab(2 * inner, 2 * inner), whole(tabs["last"].shape)],
        out_specs=[whole(shape) for shape in out_shapes],
        out_shape=[jax.ShapeDtypeStruct(shape, bf16) for shape in out_shapes],
        scratch_shapes=[
            pltpu.VMEM((outer, 2, inner, ch), bf16),
            pltpu.VMEM((outer, inner, ch), f32),
            pltpu.VMEM((length, ch), bf16),
        ],
        compiler_params=params(56),
        cost_estimate=cost(5),
        name="tap_gradient",
    )(words, limits, *products, tabs["inner"], tabs["last"])


def exchange(pieces, sign):
    count = len(pieces)
    moved = [pieces[0]]
    for k in range(1, count):
        route = [(i, (i + sign * k) % count) for i in range(count)]
        moved.append(lax.ppermute(pieces[k], "kern", route))
    return moved


def spread_out(block, axis_name, groups=None):
    return lax.all_to_all(
        block, axis_name, split_axis=0, concat_axis=0, tiled=True, axis_index_groups=groups
    )


def sum_all(row):
    for axis_name in ("dp", "kern"):
        count = lax.axis_size(axis_name)
        for bit in range(count.bit_length() - 1):
            route = [(i, i ^ (1 << bit)) for i in range(count)]
            row = row + lax.ppermute(row, axis_name, route)
    return row


def padded_rows(block):
    count = lax.axis_size("kern")
    forward = [(i, i + 1) for i in range(count - 1)]
    backward = [(target, source) for source, target in forward]
    low = lax.ppermute(block[-1:], "kern", forward)
    high = lax.ppermute(block[:1], "kern", backward)
    return jnp.concatenate([low, block, high], axis=0)


def layer_norm(values, norm_gain):
    center = values - jnp.mean(values, axis=-1, keepdims=True)
    spread = jnp.mean(center * center, axis=-1, keepdims=True)
    return center * lax.rsqrt(spread + norm_eps) * norm_gain


def shrink(tap_values):
    return tap_values - shrink_level * tap_values / jnp.sqrt(
        tap_values * tap_values + shrink_level * shrink_level
    )


def shrink_slope(tap_values):
    return 1.0 - shrink_level**3 / (tap_values * tap_values + shrink_level * shrink_level) ** 1.5


def pool_three(padded):
    return (padded[:-2] + padded[1:-1] + padded[2:]) / 3.0


def dot(left, right, dims):
    return lax.dot_general(left, right, (dims, ((), ())), preferred_element_type=f32)


def shards_general(
    tokens,
    cotangent,
    in_weight,
    out_weight,
    up_weight,
    down_weight,
    first_gain,
    second_gain,
    raw_taps,
    pad_lengths,
):
    seq_count, row_count, feat = tokens.shape
    kern = lax.axis_size("kern")
    me = lax.axis_index("kern")
    me_word = me.astype(jnp.int32).reshape(1)
    groups = lax.axis_size("dp")
    local_taps = raw_taps.shape[0]
    total_taps = local_taps * kern
    chan = feat // kern
    outer = row_count * kern // inner
    blocks = row_count // inner
    tabs = all_tables(outer)

    limits = total_taps - lax.dynamic_slice_in_dim(pad_lengths, me * chan, chan, 0)[None]
    my_raw = lax.all_to_all(raw_taps, "kern", split_axis=1, concat_axis=0, tiled=True)
    kernel_spec = tap_spectrum(me_word, shrink(my_raw)[None, None], limits, tabs)

    def apart(values):
        values = values.reshape(blocks, inner, kern, chan).transpose(2, 0, 1, 3)
        return [values[(me - k) % kern] for k in range(kern)]

    def joined(pieces):
        stack = jnp.stack(pieces)
        stack = jnp.stack([stack[(me - k) % kern] for k in range(kern)])
        return stack.transpose(1, 2, 0, 3).reshape(row_count, feat)

    def one(x, cot):
        inputs = x.astype(f32)
        first_norm, first_pull = jax.vjp(layer_norm, inputs, first_gain)
        normed = first_norm.astype(bf16)
        projected = dot(normed, in_weight, ((1,), (0,)))
        gate = projected[:, feat:]
        pieces = exchange(apart(projected[:, :feat].astype(bf16)), -1)
        pieces, spectrum = convolve(me_word, pieces, kern, kernel_spec, tabs, False)
        convolved = joined(exchange(pieces, 1)).astype(f32)
        mixed = (gate * convolved).astype(bf16)
        middle = inputs + dot(mixed, out_weight, ((1,), (0,)))
        second_norm, second_pull = jax.vjp(layer_norm, middle, second_gain)
        normed_two = second_norm.astype(bf16)
        raised = dot(normed_two, up_weight, ((1,), (0,)))
        activated, gelu_pull = jax.vjp(jax.nn.gelu, raised)
        hidden = activated.astype(bf16)
        out = (middle + dot(hidden, down_weight, ((1,), (0,)))).astype(bf16)
        grad_raised = gelu_pull(dot(cot, down_weight, ((1,), (1,))))[0].astype(bf16)
        grad_mid, second_row = second_pull(dot(grad_raised, up_weight, ((1,), (1,))))
        grad_mid = cot.astype(f32) + grad_mid
        branch = grad_mid.astype(bf16)
        grad_mixed = dot(branch, out_weight, ((1,), (1,)))
        grad_gate = (grad_mixed * convolved).astype(bf16)
        pieces = exchange(apart((grad_mixed * gate).astype(bf16)), -1)
        pieces, product = convolve(me_word, pieces, kern, kernel_spec, tabs, True, spectrum)
        grad_signal = joined(exchange(pieces, 1))
        grad_projected = jnp.concatenate([grad_signal, grad_gate], axis=-1)
        grad_first, first_row = first_pull(dot(grad_projected, in_weight, ((1,), (1,))))
        weights = (
            dot(normed, grad_projected, ((0,), (0,))),
            dot(mixed, branch, ((0,), (0,))),
            dot(normed_two, grad_raised, ((0,), (0,))),
            dot(hidden, cot, ((0,), (0,))),
        )
        return out, (grad_mid + grad_first).astype(bf16), product, (first_row, second_row), weights

    ones = [one(tokens[b], cotangent[b]) for b in range(seq_count)]
    rows, weights = ones[0][3:]
    for other in ones[1:]:
        rows, weights = jax.tree.map(jnp.add, (rows, weights), other[3:])
    def write(_, taps_ref, out_refs):
        out_refs[0][...] = taps_ref[...]

    products = [item[2] for item in ones]
    shapes = [(total_taps, chan)]
    grad_taps = tap_gradient(me_word, products, limits, tabs, shapes, write)[0]
    grad_taps = lax.all_to_all(grad_taps, "kern", split_axis=0, concat_axis=1, tiled=True)
    grad_raw = lax.psum(grad_taps, "dp").astype(f32) * shrink_slope(raw_taps)
    sums = []
    for weight in weights:
        weight = lax.psum_scatter(weight.astype(bf16), "dp", scatter_dimension=1, tiled=True)
        weight = lax.psum_scatter(weight, "kern", scatter_dimension=0, tiled=True)
        sums.append(weight.astype(f32))
    gains = sum_all(jnp.stack(rows))
    gains = lax.dynamic_slice_in_dim(gains, me * chan, chan, 1)
    return (
        jnp.stack([item[0] for item in ones]),
        jnp.stack([item[1] for item in ones]),
        *sums,
        gains[0],
        gains[1],
        grad_raw,
    )


def row_mean(values):
    return jnp.mean(values, axis=-1, keepdims=True)


def centered(values):
    center = values - row_mean(values)
    inverse = lax.rsqrt(row_mean(center * center) + norm_eps)
    return center * inverse, inverse


def norm_back(grad, normed, inverse, gain):
    scaled = grad * gain
    return inverse * (scaled - row_mean(scaled) - normed * row_mean(scaled * normed))


def mm(left, right):
    return jnp.dot(left, right, preferred_element_type=f32)


def mm_nt(left, right):
    return lax.dot_general(left, right, (((1,), (1,)), ((), ())), preferred_element_type=f32)


def mm_tn(left, right):
    return lax.dot_general(left, right, (((0,), (0,)), ((), ())), preferred_element_type=f32)


def fixed(shape):
    return pl.BlockSpec(shape, lambda *_: (0,) * len(shape))


def once(shape):
    return pl.BlockSpec(
        shape, lambda *_: (0,) * len(shape), pipeline_mode=pl.Buffered(1)
    )


def along(seq, rows, feat):
    return pl.BlockSpec((1, rows, feat), lambda i: (seq, i, 0))


def cut(me_ref, values, piece_refs, stack_ref, part=0, parts=1):
    kern, rows, ch = stack_ref.shape
    if len(piece_refs) > 1:
        for k in range(kern):
            stack_ref[k] = values[:, k * ch : (k + 1) * ch]
    for ref, lead, owner in owners(me_ref, piece_refs, kern, -1):
        block = stack_ref[owner] if len(piece_refs) > 1 else values[:, owner * ch : (owner + 1) * ch]
        pack(ref, lead, block, part, parts)


def join(me_ref, piece_refs, stack_ref, out_ref, part=0, parts=1):
    kern, rows, ch = stack_ref.shape
    blocks = rows // inner
    for ref, lead, owner in owners(me_ref, piece_refs, kern, -1):
        for at, block in unpack(ref, lead, part, parts, ch, blocks):
            width = block.shape[2]
            block = block.reshape(rows, width)
            if len(piece_refs) > 1:
                stack_ref[owner, :, at : at + width] = block
            else:
                out_ref[:, owner * ch + at : owner * ch + at + width] = block
    if len(piece_refs) > 1:
        for k in range(kern):
            out_ref[:, k * ch : (k + 1) * ch] = stack_ref[k]


def project(me, seq, tokens, gain, weight, kern, stacked, turn=False):
    _, rows, feat = tokens.shape
    chan = feat // kern
    tile = rows // 2
    shapes = piece_shapes(kern, rows, chan, stacked)
    turned_shape = [weight.shape[::-1]] if turn else []

    def kernel(me_ref, x_ref, gain_ref, weight_ref, *refs):
        normed_ref, gate_ref = refs[:2]
        piece_refs, stack_ref = refs[2 : 2 + len(shapes)], refs[-1]
        if turn:
            pl.when(pl.program_id(0) == 0)(lambda: put_turned(weight_ref, refs[-2]))
        hat, _ = centered(x_ref[0].astype(f32))
        normed = (hat * gain_ref[...]).astype(bf16)
        normed_ref[...] = normed
        projected = mm(normed, weight_ref[...])
        gate_ref[...] = projected[:, feat:]
        signal = projected[:, :feat].astype(bf16)
        for part in range(2):
            pl.when(pl.program_id(0) == part)(
                lambda: cut(me_ref, signal, piece_refs, stack_ref, part, 2)
            )

    outs = pl.pallas_call(
        kernel,
        grid=(2,),
        in_specs=[smem(), along(seq, tile, feat), fixed((feat,)), fixed(weight.shape)],
        out_specs=[
            pl.BlockSpec((tile, feat), lambda i: (i, 0)),
            pl.BlockSpec((tile, feat), lambda i: (i, 0)),
        ]
        + [fixed(shape) for shape in shapes + turned_shape],
        out_shape=[
            jax.ShapeDtypeStruct((rows, feat), bf16),
            jax.ShapeDtypeStruct((rows, feat), f32),
        ]
        + [jax.ShapeDtypeStruct(shape, bf16) for shape in shapes + turned_shape],
        scratch_shapes=[pltpu.VMEM((kern, tile, chan), bf16)],
        compiler_params=params(56),
        cost_estimate=cost(4),
        name="project",
    )(me, tokens, gain, weight)
    return outs[0], outs[1], list(outs[2 : 2 + len(shapes)]), outs[-1]


def put_turned(from_ref, to_ref):
    to_ref[...] = from_ref[...].T


def gelu_pair(raised):
    root = math.sqrt(2.0 / math.pi)
    square = raised * raised
    t = jnp.tanh(raised * (root + (root * 0.044715) * square))
    half = 0.5 + 0.5 * t
    slope = half + (0.5 * raised) * (1.0 - t * t) * (root + (3.0 * root * 0.044715) * square)
    return raised * half, slope


def own_pair(words):
    return 2 * words[3] + words[2]


def grad_hidden(words, cots, down_weight):
    seqs, rows, feat = cots.shape
    width = down_weight.shape[0]
    chunk = feat

    def kernel(_, cot_ref, down_ref, out_ref):
        out = mm_nt(cot_ref[...].reshape(seqs * rows, feat), down_ref[...])
        out_ref[...] = out.astype(bf16).reshape(seqs, rows, chunk)

    return pl.pallas_call(
        kernel,
        grid=(width // chunk,),
        in_specs=[smem(), fixed(cots.shape), pl.BlockSpec((chunk, feat), lambda i: (i, 0))],
        out_specs=pl.BlockSpec((seqs, rows, chunk), lambda i: (0, 0, i)),
        out_shape=jax.ShapeDtypeStruct((seqs, rows, width), bf16),
        compiler_params=params(56),
        cost_estimate=cost(6),
        name="grad_hidden",
    )(words, cots, down_weight)


def flipped(place):
    return 2 * (place & 1) + (place >> 1)


def feed_forward(words, seq, tokens, cots, grads, gate, conv, normed, out_weight, up_weight, down_weight, gain, kern, groups, stacked, earlier, out_before):
    seqs, rows, feat = tokens.shape
    width = up_weight.shape[1]
    count = len(conv)
    shapes = piece_shapes(kern, rows, feat // kern, stacked)
    chan = feat // kern
    pairs = groups // 2
    chunk = width // pairs
    deep = feat // groups
    half = chunk // 2
    add = earlier is not None

    def kernel(word_ref, x_ref, cot_ref, gh_ref, gate_ref, normed_ref, ow_ref, up_ref, down_ref, gain_ref, *refs):
        conv_refs, refs = refs[:count], refs[count:]
        if add:
            old, refs = refs[:7], refs[8:]
        out_ref, mid_ref, ggate_ref, ggain_ref = refs[:4]
        u_keep, u_give, d_keep, d_give, o_ref, g_ref = refs[4:10]
        piece_refs, refs = refs[10 : 10 + len(shapes)], refs[10 + len(shapes) :]
        stack_s, cv, mixed_s, middle_s, n2_s, acc_s, back_s = refs
        f = pl.program_id(0)
        cot = cot_ref.at[0]

        @pl.when(f == 0)
        def _():
            join(word_ref, conv_refs, stack_s, cv)
            mixed = (gate_ref[...] * cv[...].astype(f32)).astype(bf16)
            mixed_s[...] = mixed
            middle = x_ref[0].astype(f32) + mm(mixed, ow_ref[...])
            middle_s[...] = middle
            hat, _ = centered(middle)
            n2_s[...] = (hat * gain_ref[...]).astype(bf16)
            acc_s[...] = middle
            back_s[...] = jnp.zeros_like(back_s)

        hidden, grad_raised = [], []
        for at in range(0, rows, rows // 2):
            part = slice(at, at + rows // 2)
            act, slope = gelu_pair(mm(n2_s[part], up_ref[...]))
            hidden.append(act.astype(bf16))
            grad_raised.append((gh_ref[0, part].astype(f32) * slope).astype(bf16))
        hidden = jnp.concatenate(hidden, 0)
        grad_raised = jnp.concatenate(grad_raised, 0)
        acc_s[...] += mm(hidden, down_ref[...])
        back_s[...] += mm_nt(grad_raised, up_ref[...])
        u = mm_tn(n2_s[...], grad_raised).astype(bf16)
        d = mm_tn(cot[...], hidden).astype(bf16).reshape(pairs, 2, deep, chunk)
        even = word_ref[1] == 0
        for to, u_ref, d_ref, u_old, d_old in (
            (0, u_keep, d_keep, 0, 2),
            (1, u_give, d_give, 1, 3),
        ):
            for pair in range(pairs):
                at = pair ^ own_pair(word_ref)
                part = jnp.where(even, d[pair, to], d[pair, 1 - to])
                d_ref[at, 0] = part + old[d_old][at, 0] if add else part
            uu = jnp.where(
                even,
                u[:, to * half : (to + 1) * half],
                u[:, (1 - to) * half : (2 - to) * half],
            ).reshape(kern, 2, deep, half)
            for z in range(kern):
                at = flipped(z ^ word_ref[0])
                part = jnp.concatenate([uu[z, 0], uu[z, 1]], axis=1)
                u_ref[0, at] = part + old[u_old][0, at] if add else part

        @pl.when(f == pairs - 1)
        def _():
            out_ref[0] = acc_s[...].astype(bf16)
            hat, inverse = centered(middle_s[...])
            back = back_s[...]
            ggain = jnp.sum(back * hat, axis=0, keepdims=True)
            grad_mid = cot[...].astype(f32) + norm_back(back, hat, inverse, gain_ref[...])
            mid_ref[...] = grad_mid
            branch = grad_mid.astype(bf16)
            grad_mixed = mm_nt(branch, ow_ref[...])
            ggate = (grad_mixed * cv[...].astype(f32)).astype(bf16)
            ggate_ref[...] = ggate
            cut(word_ref, (grad_mixed * gate_ref[...]).astype(bf16), piece_refs, stack_s)
            o = mm_tn(branch, mixed_s[...])
            g = mm_tn(ggate, normed_ref[...])
            if add:
                ggain = ggain + old[6][...]
                o = o + old[4][...].astype(f32)
                g = g + old[5][...].astype(f32)
            ggain_ref[...] = ggain
            o_ref[...] = o.astype(bf16)
            g_ref[...] = g.astype(bf16)

    u_spec = pl.BlockSpec((1, kern, deep, chunk), lambda f, w: (flipped(f ^ own_pair(w)), 0, 0, 0))
    d_spec = pl.BlockSpec((pairs, 1, deep, chunk), lambda f, w: (0, flipped(f ^ w[0]), 0, 0))
    square = fixed((feat, feat))
    flat = fixed((rows, feat))
    one = pl.BlockSpec((1, rows, feat), lambda f, w: (seq, 0, 0))
    args = [words, tokens, cots, grads, gate, normed, out_weight, up_weight, down_weight, gain, *conv]
    in_specs = [
        one,
        one,
        pl.BlockSpec((1, rows, chunk), lambda f, w: (seq, 0, f)),
        once((rows, feat)),
        once((rows, feat)),
        once(out_weight.shape),
        pl.BlockSpec((feat, chunk), lambda f, w: (0, f)),
        pl.BlockSpec((chunk, feat), lambda f, w: (f, 0)),
        fixed((feat,)),
    ] + [fixed(piece.shape) for piece in conv]
    grad_specs = [u_spec, u_spec, d_spec, d_spec, square, square]
    aliases = {}
    if add:
        args += [*earlier, out_before]
        in_specs += [*grad_specs, fixed((1, feat)), pl.BlockSpec(memory_space=pl.ANY)]
        aliases = {len(args) - 1: 0}
    big = jax.ShapeDtypeStruct((pairs, kern, deep, chunk), bf16)
    outs = pl.pallas_call(
        kernel,
        grid_spec=pltpu.PrefetchScalarGridSpec(
            num_scalar_prefetch=1,
            grid=(pairs,),
            in_specs=in_specs,
            out_specs=[one, flat, flat, fixed((1, feat)), *grad_specs]
            + [fixed(shape) for shape in shapes],
            scratch_shapes=[
                pltpu.VMEM((kern, rows, feat // kern), bf16),
                pltpu.VMEM((rows, feat), bf16),
                pltpu.VMEM((rows, feat), bf16),
                pltpu.VMEM((rows, feat), f32),
                pltpu.VMEM((rows, feat), bf16),
                pltpu.VMEM((rows, feat), f32),
                pltpu.VMEM((rows, feat), f32),
            ],
        ),
        out_shape=[
            jax.ShapeDtypeStruct(tokens.shape, bf16),
            jax.ShapeDtypeStruct((rows, feat), f32),
            jax.ShapeDtypeStruct((rows, feat), bf16),
            jax.ShapeDtypeStruct((1, feat), f32),
            big,
            big,
            big,
            big,
            jax.ShapeDtypeStruct((feat, feat), bf16),
            jax.ShapeDtypeStruct((feat, feat), bf16),
        ]
        + [jax.ShapeDtypeStruct(shape, bf16) for shape in shapes],
        input_output_aliases=aliases,
        compiler_params=params(56),
        cost_estimate=cost(24),
        name="feed_forward",
    )(*args)
    return outs[:4], list(outs[4:10]), list(outs[10:])


late_rows = 160
late_packed = 240


def finish(words, seq, tokens, grad_mid, grad_gate, signal, weight, gain, kern, out_before):
    seqs, rows, feat = tokens.shape
    count = len(signal)
    chan = feat // kern
    part = rows // 2
    add = out_before is not None

    def kernel(word_ref, x_ref, mid_ref, gate_ref, weight_ref, gain_ref, *refs):
        signal_refs, refs = refs[:count], refs[count:]
        out_ref, stack_s, gs = refs[1:] if add else refs
        i = pl.program_id(0)
        for p in range(2):
            pl.when(i == p)(lambda: join(word_ref, signal_refs, stack_s, gs, p, 2))
        back = mm_nt(gs[...], weight_ref[:, :feat]) + mm_nt(gate_ref[...], weight_ref[:, feat:])
        hat, inverse = centered(x_ref[0].astype(f32))
        grad = mid_ref[...] + norm_back(back, hat, inverse, gain_ref[...])
        out_ref[0] = grad.astype(bf16)

    tiled = pl.BlockSpec((part, feat), lambda i: (i, 0))
    args = [words, tokens, grad_mid, grad_gate, weight, gain, *signal]
    in_specs = [
        smem(),
        along(seq, part, feat),
        tiled,
        tiled,
        fixed(weight.shape),
        fixed((feat,)),
    ] + [fixed(piece.shape) for piece in signal]
    aliases = {}
    if add:
        args.append(out_before)
        in_specs.append(pl.BlockSpec(memory_space=pl.ANY))
        aliases = {len(args) - 1: 0}
    return pl.pallas_call(
        kernel,
        grid=(2,),
        in_specs=in_specs,
        out_specs=along(seq, part, feat),
        out_shape=jax.ShapeDtypeStruct(tokens.shape, bf16),
        scratch_shapes=[
            pltpu.VMEM((kern, part, chan), bf16),
            pltpu.VMEM((part, feat), bf16),
        ],
        input_output_aliases=aliases,
        compiler_params=params(56),
        cost_estimate=cost(6),
        name="finish",
    )(*args)


def late_gradients(words, signals, normeds, gate_t, out_t, weight_t, gain, second_row, taps, kern, groups):
    rows, feat = normeds[0].shape
    counts = [len(signal) for signal in signals]
    chan = feat // kern
    pairs = groups // 2
    in_rows, out_rows = 2 * feat // groups, feat // groups
    late = (pairs, kern, late_packed + taps[0].shape[2], 128)

    def kernel(word_ref, *refs):
        signal_refs = []
        for count in counts:
            signal_refs.append(refs[:count])
            refs = refs[count:]
        normed_refs, refs = refs[: len(normeds)], refs[len(normeds) :]
        gt_ref, ot_ref, wt_ref, gain_ref, row_ref = refs[:5]
        tap_refs, refs = refs[5:9], refs[9:]
        late_refs, (stack_s, gs, s_ref) = (refs[:2], refs[2:4]), refs[4:]
        for seq, piece_refs in enumerate(signal_refs):
            join(word_ref, piece_refs, stack_s, gs)
            s = mm_tn(gs[...], normed_refs[seq][...])
            s_ref[...] = s if seq == 0 else s_ref[...] + s
        first = jnp.sum(s_ref[...] * wt_ref[:feat].astype(f32), axis=0, keepdims=True)
        first += jnp.sum(
            gt_ref[...].astype(f32) * wt_ref[feat:].astype(f32), axis=0, keepdims=True
        )
        zero = jnp.zeros((2 * late_rows - in_rows - out_rows - 2, feat), f32)
        gains = jnp.concatenate([first / gain_ref[...], row_ref[...], zero], 0).astype(bf16)
        for h in range(2):
            for to in range(2):
                late_refs[h][to][:, :, late_packed:] = tap_refs[2 * h + to][...]
        for to, side in ((0, word_ref[1]), (1, 1 - word_ref[1])):
            for pair in range(pairs):
                from_ref = s_ref if pair < pairs // 2 else gt_ref
                at_in = (2 * (pair % (pairs // 2)) + side) * in_rows
                at_in = pl.multiple_of(at_in, in_rows)
                at_out = pl.multiple_of((2 * pair + side) * out_rows, out_rows)
                columns = from_ref[pl.ds(at_in, in_rows), :].astype(bf16)
                values = [
                    columns[:late_rows],
                    jnp.concatenate(
                        [columns[late_rows:], ot_ref[pl.ds(at_out, out_rows), :], gains], 0
                    ),
                ]
                at = pair ^ own_pair(word_ref)
                for h in range(2):
                    place = flipped(at) if h == 0 else at
                    for z in range(kern):
                        late_pack(
                            late_refs[h][to],
                            (place, flipped(z ^ word_ref[0])),
                            values[h][:, z * chan : (z + 1) * chan],
                        )

    args = [words]
    for signal in signals:
        args += signal
    args += [*normeds, gate_t, out_t, weight_t, gain, second_row, *taps]
    return pl.pallas_call(
        kernel,
        in_specs=[smem()] + [pl.BlockSpec(memory_space=pltpu.VMEM)] * (len(args) - 1),
        out_specs=[pl.BlockSpec(memory_space=pltpu.VMEM)] * 4,
        out_shape=[jax.ShapeDtypeStruct(late, bf16)] * 4,
        scratch_shapes=[
            pltpu.VMEM((kern, rows, chan), bf16),
            pltpu.VMEM((rows, feat), bf16),
            pltpu.VMEM((feat, feat), f32),
        ],
        compiler_params=pltpu.CompilerParams(vmem_limit_bytes=56 * 2**20),
        cost_estimate=cost(6),
        name="late_gradients",
    )(*args)


def late_pack(ref, lead, values):
    rows = values.shape[0]
    half = (rows // 2 + 15) // 16 * 16
    ref[(*lead, slice(0, rows))] = values[:, :128]
    ref[(*lead, slice(rows, rows + half), slice(0, 64))] = values[:half, 128:]
    ref[(*lead, slice(rows, 2 * rows - half), slice(64, 128))] = values[half:, 128:]


def late_unpack(block, rows):
    half = (rows // 2 + 15) // 16 * 16
    rest = block[..., rows : rows + half, :]
    rest = jnp.concatenate([rest[..., :64], rest[..., : rows - half, 64:]], axis=-2)
    return jnp.concatenate([block[..., :rows, :], rest], axis=-1)


def swap(block, axis_name, bit):
    route = [(i, i ^ (1 << bit)) for i in range(lax.axis_size(axis_name))]
    return lax.ppermute(block, axis_name, route)


def added(block):
    return jnp.sum(block.astype(f32), axis=0)


class Folding:
    bits = ((("dp", 1), ("dp", 2)), (("dp", 2), ("dp", 1)))

    def __init__(self, first, second):
        self.rows = first[0].shape[2]
        self.rest = first[0].shape[2:]
        self.mine = [first[0], second[0]]
        self.got = [swap(first[1], "dp", 0), swap(second[1], "dp", 0)]
        self.stage = 0

    def half(self, which, side):
        left = 3 - self.stage
        shape = (2, 2**left) + self.rest
        mine = self.mine[which].reshape(shape)
        got = self.got[which].reshape(shape)
        return mine[side].astype(f32) + got[side].astype(f32)

    def step(self):
        gives = [self.half(which, 1).astype(bf16) for which in range(len(self.mine))]
        self.mine = [self.half(which, 0).astype(bf16) for which in range(len(self.mine))]
        if self.stage < 2:
            self.got = [swap(give, *self.bits[which][self.stage]) for which, give in enumerate(gives)]
        else:
            if len(gives) > 1:
                gives = [jnp.concatenate(gives, axis=-2)]
                self.mine = [jnp.concatenate(self.mine, axis=-2)]
                self.rest = (2 * self.rows, self.rest[1])
            self.got = [swap(gives[0], "kern", self.stage - 2)]
        self.stage += 1
        return gives

    def take(self, rows):
        taken = []
        for which in range(2):
            shape = (2 ** (4 - self.stage),) + self.rest
            mine, got = self.mine[which].reshape(shape), self.got[which].reshape(shape)
            taken.append(mine[:, rows:].astype(f32) + got[:, rows:].astype(f32))
            self.mine[which], self.got[which] = mine[:, :rows], got[:, :rows]
        self.rows, self.rest = rows, (rows, self.rest[1])
        return [block.astype(bf16) for block in taken]

    def hold(self, anchor):
        self.mine = after(anchor, self.mine)

    def totals(self):
        block = self.mine[0].reshape(self.rest).astype(f32) + self.got[0].reshape(self.rest).astype(f32)
        return block[: self.rows], block[self.rows :]


def after(anchor, values):
    return lax.optimization_barrier((anchor, values))[1]


def shards(
    tokens,
    cotangent,
    in_weight,
    out_weight,
    up_weight,
    down_weight,
    first_gain,
    second_gain,
    raw_taps,
    pad_lengths,
):
    seq_count, row_count, feat = tokens.shape
    width = up_weight.shape[1]
    kern = lax.axis_size("kern")
    groups = lax.axis_size("dp")
    me = lax.axis_index("kern").astype(jnp.int32)
    my_group = lax.axis_index("dp").astype(jnp.int32)
    words = jnp.stack([me, my_group % 2, my_group // 2 % 2, my_group // 4])
    local_taps = raw_taps.shape[0]
    total_taps = local_taps * kern
    chan = feat // kern
    outer = row_count * kern // inner
    share = local_taps // groups
    deep = feat // groups
    in_rows = 2 * deep
    tabs = all_tables(outer)
    seqs = range(seq_count)

    def across(pieces, sign, *anchors):
        if anchors:
            pieces = after(anchors, pieces)
        if len(pieces) == 1:
            return [spread_out(pieces[0], "kern")]
        return exchange(pieces, sign)

    def copies(block):
        return jnp.broadcast_to(block[None], (groups, *block.shape))

    def to_all(block):
        return spread_out(copies(block), "dp")

    my_taps = lax.dynamic_slice_in_dim(raw_taps, my_group * share, share, 0)
    my_taps = shrink(my_taps).astype(bf16).reshape(share, kern, chan).transpose(1, 0, 2)
    limits = total_taps - lax.dynamic_slice_in_dim(pad_lengths, me * chan, chan, 0)[None]

    my_taps = spread_out(my_taps, "kern")

    heads, arrived = [], []
    for b in seqs:
        head = project(words, b, tokens, first_gain, in_weight, kern, b > 0, b == seq_count - 1)
        words = after(head[0], words)
        heads.append(head)
        if b == 0:
            all_taps = to_all(after(head[0], my_taps))
            arrived.append(across(head[2], -1))
        else:
            hidden_back = grad_hidden(words, cotangent, down_weight)
            words = after(hidden_back, words)
            arrived.append(across(head[2], -1, *arrived, all_taps, hidden_back))

    kernel_spec = tap_spectrum(words, all_taps, limits, tabs)
    words = after(kernel_spec, words)

    convs, returned = [], []
    for b in seqs:
        conv = convolve(words, arrived[b], kern, kernel_spec, tabs, False, None, b > 0)
        words = after(conv[1], words)
        convs.append(conv)
        returned.append(across(conv[0], 1, *returned))

    slope = lax.optimization_barrier(shrink_slope(raw_taps))
    words = after(slope, words)

    mids, arrived_back = [], []
    earlier, out_tokens = None, None
    for b in seqs:
        mid, grads, pieces = feed_forward(
            words,
            b,
            tokens,
            cotangent,
            hidden_back,
            heads[b][1],
            returned[b],
            heads[b][0],
            out_weight,
            up_weight,
            down_weight,
            second_gain,
            kern,
            groups,
            True,
            earlier,
            out_tokens,
        )
        words = after(mid[3], words)
        out_tokens, second_row = mid[0], mid[3]
        earlier = [*grads, second_row]
        mids.append(mid)
        arrived_back.append(across(pieces, -1, returned[-1], *arrived_back))
    u_keep, u_give, d_keep, d_give, out_t, gate_t = grads
    u_give, d_give = after(arrived_back[:-1], (u_give, d_give))
    wide_sums = Folding((u_keep, u_give), (d_keep, d_give))

    corrs, signal_back = [], []
    for b in seqs:
        corr = convolve(
            words, arrived_back[b], kern, kernel_spec, tabs, True, convs[b][1], b > 0
        )
        words = after(corr[1], words)
        corrs.append(corr)
        if b == 0:
            steps = wide_sums.step()
            words = after(steps, words)
            signal_back.append(across(corr[0], 1, steps))
        else:
            signal_back.append(across(corr[0], 1))

    wide_sums.hold(signal_back[0])
    words = after(wide_sums.step(), words)

    def write(word_ref, taps_ref, out_refs):
        for to, side in ((0, word_ref[1]), (1, 1 - word_ref[1])):
            for pair in range(groups // 2):
                for z in range(kern):
                    start = (z * groups + 2 * pair + side) * share
                    block = taps_ref[pl.ds(pl.multiple_of(start, share), share), :]
                    at = pair ^ own_pair(word_ref)
                    for h in range(2):
                        place = (flipped(at) if h == 0 else at, flipped(z ^ word_ref[0]))
                        half = block[h * share // 2 : (h + 1) * share // 2]
                        late_pack(out_refs[2 * h + to], place, half)

    shapes = [(groups // 2, kern, share // 4 * 3, 128)] * 4
    products = [corr[1] for corr in corrs]
    grad_taps = tap_gradient(words, products, limits, tabs, shapes, write)
    words = after(grad_taps, words)
    words = after(wide_sums.step(), words)

    late = late_gradients(
        words,
        signal_back,
        [head[0] for head in heads],
        gate_t,
        out_t,
        heads[-1][3],
        first_gain,
        second_row,
        grad_taps,
        kern,
        groups,
    )

    late_sums = Folding(late[:2], late[2:])
    grad_tokens = None
    for b in seqs:
        steps = late_sums.step()
        if b == 0:
            wide_sums.hold(steps)
            wide_sums.step()
        grad_tokens = finish(
            after(steps, words),
            b,
            tokens,
            mids[b][1],
            mids[b][2],
            signal_back[b],
            in_weight,
            first_gain,
            kern,
            grad_tokens,
        )
        late_sums.hold(grad_tokens)
    taps = jnp.stack(late_sums.take(late_packed), axis=1)
    steps = late_sums.step()
    taps = [taps[flipped(r)] for r in range(kern)]
    for r in range(1, kern):
        taps[r] = lax.ppermute(taps[r], "kern", [(i, i ^ r) for i in range(kern)])
    taps = late_unpack(jnp.stack(taps), share // 2).reshape(kern, share, chan)
    taps = jnp.concatenate(
        [lax.dynamic_index_in_dim(taps, me ^ z, 0, keepdims=False) for z in range(kern)], axis=1
    )
    taps = copies(taps)
    late_sums.hold(taps)
    wide_sums.hold(late_sums.step())
    up, down = wide_sums.totals()
    grad_taps = spread_out(taps, "dp").reshape(local_taps, feat)
    grad_raw = grad_taps.astype(f32) * slope

    sum_up = jnp.concatenate(jnp.split(up, 2, axis=1), axis=0)
    sum_down = down.T
    late = jnp.concatenate([late_unpack(block, late_rows) for block in late_sums.totals()], axis=0)
    sum_in = late[:in_rows].T
    sum_out = late[in_rows : in_rows + deep].T
    return (
        out_tokens,
        grad_tokens,
        sum_in,
        sum_out,
        sum_up,
        sum_down,
        late[in_rows + deep],
        late[in_rows + deep + 1],
        grad_raw,
    )


def solution(mesh):
    placed = (
        P("dp", "kern", None),
        P("dp", "kern", None),
        P(),
        P(),
        P(),
        P(),
        P(),
        P(),
        P("kern", None),
        P(),
    )
    placed_out = (
        P("dp", "kern", None),
        P("dp", "kern", None),
        P("kern", "dp"),
        P("kern", "dp"),
        P("kern", "dp"),
        P("kern", "dp"),
        P("kern"),
        P("kern"),
        P("kern", None),
    )
    groups, kern = mesh.shape["dp"], mesh.shape["kern"]

    def layer(*arrays):
        seq_count, length, feat = arrays[0].shape
        seq_count = seq_count // groups
        width = arrays[4].shape[1]
        rows = length // kern
        tiles = (
            feat % (16 * groups) == 0
            and width % (128 * groups) == 0
            and width == groups // 2 * feat
            and groups == 8
            and kern == 4
            and rows % (2 * inner) == 0
            and 3 * feat // groups + 2 <= 2 * late_rows
            and seq_count == 2
            and feat // kern == 192
            and arrays[8].shape[0] == 64 * groups * kern
        )
        return run(shards if tiles else shards_general)(*arrays)

    def run(body):
        return jax.shard_map(
            body,
            mesh=mesh,
            in_specs=placed,
            out_specs=placed_out,
            check_vma=False,
        )

    return layer
```

```python
import math

import jax
import jax.numpy as jnp
import ml_dtypes
import numpy as np
from jax import lax
from jax.experimental import pallas as pl
from jax.experimental.pallas import tpu as pltpu
from jax.sharding import PartitionSpec as P

shrink_level = 0.003
norm_eps = 1e-05
bf16 = jnp.bfloat16
f32 = jnp.float32
inner = 128
group = 16
wide = 8


def inner_tables(outer):
    length = outer * inner
    k1 = np.arange(outer)[:, None, None]
    k2 = np.arange(inner)[None, :, None]
    n2 = np.arange(inner)[None, None, :]
    turns = (n2 * (4 * (outer * k2 + k1) + 1)) % (4 * length)
    angle = turns * (2 * math.pi / (4 * length))
    c, s = np.cos(angle), np.sin(angle)
    table = np.concatenate([np.concatenate([c, s], 2), np.concatenate([-s, c], 2)], 1)
    return table.astype(ml_dtypes.bfloat16)


def outer_tables(outer):
    k1 = np.arange(outer)[:, None]
    n1 = np.arange(outer)[None, :]
    angle = (n1 * (4 * k1 + 1)) % (4 * outer) * (2 * math.pi / (4 * outer))
    parts = np.stack([np.cos(angle), -np.sin(angle)], 1)
    table = np.einsum("kcn,ij->kcinj", parts, np.eye(group))
    table = table.reshape(outer * 2 * group, outer * group)
    return table.astype(ml_dtypes.bfloat16), table.T.astype(ml_dtypes.bfloat16)


def all_tables(outer):
    first, last = outer_tables(outer)
    tabs = {"inner": inner_tables(outer), "first": first, "last": last}
    return {key: jnp.asarray(value) for key, value in tabs.items()}


def outer_forward(x_ref, table_ref, y_ref):
    outer, _, ch = x_ref.shape

    def step(j, carry):
        rows = pl.ds(pl.multiple_of(j * group, group), group)
        x = x_ref[:, rows, :].reshape(outer * group, ch)
        y = jnp.dot(table_ref[...], x, preferred_element_type=f32).astype(bf16)
        y = y.reshape(outer, 2, group, ch)
        y_ref[:, 0, rows, :] = y[:, 0]
        y_ref[:, 1, rows, :] = y[:, 1]
        return carry

    lax.fori_loop(0, inner // group, step, 0, unroll=8)


def outer_back(w_ref, table_ref, x_ref):
    outer, _, _, ch = w_ref.shape

    def step(j, carry):
        rows = pl.ds(pl.multiple_of(j * group, group), group)
        w = w_ref[:, :, rows, :].reshape(outer * 2 * group, ch)
        x = jnp.dot(table_ref[...], w, preferred_element_type=f32)
        x_ref[:, rows, :] = x.astype(x_ref.dtype).reshape(outer, group, ch)
        return carry

    lax.fori_loop(0, inner // group, step, 0, unroll=8)


def whole(shape):
    return pl.BlockSpec(shape, lambda i: (0,) * len(shape))


def slab(*shape):
    return pl.BlockSpec((wide,) + shape, lambda i: (i,) + (0,) * len(shape))


def smem():
    return pl.BlockSpec(memory_space=pltpu.SMEM)


def params(mib):
    return pltpu.CompilerParams(
        vmem_limit_bytes=mib * 2**20, dimension_semantics=("arbitrary",)
    )


def cost(micros):
    return pl.CostEstimate(
        flops=int(micros * 8e8), bytes_accessed=int(micros * 1e6), transcendentals=0
    )


def tap_spectrum(words, taps, limits, tabs):
    groups, kern, share, ch = taps.shape
    length = groups * kern * share
    outer = length // inner

    def kernel(_, taps_ref, limit_ref, table_ref, first_ref, out_ref, x_ref, y_ref, flat_ref):
        @pl.when(pl.program_id(0) == 0)
        def _():
            for z in range(kern):
                for p in range(groups):
                    at = (z * groups + p) * share
                    flat_ref[at : at + share] = taps_ref[p, z].astype(f32)
            values = flat_ref[...]
            edge = jnp.zeros((1, ch), f32)
            below = jnp.concatenate([edge, values[:-1]], 0)
            above = jnp.concatenate([values[1:], edge], 0)
            index = lax.broadcasted_iota(jnp.int32, (length, ch), 0)
            values = jnp.where(index < limit_ref[...], (below + values + above) / 3.0, 0.0)
            x_ref[...] = values.astype(bf16).reshape(outer, inner, ch)
            outer_forward(x_ref, first_ref, y_ref)

        for i in range(wide):
            y = y_ref[pl.program_id(0) * wide + i].reshape(2 * inner, ch)
            s = jnp.dot(table_ref[i], y, preferred_element_type=f32)
            out_ref[i] = (s * (1.0 / length)).astype(bf16)

    return pl.pallas_call(
        kernel,
        grid=(outer // wide,),
        in_specs=[
            smem(),
            whole(taps.shape),
            whole((1, ch)),
            slab(2 * inner, 2 * inner),
            whole(tabs["first"].shape),
        ],
        out_specs=slab(2 * inner, ch),
        out_shape=jax.ShapeDtypeStruct((outer, 2 * inner, ch), bf16),
        scratch_shapes=[
            pltpu.VMEM((outer, inner, ch), bf16),
            pltpu.VMEM((outer, 2, inner, ch), bf16),
            pltpu.VMEM((length, ch), f32),
        ],
        compiler_params=params(56),
        cost_estimate=cost(6),
        name="tap_spectrum",
    )(words, taps, limits, tabs["inner"], tabs["first"])


def packed(rows, ch):
    if ch % 128 == 64 and rows % (2 * inner) == 0:
        return (rows // inner * (2 * ch // 128) // 2, inner, 128)
    return (rows // inner, inner, ch)


def pack(ref, lead, values, part, parts):
    rows, ch = values.shape
    blocks = rows // inner
    if ref.shape[-1] == ch:
        ref[(*lead, pl.ds(part * blocks, blocks))] = values.reshape(blocks, inner, ch)
        return
    full = ch // 128
    for j in range(full):
        at = (j * parts + part) * blocks
        lanes = values[:, j * 128 : (j + 1) * 128]
        ref[(*lead, pl.ds(at, blocks))] = lanes.reshape(blocks, inner, 128)
    rest = values[:, full * 128 :]
    half = parts * blocks // 2
    for t in range(blocks):
        at = part * blocks + t
        side, row = at // half, at % half
        ref[(*lead, full * parts * blocks + row, slice(None), slice(side * 64, side * 64 + 64))] = (
            rest[t * inner : (t + 1) * inner]
        )


def unpack(ref, lead, part, parts, ch, blocks):
    if ref.shape[-1] == ch:
        return [(0, ref[(*lead, pl.ds(part * blocks, blocks))])]
    full = ch // 128
    out = []
    for j in range(full):
        at = (j * parts + part) * blocks
        out.append((j * 128, ref[(*lead, pl.ds(at, blocks))]))
    half = parts * blocks // 2
    rest = []
    for t in range(blocks):
        at = part * blocks + t
        side, row = at // half, at % half
        rest.append(
            ref[(*lead, full * parts * blocks + row, slice(None), slice(side * 64, side * 64 + 64))]
        )
    out.append((full * 128, jnp.stack(rest)))
    return out


def owners(me_ref, refs, kern, sign):
    if len(refs) == 1 and kern > 1:
        return [(refs[0], (k,), k) for k in range(kern)]
    return [
        (ref, (), lax.rem(me_ref[0] + (k if sign > 0 else kern - k), kern))
        for k, ref in enumerate(refs)
    ]


def piece_shapes(kern, rows, ch, stacked):
    shape = packed(rows, ch)
    return [(kern, *shape)] if stacked else [shape] * kern


def place_pieces(me_ref, piece_refs, x_ref, kern):
    outer, _, ch = x_ref.shape
    blocks = outer // kern
    for ref, lead, owner in owners(me_ref, piece_refs, kern, 1):
        for at, block in unpack(ref, lead, 0, 1, ch, blocks):
            x_ref[pl.ds(owner * blocks, blocks), :, at : at + block.shape[2]] = block


def take_pieces(me_ref, x_ref, piece_refs, kern):
    outer, _, ch = x_ref.shape
    blocks = outer // kern
    for ref, lead, owner in owners(me_ref, piece_refs, kern, 1):
        pack(ref, lead, x_ref[pl.ds(owner * blocks, blocks)].reshape(blocks * inner, ch), 0, 1)


def convolve(me, pieces, kern, kernel_spec, tabs, flip, other_spec=None, stacked=False):
    count = len(pieces)
    outer, _, ch = kernel_spec.shape
    shapes = piece_shapes(kern, outer * inner // kern, ch, stacked)

    def kernel(me_ref, *refs):
        piece_refs, refs = refs[:count], refs[count:]
        spec_ref, table_ref, first_ref, last_ref = refs[:4]
        refs = refs[4:]
        if flip:
            other_ref, refs = refs[0], refs[1:]
        out_refs, refs = refs[: len(shapes)], refs[len(shapes) :]
        save_ref, x_ref, y_ref, w_ref = refs
        step = pl.program_id(0)

        @pl.when(step == 0)
        def _():
            place_pieces(me_ref, piece_refs, x_ref, kern)
            outer_forward(x_ref, first_ref, y_ref)

        for i in range(wide):
            at = step * wide + i
            y = y_ref[at].reshape(2 * inner, ch)
            s = jnp.dot(table_ref[i], y, preferred_element_type=f32)
            sr, si = s[:inner], s[inner:]
            kr = spec_ref[i, :inner].astype(f32)
            ki = spec_ref[i, inner:].astype(f32)
            if flip:
                orr = other_ref[i, :inner].astype(f32)
                oi = other_ref[i, inner:].astype(f32)
                save_ref[i, :inner] = (sr * orr + si * oi).astype(bf16)
                save_ref[i, inner:] = (si * orr - sr * oi).astype(bf16)
                zr, zi = sr * kr + si * ki, si * kr - sr * ki
            else:
                save_ref[i] = s.astype(bf16)
                zr, zi = sr * kr - si * ki, sr * ki + si * kr
            z = jnp.concatenate([zr, zi], 0).astype(bf16)
            w = mm_tn(table_ref[i], z)
            w_ref[at] = w.astype(bf16).reshape(2, inner, ch)

        @pl.when(step == pl.num_programs(0) - 1)
        def _():
            outer_back(w_ref, last_ref, x_ref)
            take_pieces(me_ref, x_ref, out_refs, kern)

    args = [me, *pieces, kernel_spec, tabs["inner"], tabs["first"], tabs["last"]]
    in_specs = [smem()] + [whole(piece.shape) for piece in pieces] + [
        slab(2 * inner, ch),
        slab(2 * inner, 2 * inner),
        whole(tabs["first"].shape),
        whole(tabs["last"].shape),
    ]
    if flip:
        args.append(other_spec)
        in_specs.append(slab(2 * inner, ch))
    outs = pl.pallas_call(
        kernel,
        grid=(outer // wide,),
        in_specs=in_specs,
        out_specs=[whole(shape) for shape in shapes] + [slab(2 * inner, ch)],
        out_shape=[jax.ShapeDtypeStruct(shape, bf16) for shape in shapes]
        + [jax.ShapeDtypeStruct((outer, 2 * inner, ch), bf16)],
        scratch_shapes=[
            pltpu.VMEM((outer, inner, ch), bf16),
            pltpu.VMEM((outer, 2, inner, ch), bf16),
            pltpu.VMEM((outer, 2, inner, ch), bf16),
        ],
        compiler_params=params(56),
        cost_estimate=cost(8),
        name="correlate" if flip else "convolve",
    )(*args)
    return list(outs[:-1]), outs[-1]


def tap_gradient(words, products, limits, tabs, out_shapes, write):
    outer, _, ch = products[0].shape
    length = outer * inner

    def kernel(word_ref, limit_ref, *refs):
        spec_refs, refs = refs[: len(products)], refs[len(products) :]
        table_ref, last_ref, refs = refs[0], refs[1], refs[2:]
        out_refs, (w_ref, x_ref, t_ref) = refs[: len(out_shapes)], refs[len(out_shapes) :]
        step = pl.program_id(0)
        for i in range(wide):
            z = spec_refs[0][i].astype(f32)
            for spec_ref in spec_refs[1:]:
                z = z + spec_ref[i].astype(f32)
            w = mm_tn(table_ref[i], (z * (1.0 / length)).astype(bf16))
            w_ref[step * wide + i] = w.astype(bf16).reshape(2, inner, ch)

        @pl.when(step == pl.num_programs(0) - 1)
        def _():
            outer_back(w_ref, last_ref, x_ref)
            taps = x_ref[...].reshape(length, ch)
            index = lax.broadcasted_iota(jnp.int32, (length, ch), 0)
            taps = jnp.where(index < limit_ref[...], taps, 0.0)
            edge = jnp.zeros((1, ch), f32)
            below = jnp.concatenate([edge, taps[:-1]], 0)
            above = jnp.concatenate([taps[1:], edge], 0)
            t_ref[...] = ((below + taps + above) / 3.0).astype(bf16)
            write(word_ref, t_ref, out_refs)

    return pl.pallas_call(
        kernel,
        grid=(outer // wide,),
        in_specs=[smem(), whole((1, ch))]
        + [slab(2 * inner, ch)] * len(products)
        + [slab(2 * inner, 2 * inner), whole(tabs["last"].shape)],
        out_specs=[whole(shape) for shape in out_shapes],
        out_shape=[jax.ShapeDtypeStruct(shape, bf16) for shape in out_shapes],
        scratch_shapes=[
            pltpu.VMEM((outer, 2, inner, ch), bf16),
            pltpu.VMEM((outer, inner, ch), f32),
            pltpu.VMEM((length, ch), bf16),
        ],
        compiler_params=params(56),
        cost_estimate=cost(5),
        name="tap_gradient",
    )(words, limits, *products, tabs["inner"], tabs["last"])


def exchange(pieces, sign):
    count = len(pieces)
    moved = [pieces[0]]
    for k in range(1, count):
        route = [(i, (i + sign * k) % count) for i in range(count)]
        moved.append(lax.ppermute(pieces[k], "kern", route))
    return moved


def spread_out(block, axis_name, groups=None):
    return lax.all_to_all(
        block, axis_name, split_axis=0, concat_axis=0, tiled=True, axis_index_groups=groups
    )


def sum_all(row):
    for axis_name in ("dp", "kern"):
        count = lax.axis_size(axis_name)
        for bit in range(count.bit_length() - 1):
            route = [(i, i ^ (1 << bit)) for i in range(count)]
            row = row + lax.ppermute(row, axis_name, route)
    return row


def padded_rows(block):
    count = lax.axis_size("kern")
    forward = [(i, i + 1) for i in range(count - 1)]
    backward = [(target, source) for source, target in forward]
    low = lax.ppermute(block[-1:], "kern", forward)
    high = lax.ppermute(block[:1], "kern", backward)
    return jnp.concatenate([low, block, high], axis=0)


def layer_norm(values, norm_gain):
    center = values - jnp.mean(values, axis=-1, keepdims=True)
    spread = jnp.mean(center * center, axis=-1, keepdims=True)
    return center * lax.rsqrt(spread + norm_eps) * norm_gain


def shrink(tap_values):
    return tap_values - shrink_level * tap_values / jnp.sqrt(
        tap_values * tap_values + shrink_level * shrink_level
    )


def shrink_slope(tap_values):
    return 1.0 - shrink_level**3 / (tap_values * tap_values + shrink_level * shrink_level) ** 1.5


def pool_three(padded):
    return (padded[:-2] + padded[1:-1] + padded[2:]) / 3.0


def dot(left, right, dims):
    return lax.dot_general(left, right, (dims, ((), ())), preferred_element_type=f32)


def shards_general(
    tokens,
    cotangent,
    in_weight,
    out_weight,
    up_weight,
    down_weight,
    first_gain,
    second_gain,
    raw_taps,
    pad_lengths,
):
    seq_count, row_count, feat = tokens.shape
    kern = lax.axis_size("kern")
    me = lax.axis_index("kern")
    me_word = me.astype(jnp.int32).reshape(1)
    groups = lax.axis_size("dp")
    local_taps = raw_taps.shape[0]
    total_taps = local_taps * kern
    chan = feat // kern
    outer = row_count * kern // inner
    blocks = row_count // inner
    tabs = all_tables(outer)

    limits = total_taps - lax.dynamic_slice_in_dim(pad_lengths, me * chan, chan, 0)[None]
    my_raw = lax.all_to_all(raw_taps, "kern", split_axis=1, concat_axis=0, tiled=True)
    kernel_spec = tap_spectrum(me_word, shrink(my_raw)[None, None], limits, tabs)

    def apart(values):
        values = values.reshape(blocks, inner, kern, chan).transpose(2, 0, 1, 3)
        return [values[(me - k) % kern] for k in range(kern)]

    def joined(pieces):
        stack = jnp.stack(pieces)
        stack = jnp.stack([stack[(me - k) % kern] for k in range(kern)])
        return stack.transpose(1, 2, 0, 3).reshape(row_count, feat)

    def one(x, cot):
        inputs = x.astype(f32)
        first_norm, first_pull = jax.vjp(layer_norm, inputs, first_gain)
        normed = first_norm.astype(bf16)
        projected = dot(normed, in_weight, ((1,), (0,)))
        gate = projected[:, feat:]
        pieces = exchange(apart(projected[:, :feat].astype(bf16)), -1)
        pieces, spectrum = convolve(me_word, pieces, kern, kernel_spec, tabs, False)
        convolved = joined(exchange(pieces, 1)).astype(f32)
        mixed = (gate * convolved).astype(bf16)
        middle = inputs + dot(mixed, out_weight, ((1,), (0,)))
        second_norm, second_pull = jax.vjp(layer_norm, middle, second_gain)
        normed_two = second_norm.astype(bf16)
        raised = dot(normed_two, up_weight, ((1,), (0,)))
        activated, gelu_pull = jax.vjp(jax.nn.gelu, raised)
        hidden = activated.astype(bf16)
        out = (middle + dot(hidden, down_weight, ((1,), (0,)))).astype(bf16)
        grad_raised = gelu_pull(dot(cot, down_weight, ((1,), (1,))))[0].astype(bf16)
        grad_mid, second_row = second_pull(dot(grad_raised, up_weight, ((1,), (1,))))
        grad_mid = cot.astype(f32) + grad_mid
        branch = grad_mid.astype(bf16)
        grad_mixed = dot(branch, out_weight, ((1,), (1,)))
        grad_gate = (grad_mixed * convolved).astype(bf16)
        pieces = exchange(apart((grad_mixed * gate).astype(bf16)), -1)
        pieces, product = convolve(me_word, pieces, kern, kernel_spec, tabs, True, spectrum)
        grad_signal = joined(exchange(pieces, 1))
        grad_projected = jnp.concatenate([grad_signal, grad_gate], axis=-1)
        grad_first, first_row = first_pull(dot(grad_projected, in_weight, ((1,), (1,))))
        weights = (
            dot(normed, grad_projected, ((0,), (0,))),
            dot(mixed, branch, ((0,), (0,))),
            dot(normed_two, grad_raised, ((0,), (0,))),
            dot(hidden, cot, ((0,), (0,))),
        )
        return out, (grad_mid + grad_first).astype(bf16), product, (first_row, second_row), weights

    ones = [one(tokens[b], cotangent[b]) for b in range(seq_count)]
    rows, weights = ones[0][3:]
    for other in ones[1:]:
        rows, weights = jax.tree.map(jnp.add, (rows, weights), other[3:])
    def write(_, taps_ref, out_refs):
        out_refs[0][...] = taps_ref[...]

    products = [item[2] for item in ones]
    shapes = [(total_taps, chan)]
    grad_taps = tap_gradient(me_word, products, limits, tabs, shapes, write)[0]
    grad_taps = lax.all_to_all(grad_taps, "kern", split_axis=0, concat_axis=1, tiled=True)
    grad_raw = lax.psum(grad_taps, "dp").astype(f32) * shrink_slope(raw_taps)
    sums = []
    for weight in weights:
        weight = lax.psum_scatter(weight.astype(bf16), "dp", scatter_dimension=1, tiled=True)
        weight = lax.psum_scatter(weight, "kern", scatter_dimension=0, tiled=True)
        sums.append(weight.astype(f32))
    gains = sum_all(jnp.stack(rows))
    gains = lax.dynamic_slice_in_dim(gains, me * chan, chan, 1)
    return (
        jnp.stack([item[0] for item in ones]),
        jnp.stack([item[1] for item in ones]),
        *sums,
        gains[0],
        gains[1],
        grad_raw,
    )


def row_mean(values):
    return jnp.mean(values, axis=-1, keepdims=True)


def centered(values):
    center = values - row_mean(values)
    inverse = lax.rsqrt(row_mean(center * center) + norm_eps)
    return center * inverse, inverse


def norm_back(grad, normed, inverse, gain):
    scaled = grad * gain
    return inverse * (scaled - row_mean(scaled) - normed * row_mean(scaled * normed))


def mm(left, right):
    return jnp.dot(left, right, preferred_element_type=f32)


def mm_nt(left, right):
    return lax.dot_general(left, right, (((1,), (1,)), ((), ())), preferred_element_type=f32)


def mm_tn(left, right):
    return lax.dot_general(left, right, (((0,), (0,)), ((), ())), preferred_element_type=f32)


def fixed(shape):
    return pl.BlockSpec(shape, lambda *_: (0,) * len(shape))


def once(shape):
    return pl.BlockSpec(
        shape, lambda *_: (0,) * len(shape), pipeline_mode=pl.Buffered(1)
    )


def along(seq, rows, feat):
    return pl.BlockSpec((1, rows, feat), lambda i: (seq, i, 0))


def cut(me_ref, values, piece_refs, stack_ref, part=0, parts=1):
    kern, rows, ch = stack_ref.shape
    if len(piece_refs) > 1:
        for k in range(kern):
            stack_ref[k] = values[:, k * ch : (k + 1) * ch]
    for ref, lead, owner in owners(me_ref, piece_refs, kern, -1):
        block = stack_ref[owner] if len(piece_refs) > 1 else values[:, owner * ch : (owner + 1) * ch]
        pack(ref, lead, block, part, parts)


def join(me_ref, piece_refs, stack_ref, out_ref, part=0, parts=1):
    kern, rows, ch = stack_ref.shape
    blocks = rows // inner
    for ref, lead, owner in owners(me_ref, piece_refs, kern, -1):
        for at, block in unpack(ref, lead, part, parts, ch, blocks):
            width = block.shape[2]
            block = block.reshape(rows, width)
            if len(piece_refs) > 1:
                stack_ref[owner, :, at : at + width] = block
            else:
                out_ref[:, owner * ch + at : owner * ch + at + width] = block
    if len(piece_refs) > 1:
        for k in range(kern):
            out_ref[:, k * ch : (k + 1) * ch] = stack_ref[k]


def project(me, seq, tokens, gain, weight, kern, stacked, turn=False):
    _, rows, feat = tokens.shape
    chan = feat // kern
    parts = 1
    tile = rows // parts
    shapes = piece_shapes(kern, rows, chan, stacked)
    turned_shape = [weight.shape[::-1]] if turn else []

    def kernel(me_ref, x_ref, gain_ref, weight_ref, *refs):
        normed_ref, gate_ref = refs[:2]
        piece_refs, stack_ref = refs[2 : 2 + len(shapes)], refs[-1]
        if turn:
            pl.when(pl.program_id(0) == 0)(lambda: put_turned(weight_ref, refs[-2]))
        hat, _ = centered(x_ref[0].astype(f32))
        normed = (hat * gain_ref[...]).astype(bf16)
        normed_ref[...] = normed
        projected = mm(normed, weight_ref[...])
        gate_ref[...] = projected[:, feat:]
        signal = projected[:, :feat].astype(bf16)
        for part in range(parts):
            pl.when(pl.program_id(0) == part)(
                lambda: cut(me_ref, signal, piece_refs, stack_ref, part, parts)
            )

    outs = pl.pallas_call(
        kernel,
        grid=(parts,),
        in_specs=[smem(), along(seq, tile, feat), fixed((feat,)), fixed(weight.shape)],
        out_specs=[
            pl.BlockSpec((tile, feat), lambda i: (i, 0)),
            pl.BlockSpec((tile, feat), lambda i: (i, 0)),
        ]
        + [fixed(shape) for shape in shapes + turned_shape],
        out_shape=[
            jax.ShapeDtypeStruct((rows, feat), bf16),
            jax.ShapeDtypeStruct((rows, feat), f32),
        ]
        + [jax.ShapeDtypeStruct(shape, bf16) for shape in shapes + turned_shape],
        scratch_shapes=[pltpu.VMEM((kern, tile, chan), bf16)],
        compiler_params=params(56),
        cost_estimate=cost(4),
        name="project",
    )(me, tokens, gain, weight)
    return outs[0], outs[1], list(outs[2 : 2 + len(shapes)]), outs[-1]


def put_turned(from_ref, to_ref):
    to_ref[...] = from_ref[...].T


def gelu_pair(raised):
    root = math.sqrt(2.0 / math.pi)
    square = raised * raised
    t = jnp.tanh(raised * (root + (root * 0.044715) * square))
    half = 0.5 + 0.5 * t
    slope = half + (0.5 * raised) * (1.0 - t * t) * (root + (3.0 * root * 0.044715) * square)
    return raised * half, slope


def own_pair(words):
    return 2 * words[3] + words[2]


def grad_hidden(words, cots, down_weight):
    seqs, rows, feat = cots.shape
    width = down_weight.shape[0]
    chunk = feat

    def kernel(_, cot_ref, down_ref, out_ref):
        out = mm_nt(cot_ref[...].reshape(seqs * rows, feat), down_ref[...])
        out_ref[...] = out.astype(bf16).reshape(seqs, rows, chunk)

    return pl.pallas_call(
        kernel,
        grid=(width // chunk,),
        in_specs=[smem(), fixed(cots.shape), pl.BlockSpec((chunk, feat), lambda i: (i, 0))],
        out_specs=pl.BlockSpec((seqs, rows, chunk), lambda i: (0, 0, i)),
        out_shape=jax.ShapeDtypeStruct((seqs, rows, width), bf16),
        compiler_params=params(56),
        cost_estimate=cost(6),
        name="grad_hidden",
    )(words, cots, down_weight)


def flipped(place):
    return 2 * (place & 1) + (place >> 1)


def feed_forward(words, seq, tokens, cots, grads, gate, conv, normed, out_weight, up_weight, down_weight, gain, kern, groups, stacked, earlier, out_before):
    seqs, rows, feat = tokens.shape
    width = up_weight.shape[1]
    count = len(conv)
    shapes = piece_shapes(kern, rows, feat // kern, stacked)
    chan = feat // kern
    pairs = groups // 2
    chunk = width // pairs
    deep = feat // groups
    half = chunk // 2
    add = earlier is not None

    def kernel(word_ref, x_ref, cot_ref, gh_ref, gate_ref, ow_ref, up_ref, down_ref, gain_ref, *refs):
        conv_refs, refs = refs[:count], refs[count:]
        if add:
            old, refs = refs[:5], refs[5:]
        far_refs, refs = refs[: len(far)], refs[len(far) :]
        ggain_ref, out_ref, mid_ref, ggate_ref = refs[:4]
        u_keep, u_give, d_keep, d_give, o_ref, g_ref = refs[4:10]
        piece_refs, refs = refs[10 : 10 + len(shapes)], refs[10 + len(shapes) :]
        stack_s, cv, mixed_s, middle_s, n2_s, acc_s, back_s, o_s, g_s = refs[:9]
        piece_s, refs = refs[9 : 9 + len(shapes)], refs[9 + len(shapes) :]
        near_refs, in_sem, out_sem = refs[: len(loaded)], refs[-2], refs[-1]
        f = pl.program_id(0)
        loads = [
            pltpu.make_async_copy(far_ref, near_ref, in_sem.at[i])
            for i, (far_ref, near_ref) in enumerate(zip(far_refs, near_refs))
        ]
        cot = cot_ref.at[0]

        @pl.when(f == 0)
        def _():
            for load in loads:
                load.start()
            join(word_ref, conv_refs, stack_s, cv)
            mixed = (gate_ref[...] * cv[...].astype(f32)).astype(bf16)
            mixed_s[...] = mixed
            middle = x_ref[0].astype(f32) + mm(mixed, ow_ref[...])
            middle_s[...] = middle
            hat, _ = centered(middle)
            n2_s[...] = (hat * gain_ref[...]).astype(bf16)
            acc_s[...] = middle
            back_s[...] = jnp.zeros_like(back_s)

        hidden, grad_raised = [], []
        for at in range(0, rows, rows // 2):
            part = slice(at, at + rows // 2)
            act, slope = gelu_pair(mm(n2_s[part], up_ref[...]))
            hidden.append(act.astype(bf16))
            grad_raised.append((gh_ref[0, part].astype(f32) * slope).astype(bf16))
        hidden = jnp.concatenate(hidden, 0)
        grad_raised = jnp.concatenate(grad_raised, 0)
        acc_s[...] += mm(hidden, down_ref[...])
        back_s[...] += mm_nt(grad_raised, up_ref[...])
        u = mm_tn(n2_s[...], grad_raised).astype(bf16)
        d = mm_tn(cot[...], hidden).astype(bf16).reshape(pairs, 2, deep, chunk)
        even = word_ref[1] == 0
        for to, u_ref, d_ref, u_old, d_old in (
            (0, u_keep, d_keep, 0, 2),
            (1, u_give, d_give, 1, 3),
        ):
            for pair in range(pairs):
                at = pair ^ own_pair(word_ref)
                part = jnp.where(even, d[pair, to], d[pair, 1 - to])
                d_ref[at, 0] = part + old[d_old][at, 0] if add else part
            uu = jnp.where(
                even,
                u[:, to * half : (to + 1) * half],
                u[:, (1 - to) * half : (2 - to) * half],
            ).reshape(kern, 2, deep, half)
            for z in range(kern):
                at = flipped(z ^ word_ref[0])
                part = jnp.concatenate([uu[z, 0], uu[z, 1]], axis=1)
                u_ref[0, at] = part + old[u_old][0, at] if add else part

        @pl.when(f == pairs - 1)
        def _():
            stores = []

            def store(near_ref, far_ref):
                stores.append(pltpu.make_async_copy(near_ref, far_ref, out_sem.at[len(stores)]))
                stores[-1].start()

            n2_s[...] = acc_s[...].astype(bf16)
            store(n2_s, out_ref.at[seq])
            hat, inverse = centered(middle_s[...])
            back = back_s[...]
            ggain = jnp.sum(back * hat, axis=0, keepdims=True)
            ggain_ref[...] = ggain + old[4][...] if add else ggain
            grad_mid = cot[...].astype(f32) + norm_back(back, hat, inverse, gain_ref[...])
            back_s[...] = grad_mid
            store(back_s, mid_ref)
            branch = grad_mid.astype(bf16)
            grad_mixed = mm_nt(branch, ow_ref[...])
            cut(word_ref, (grad_mixed * gate_ref[...]).astype(bf16), piece_s, stack_s)
            for near_ref, far_ref in zip(piece_s, piece_refs):
                store(near_ref, far_ref)
            ggate = (grad_mixed * cv[...].astype(f32)).astype(bf16)
            cv[...] = ggate
            store(cv, ggate_ref)
            for load in loads:
                load.wait()
            o = mm_tn(branch, mixed_s[...])
            o_s[...] = (o + near_refs[1][...].astype(f32) if add else o).astype(bf16)
            store(o_s, o_ref)
            g = mm_tn(ggate, near_refs[0][...])
            g_s[...] = (g + near_refs[2][...].astype(f32) if add else g).astype(bf16)
            store(g_s, g_ref)
            for item in stores:
                item.wait()

    u_spec = pl.BlockSpec((1, kern, deep, chunk), lambda f, w: (flipped(f ^ own_pair(w)), 0, 0, 0))
    d_spec = pl.BlockSpec((pairs, 1, deep, chunk), lambda f, w: (0, flipped(f ^ w[0]), 0, 0))
    anywhere = pl.BlockSpec(memory_space=pl.ANY)
    one = pl.BlockSpec((1, rows, feat), lambda f, w: (seq, 0, 0))
    args = [words, tokens, cots, grads, gate, out_weight, up_weight, down_weight, gain, *conv]
    in_specs = [
        one,
        one,
        pl.BlockSpec((1, rows, chunk), lambda f, w: (seq, 0, f)),
        once((rows, feat)),
        once(out_weight.shape),
        pl.BlockSpec((feat, chunk), lambda f, w: (0, f)),
        pl.BlockSpec((chunk, feat), lambda f, w: (f, 0)),
        fixed((feat,)),
    ] + [fixed(piece.shape) for piece in conv]
    grad_specs = [u_spec, u_spec, d_spec, d_spec]
    loaded = [normed]
    aliases = {}
    if add:
        *big_before, o_before, g_before, row_before = earlier
        args += [*big_before, row_before]
        in_specs += [*grad_specs, fixed((1, feat))]
        loaded += [o_before, g_before]
    far = list(loaded)
    if add:
        far.append(out_before)
        aliases = {len(args) + len(loaded): 1}
    args += far
    in_specs += [anywhere] * len(far)
    big = jax.ShapeDtypeStruct((pairs, kern, deep, chunk), bf16)
    outs = pl.pallas_call(
        kernel,
        grid_spec=pltpu.PrefetchScalarGridSpec(
            num_scalar_prefetch=1,
            grid=(pairs,),
            in_specs=in_specs,
            out_specs=[fixed((1, feat))]
            + [anywhere] * 3
            + grad_specs
            + [anywhere] * (2 + len(shapes)),
            scratch_shapes=[
                pltpu.VMEM((kern, rows, feat // kern), bf16),
                pltpu.VMEM((rows, feat), bf16),
                pltpu.VMEM((rows, feat), bf16),
                pltpu.VMEM((rows, feat), f32),
                pltpu.VMEM((rows, feat), bf16),
                pltpu.VMEM((rows, feat), f32),
                pltpu.VMEM((rows, feat), f32),
                pltpu.VMEM((feat, feat), bf16),
                pltpu.VMEM((feat, feat), bf16),
            ]
            + [pltpu.VMEM(shape, bf16) for shape in shapes]
            + [pltpu.VMEM(block.shape, bf16) for block in loaded]
            + [
                pltpu.SemaphoreType.DMA((len(loaded),)),
                pltpu.SemaphoreType.DMA((5 + len(shapes),)),
            ],
        ),
        out_shape=[
            jax.ShapeDtypeStruct((1, feat), f32),
            jax.ShapeDtypeStruct(tokens.shape, bf16),
            jax.ShapeDtypeStruct((rows, feat), f32),
            jax.ShapeDtypeStruct((rows, feat), bf16),
            big,
            big,
            big,
            big,
            jax.ShapeDtypeStruct((feat, feat), bf16),
            jax.ShapeDtypeStruct((feat, feat), bf16),
        ]
        + [jax.ShapeDtypeStruct(shape, bf16) for shape in shapes],
        input_output_aliases=aliases,
        compiler_params=params(56),
        cost_estimate=cost(24),
        name="feed_forward",
    )(*args)
    row, out, mid, ggate = outs[:4]
    return (out, mid, ggate, row), list(outs[4:10]), list(outs[10:])


late_rows = 160
late_packed = 240


def finish(words, seq, tokens, grad_mid, grad_gate, signal, weight, gain, kern, out_before):
    seqs, rows, feat = tokens.shape
    count = len(signal)
    chan = feat // kern
    part = rows // 2
    add = out_before is not None

    def kernel(word_ref, x_ref, mid_ref, gate_ref, weight_ref, gain_ref, *refs):
        signal_refs, refs = refs[:count], refs[count:]
        out_ref, stack_s, gs = refs[1:] if add else refs
        i = pl.program_id(0)
        for p in range(2):
            pl.when(i == p)(lambda: join(word_ref, signal_refs, stack_s, gs, p, 2))
        back = mm_nt(gs[...], weight_ref[:, :feat]) + mm_nt(gate_ref[...], weight_ref[:, feat:])
        hat, inverse = centered(x_ref[0].astype(f32))
        grad = mid_ref[...] + norm_back(back, hat, inverse, gain_ref[...])
        out_ref[0] = grad.astype(bf16)

    tiled = pl.BlockSpec((part, feat), lambda i: (i, 0))
    args = [words, tokens, grad_mid, grad_gate, weight, gain, *signal]
    in_specs = [
        smem(),
        along(seq, part, feat),
        tiled,
        tiled,
        fixed(weight.shape),
        fixed((feat,)),
    ] + [fixed(piece.shape) for piece in signal]
    aliases = {}
    if add:
        args.append(out_before)
        in_specs.append(pl.BlockSpec(memory_space=pl.ANY))
        aliases = {len(args) - 1: 0}
    return pl.pallas_call(
        kernel,
        grid=(2,),
        in_specs=in_specs,
        out_specs=along(seq, part, feat),
        out_shape=jax.ShapeDtypeStruct(tokens.shape, bf16),
        scratch_shapes=[
            pltpu.VMEM((kern, part, chan), bf16),
            pltpu.VMEM((part, feat), bf16),
        ],
        input_output_aliases=aliases,
        compiler_params=params(56),
        cost_estimate=cost(6),
        name="finish",
    )(*args)


def late_gradients(words, signals, normeds, gate_t, out_t, weight_t, gain, second_row, taps, kern, groups):
    rows, feat = normeds[0].shape
    counts = [len(signal) for signal in signals]
    chan = feat // kern
    pairs = groups // 2
    in_rows, out_rows = 2 * feat // groups, feat // groups
    late = (pairs, kern, late_packed + taps[0].shape[2], 128)

    def kernel(word_ref, *refs):
        signal_refs = []
        for count in counts:
            signal_refs.append(refs[:count])
            refs = refs[count:]
        normed_refs, refs = refs[: len(normeds)], refs[len(normeds) :]
        gain_ref, row_ref, refs = refs[0], refs[1], refs[2:]
        far_refs, late_refs, refs = refs[:7], refs[7:11], refs[11:]
        (stack_s, gs, s_ref), near_refs, refs = refs[:3], refs[3:10], refs[10:]
        late_s, in_sem, out_sem = refs[:4], refs[4], refs[5]
        loads = [
            pltpu.make_async_copy(far, near, in_sem.at[i])
            for i, (far, near) in enumerate(zip(far_refs, near_refs))
        ]
        for load in loads:
            load.start()
        gt_ref, ot_ref, wt_ref, tap_refs = *near_refs[:3], near_refs[3:]
        for seq, piece_refs in enumerate(signal_refs):
            join(word_ref, piece_refs, stack_s, gs)
            s = mm_tn(gs[...], normed_refs[seq][...])
            s_ref[...] = s if seq == 0 else s_ref[...] + s
        for load in loads:
            load.wait()
        first = jnp.sum(s_ref[...] * wt_ref[:feat].astype(f32), axis=0, keepdims=True)
        first += jnp.sum(
            gt_ref[...].astype(f32) * wt_ref[feat:].astype(f32), axis=0, keepdims=True
        )
        zero = jnp.zeros((2 * late_rows - in_rows - out_rows - 2, feat), f32)
        gains = jnp.concatenate([first / gain_ref[...], row_ref[...], zero], 0).astype(bf16)
        stores = []
        for to, side in ((0, word_ref[1]), (1, 1 - word_ref[1])):
            for pair in range(pairs):
                from_ref = s_ref if pair < pairs // 2 else gt_ref
                at_in = (2 * (pair % (pairs // 2)) + side) * in_rows
                at_in = pl.multiple_of(at_in, in_rows)
                at_out = pl.multiple_of((2 * pair + side) * out_rows, out_rows)
                columns = from_ref[pl.ds(at_in, in_rows), :].astype(bf16)
                values = [
                    columns[:late_rows],
                    jnp.concatenate(
                        [columns[late_rows:], ot_ref[pl.ds(at_out, out_rows), :], gains], 0
                    ),
                ]
                at = pair ^ own_pair(word_ref)
                for h in range(2):
                    place = flipped(at) if h == 0 else at
                    which = 2 * h + to
                    for z in range(kern):
                        late_pack(
                            late_s[which],
                            (place, flipped(z ^ word_ref[0])),
                            values[h][:, z * chan : (z + 1) * chan],
                        )
                    late_s[which][place, :, late_packed:] = tap_refs[which][place]
                    stores.append(
                        pltpu.make_async_copy(
                            late_s[which].at[place],
                            late_refs[which].at[place],
                            out_sem.at[which, pair],
                        )
                    )
                    stores[-1].start()
        for store in stores:
            store.wait()

    args = [words]
    for signal in signals:
        args += signal
    args += [*normeds, gain, second_row]
    far = [gate_t, out_t, weight_t, *taps]
    return pl.pallas_call(
        kernel,
        in_specs=[smem()]
        + [pl.BlockSpec(memory_space=pltpu.VMEM)] * (len(args) - 1)
        + [pl.BlockSpec(memory_space=pl.ANY)] * len(far),
        out_specs=[pl.BlockSpec(memory_space=pl.ANY)] * 4,
        out_shape=[jax.ShapeDtypeStruct(late, bf16)] * 4,
        scratch_shapes=[
            pltpu.VMEM((kern, rows, chan), bf16),
            pltpu.VMEM((rows, feat), bf16),
            pltpu.VMEM((feat, feat), f32),
        ]
        + [pltpu.VMEM(block.shape, block.dtype) for block in far]
        + [pltpu.VMEM(late, bf16)] * 4
        + [pltpu.SemaphoreType.DMA((len(far),)), pltpu.SemaphoreType.DMA((4, pairs))],
        compiler_params=pltpu.CompilerParams(vmem_limit_bytes=56 * 2**20),
        cost_estimate=cost(6),
        name="late_gradients",
    )(*args, *far)


def late_pack(ref, lead, values):
    rows = values.shape[0]
    half = (rows // 2 + 15) // 16 * 16
    ref[(*lead, slice(0, rows))] = values[:, :128]
    ref[(*lead, slice(rows, rows + half), slice(0, 64))] = values[:half, 128:]
    ref[(*lead, slice(rows, 2 * rows - half), slice(64, 128))] = values[half:, 128:]


def late_unpack(block, rows):
    half = (rows // 2 + 15) // 16 * 16
    rest = block[..., rows : rows + half, :]
    rest = jnp.concatenate([rest[..., :64], rest[..., : rows - half, 64:]], axis=-2)
    return jnp.concatenate([block[..., :rows, :], rest], axis=-1)


def swap(block, axis_name, bit):
    route = [(i, i ^ (1 << bit)) for i in range(lax.axis_size(axis_name))]
    return lax.ppermute(block, axis_name, route)


def added(block):
    return jnp.sum(block.astype(f32), axis=0)


class Folding:
    bits = ((("dp", 1), ("dp", 2)), (("dp", 2), ("dp", 1)))

    def __init__(self, first, second):
        self.rows = first[0].shape[2]
        self.rest = first[0].shape[2:]
        self.mine = [first[0], second[0]]
        self.got = [swap(first[1], "dp", 0), swap(second[1], "dp", 0)]
        self.stage = 0

    def half(self, which, side):
        left = 3 - self.stage
        shape = (2, 2**left) + self.rest
        mine = self.mine[which].reshape(shape)
        got = self.got[which].reshape(shape)
        return mine[side].astype(f32) + got[side].astype(f32)

    def step(self):
        gives = [self.half(which, 1).astype(bf16) for which in range(len(self.mine))]
        self.mine = [self.half(which, 0).astype(bf16) for which in range(len(self.mine))]
        if self.stage < 2:
            self.got = [swap(give, *self.bits[which][self.stage]) for which, give in enumerate(gives)]
        else:
            if len(gives) > 1:
                gives = [jnp.concatenate(gives, axis=-2)]
                self.mine = [jnp.concatenate(self.mine, axis=-2)]
                self.rest = (2 * self.rows, self.rest[1])
            self.got = [swap(gives[0], "kern", self.stage - 2)]
        self.stage += 1
        return gives

    def take(self, rows):
        taken = []
        for which in range(2):
            shape = (2 ** (4 - self.stage),) + self.rest
            mine, got = self.mine[which].reshape(shape), self.got[which].reshape(shape)
            taken.append(mine[:, rows:].astype(f32) + got[:, rows:].astype(f32))
            self.mine[which], self.got[which] = mine[:, :rows], got[:, :rows]
        self.rows, self.rest = rows, (rows, self.rest[1])
        return [block.astype(bf16) for block in taken]

    def hold(self, anchor):
        self.mine = after(anchor, self.mine)

    def totals(self):
        block = self.mine[0].reshape(self.rest).astype(f32) + self.got[0].reshape(self.rest).astype(f32)
        return block[: self.rows], block[self.rows :]


def after(anchor, values):
    return lax.optimization_barrier((anchor, values))[1]


def shards(
    tokens,
    cotangent,
    in_weight,
    out_weight,
    up_weight,
    down_weight,
    first_gain,
    second_gain,
    raw_taps,
    pad_lengths,
):
    seq_count, row_count, feat = tokens.shape
    width = up_weight.shape[1]
    kern = lax.axis_size("kern")
    groups = lax.axis_size("dp")
    me = lax.axis_index("kern").astype(jnp.int32)
    my_group = lax.axis_index("dp").astype(jnp.int32)
    words = jnp.stack([me, my_group % 2, my_group // 2 % 2, my_group // 4])
    local_taps = raw_taps.shape[0]
    total_taps = local_taps * kern
    chan = feat // kern
    outer = row_count * kern // inner
    share = local_taps // groups
    deep = feat // groups
    in_rows = 2 * deep
    tabs = all_tables(outer)
    seqs = range(seq_count)

    def across(pieces, sign, *anchors):
        if anchors:
            pieces = after(anchors, pieces)
        if len(pieces) == 1:
            return [spread_out(pieces[0], "kern")]
        return exchange(pieces, sign)

    def copies(block):
        return jnp.broadcast_to(block[None], (groups, *block.shape))

    def to_all(block):
        return spread_out(copies(block), "dp")

    my_taps = lax.dynamic_slice_in_dim(raw_taps, my_group * share, share, 0)
    my_taps = shrink(my_taps).astype(bf16).reshape(share, kern, chan).transpose(1, 0, 2)
    limits = total_taps - lax.dynamic_slice_in_dim(pad_lengths, me * chan, chan, 0)[None]

    my_taps = spread_out(my_taps, "kern")

    heads, arrived = [], []
    for b in seqs:
        head = project(words, b, tokens, first_gain, in_weight, kern, b > 0, b == seq_count - 1)
        words = after(head[0], words)
        heads.append(head)
        if b == 0:
            all_taps = to_all(after(head[0], my_taps))
            arrived.append(across(head[2], -1))
        else:
            hidden_back = grad_hidden(words, cotangent, down_weight)
            words = after(hidden_back, words)
            arrived.append(across(head[2], -1, *arrived, all_taps, hidden_back))

    kernel_spec = tap_spectrum(words, all_taps, limits, tabs)
    words = after(kernel_spec, words)

    convs, returned = [], []
    for b in seqs:
        conv = convolve(words, arrived[b], kern, kernel_spec, tabs, False, None, b > 0)
        words = after(conv[1], words)
        convs.append(conv)
        returned.append(across(conv[0], 1, *returned))

    slope = lax.optimization_barrier(shrink_slope(raw_taps))
    words = after(slope, words)

    mids, arrived_back = [], []
    earlier, out_tokens = None, None
    for b in seqs:
        mid, grads, pieces = feed_forward(
            words,
            b,
            tokens,
            cotangent,
            hidden_back,
            heads[b][1],
            returned[b],
            heads[b][0],
            out_weight,
            up_weight,
            down_weight,
            second_gain,
            kern,
            groups,
            True,
            earlier,
            out_tokens,
        )
        words = after(mid[3], words)
        out_tokens, second_row = mid[0], mid[3]
        earlier = [*grads, second_row]
        mids.append(mid)
        arrived_back.append(across(pieces, -1, returned[-1], *arrived_back))
    u_keep, u_give, d_keep, d_give, out_t, gate_t = grads
    u_give, d_give = after(arrived_back[:-1], (u_give, d_give))
    wide_sums = Folding((u_keep, u_give), (d_keep, d_give))

    corrs, signal_back = [], []
    for b in seqs:
        corr = convolve(
            words, arrived_back[b], kern, kernel_spec, tabs, True, convs[b][1], b > 0
        )
        words = after(corr[1], words)
        corrs.append(corr)
        if b == 0:
            steps = wide_sums.step()
            words = after(steps, words)
            signal_back.append(across(corr[0], 1, steps))
        else:
            signal_back.append(across(corr[0], 1))

    wide_sums.hold(signal_back[0])
    words = after(wide_sums.step(), words)

    def write(word_ref, taps_ref, out_refs):
        for to, side in ((0, word_ref[1]), (1, 1 - word_ref[1])):
            for pair in range(groups // 2):
                for z in range(kern):
                    start = (z * groups + 2 * pair + side) * share
                    block = taps_ref[pl.ds(pl.multiple_of(start, share), share), :]
                    at = pair ^ own_pair(word_ref)
                    for h in range(2):
                        place = (flipped(at) if h == 0 else at, flipped(z ^ word_ref[0]))
                        half = block[h * share // 2 : (h + 1) * share // 2]
                        late_pack(out_refs[2 * h + to], place, half)

    shapes = [(groups // 2, kern, share // 4 * 3, 128)] * 4
    products = [corr[1] for corr in corrs]
    grad_taps = tap_gradient(words, products, limits, tabs, shapes, write)
    words = after(grad_taps, words)
    words = after(wide_sums.step(), words)

    late = late_gradients(
        words,
        signal_back,
        [head[0] for head in heads],
        gate_t,
        out_t,
        heads[-1][3],
        first_gain,
        second_row,
        grad_taps,
        kern,
        groups,
    )

    late_sums = Folding(late[:2], late[2:])
    grad_tokens = None
    for b in seqs:
        steps = late_sums.step()
        if b == 0:
            wide_sums.hold(steps)
            wide_sums.step()
        grad_tokens = finish(
            after(steps, words),
            b,
            tokens,
            mids[b][1],
            mids[b][2],
            signal_back[b],
            in_weight,
            first_gain,
            kern,
            grad_tokens,
        )
        late_sums.hold(grad_tokens)
    taps = jnp.stack(late_sums.take(late_packed), axis=1)
    steps = late_sums.step()
    taps = [taps[flipped(r)] for r in range(kern)]
    for r in range(1, kern):
        taps[r] = lax.ppermute(taps[r], "kern", [(i, i ^ r) for i in range(kern)])
    taps = late_unpack(jnp.stack(taps), share // 2).reshape(kern, share, chan)
    taps = jnp.concatenate(
        [lax.dynamic_index_in_dim(taps, me ^ z, 0, keepdims=False) for z in range(kern)], axis=1
    )
    taps = copies(taps)
    late_sums.hold(taps)
    wide_sums.hold(late_sums.step())
    up, down = wide_sums.totals()
    grad_taps = spread_out(taps, "dp").reshape(local_taps, feat)
    grad_raw = grad_taps.astype(f32) * slope

    sum_up = jnp.concatenate(jnp.split(up, 2, axis=1), axis=0)
    sum_down = down.T
    late = jnp.concatenate([late_unpack(block, late_rows) for block in late_sums.totals()], axis=0)
    sum_in = late[:in_rows].T
    sum_out = late[in_rows : in_rows + deep].T
    return (
        out_tokens,
        grad_tokens,
        sum_in,
        sum_out,
        sum_up,
        sum_down,
        late[in_rows + deep],
        late[in_rows + deep + 1],
        grad_raw,
    )


def solution(mesh):
    placed = (
        P("dp", "kern", None),
        P("dp", "kern", None),
        P(),
        P(),
        P(),
        P(),
        P(),
        P(),
        P("kern", None),
        P(),
    )
    placed_out = (
        P("dp", "kern", None),
        P("dp", "kern", None),
        P("kern", "dp"),
        P("kern", "dp"),
        P("kern", "dp"),
        P("kern", "dp"),
        P("kern"),
        P("kern"),
        P("kern", None),
    )
    groups, kern = mesh.shape["dp"], mesh.shape["kern"]

    def layer(*arrays):
        seq_count, length, feat = arrays[0].shape
        seq_count = seq_count // groups
        width = arrays[4].shape[1]
        rows = length // kern
        tiles = (
            feat % (16 * groups) == 0
            and width % (128 * groups) == 0
            and width == groups // 2 * feat
            and groups == 8
            and kern == 4
            and rows % (2 * inner) == 0
            and 3 * feat // groups + 2 <= 2 * late_rows
            and seq_count == 2
            and feat // kern == 192
            and arrays[8].shape[0] == 64 * groups * kern
        )
        return run(shards if tiles else shards_general)(*arrays)

    def run(body):
        return jax.shard_map(
            body,
            mesh=mesh,
            in_specs=placed,
            out_specs=placed_out,
            check_vma=False,
        )

    return layer
```

```python
import math

import jax
import jax.numpy as jnp
import ml_dtypes
import numpy as np
from jax import lax
from jax.experimental import pallas as pl
from jax.experimental.pallas import tpu as pltpu
from jax.sharding import PartitionSpec as P

shrink_level = 0.003
norm_eps = 1e-05
bf16 = jnp.bfloat16
f32 = jnp.float32
inner = 128
group = 16
wide = 8


def inner_tables(outer):
    length = outer * inner
    k1 = np.arange(outer)[:, None, None]
    k2 = np.arange(inner)[None, :, None]
    n2 = np.arange(inner)[None, None, :]
    turns = (n2 * (4 * (outer * k2 + k1) + 1)) % (4 * length)
    angle = turns * (2 * math.pi / (4 * length))
    c, s = np.cos(angle), np.sin(angle)
    table = np.concatenate([np.concatenate([c, s], 2), np.concatenate([-s, c], 2)], 1)
    return table.astype(ml_dtypes.bfloat16)


def outer_tables(outer):
    k1 = np.arange(outer)[:, None]
    n1 = np.arange(outer)[None, :]
    angle = (n1 * (4 * k1 + 1)) % (4 * outer) * (2 * math.pi / (4 * outer))
    parts = np.stack([np.cos(angle), -np.sin(angle)], 1)
    table = np.einsum("kcn,ij->kcinj", parts, np.eye(group))
    table = table.reshape(outer * 2 * group, outer * group)
    return table.astype(ml_dtypes.bfloat16), table.T.astype(ml_dtypes.bfloat16)


def all_tables(outer):
    first, last = outer_tables(outer)
    tabs = {"inner": inner_tables(outer), "first": first, "last": last}
    return {key: jnp.asarray(value) for key, value in tabs.items()}


def outer_forward(x_ref, table_ref, y_ref):
    outer, _, ch = x_ref.shape

    def step(j, carry):
        rows = pl.ds(pl.multiple_of(j * group, group), group)
        x = x_ref[:, rows, :].reshape(outer * group, ch)
        y = jnp.dot(table_ref[...], x, preferred_element_type=f32).astype(bf16)
        y = y.reshape(outer, 2, group, ch)
        y_ref[:, 0, rows, :] = y[:, 0]
        y_ref[:, 1, rows, :] = y[:, 1]
        return carry

    lax.fori_loop(0, inner // group, step, 0, unroll=8)


def outer_back(w_ref, table_ref, x_ref):
    outer, _, _, ch = w_ref.shape

    def step(j, carry):
        rows = pl.ds(pl.multiple_of(j * group, group), group)
        w = w_ref[:, :, rows, :].reshape(outer * 2 * group, ch)
        x = jnp.dot(table_ref[...], w, preferred_element_type=f32)
        x_ref[:, rows, :] = x.astype(x_ref.dtype).reshape(outer, group, ch)
        return carry

    lax.fori_loop(0, inner // group, step, 0, unroll=8)


def whole(shape):
    return pl.BlockSpec(shape, lambda i: (0,) * len(shape))


def slab(*shape):
    return pl.BlockSpec((wide,) + shape, lambda i: (i,) + (0,) * len(shape))


def smem():
    return pl.BlockSpec(memory_space=pltpu.SMEM)


def params(mib):
    return pltpu.CompilerParams(
        vmem_limit_bytes=mib * 2**20, dimension_semantics=("arbitrary",)
    )


def cost(micros):
    return pl.CostEstimate(
        flops=int(micros * 8e8), bytes_accessed=int(micros * 1e6), transcendentals=0
    )


def tap_spectrum(words, taps, limits, tabs):
    groups, kern, share, ch = taps.shape
    length = groups * kern * share
    outer = length // inner

    def kernel(_, taps_ref, limit_ref, table_ref, first_ref, out_ref, x_ref, y_ref, flat_ref):
        @pl.when(pl.program_id(0) == 0)
        def _():
            for z in range(kern):
                for p in range(groups):
                    at = (z * groups + p) * share
                    flat_ref[at : at + share] = taps_ref[p, z].astype(f32)
            values = flat_ref[...]
            edge = jnp.zeros((1, ch), f32)
            below = jnp.concatenate([edge, values[:-1]], 0)
            above = jnp.concatenate([values[1:], edge], 0)
            index = lax.broadcasted_iota(jnp.int32, (length, ch), 0)
            values = jnp.where(index < limit_ref[...], (below + values + above) / 3.0, 0.0)
            x_ref[...] = values.astype(bf16).reshape(outer, inner, ch)
            outer_forward(x_ref, first_ref, y_ref)

        for i in range(wide):
            y = y_ref[pl.program_id(0) * wide + i].reshape(2 * inner, ch)
            s = jnp.dot(table_ref[i], y, preferred_element_type=f32)
            out_ref[i] = (s * (1.0 / length)).astype(bf16)

    return pl.pallas_call(
        kernel,
        grid=(outer // wide,),
        in_specs=[
            smem(),
            whole(taps.shape),
            whole((1, ch)),
            slab(2 * inner, 2 * inner),
            whole(tabs["first"].shape),
        ],
        out_specs=slab(2 * inner, ch),
        out_shape=jax.ShapeDtypeStruct((outer, 2 * inner, ch), bf16),
        scratch_shapes=[
            pltpu.VMEM((outer, inner, ch), bf16),
            pltpu.VMEM((outer, 2, inner, ch), bf16),
            pltpu.VMEM((length, ch), f32),
        ],
        compiler_params=params(56),
        cost_estimate=cost(6),
        name="tap_spectrum",
    )(words, taps, limits, tabs["inner"], tabs["first"])


def packed(rows, ch):
    if ch % 128 == 64 and rows % (2 * inner) == 0:
        return (rows // inner * (2 * ch // 128) // 2, inner, 128)
    return (rows // inner, inner, ch)


def pack(ref, lead, values, part, parts):
    rows, ch = values.shape
    blocks = rows // inner
    if ref.shape[-1] == ch:
        ref[(*lead, pl.ds(part * blocks, blocks))] = values.reshape(blocks, inner, ch)
        return
    full = ch // 128
    for j in range(full):
        at = (j * parts + part) * blocks
        lanes = values[:, j * 128 : (j + 1) * 128]
        ref[(*lead, pl.ds(at, blocks))] = lanes.reshape(blocks, inner, 128)
    rest = values[:, full * 128 :]
    half = parts * blocks // 2
    for t in range(blocks):
        at = part * blocks + t
        side, row = at // half, at % half
        ref[(*lead, full * parts * blocks + row, slice(None), slice(side * 64, side * 64 + 64))] = (
            rest[t * inner : (t + 1) * inner]
        )


def unpack(ref, lead, part, parts, ch, blocks):
    if ref.shape[-1] == ch:
        return [(0, ref[(*lead, pl.ds(part * blocks, blocks))])]
    full = ch // 128
    out = []
    for j in range(full):
        at = (j * parts + part) * blocks
        out.append((j * 128, ref[(*lead, pl.ds(at, blocks))]))
    half = parts * blocks // 2
    rest = []
    for t in range(blocks):
        at = part * blocks + t
        side, row = at // half, at % half
        rest.append(
            ref[(*lead, full * parts * blocks + row, slice(None), slice(side * 64, side * 64 + 64))]
        )
    out.append((full * 128, jnp.stack(rest)))
    return out


def owners(me_ref, refs, kern, sign):
    if len(refs) == 1 and kern > 1:
        return [(refs[0], (k,), k) for k in range(kern)]
    return [
        (ref, (), lax.rem(me_ref[0] + (k if sign > 0 else kern - k), kern))
        for k, ref in enumerate(refs)
    ]


def piece_shapes(kern, rows, ch, stacked):
    shape = packed(rows, ch)
    return [(kern, *shape)] if stacked else [shape] * kern


def place_pieces(me_ref, piece_refs, x_ref, kern):
    outer, _, ch = x_ref.shape
    blocks = outer // kern
    for ref, lead, owner in owners(me_ref, piece_refs, kern, 1):
        for at, block in unpack(ref, lead, 0, 1, ch, blocks):
            x_ref[pl.ds(owner * blocks, blocks), :, at : at + block.shape[2]] = block


def take_pieces(me_ref, x_ref, piece_refs, kern):
    outer, _, ch = x_ref.shape
    blocks = outer // kern
    for ref, lead, owner in owners(me_ref, piece_refs, kern, 1):
        pack(ref, lead, x_ref[pl.ds(owner * blocks, blocks)].reshape(blocks * inner, ch), 0, 1)


def convolve(me, pieces, kern, kernel_spec, tabs, flip, other_spec=None, stacked=False):
    count = len(pieces)
    outer, _, ch = kernel_spec.shape
    shapes = piece_shapes(kern, outer * inner // kern, ch, stacked)

    def kernel(me_ref, *refs):
        piece_refs, refs = refs[:count], refs[count:]
        spec_ref, table_ref, first_ref, last_ref = refs[:4]
        refs = refs[4:]
        if flip:
            other_ref, refs = refs[0], refs[1:]
        out_refs, refs = refs[: len(shapes)], refs[len(shapes) :]
        save_ref, x_ref, y_ref, w_ref = refs
        step = pl.program_id(0)

        @pl.when(step == 0)
        def _():
            place_pieces(me_ref, piece_refs, x_ref, kern)
            outer_forward(x_ref, first_ref, y_ref)

        for i in range(wide):
            at = step * wide + i
            y = y_ref[at].reshape(2 * inner, ch)
            s = jnp.dot(table_ref[i], y, preferred_element_type=f32)
            sr, si = s[:inner], s[inner:]
            kr = spec_ref[i, :inner].astype(f32)
            ki = spec_ref[i, inner:].astype(f32)
            if flip:
                orr = other_ref[i, :inner].astype(f32)
                oi = other_ref[i, inner:].astype(f32)
                save_ref[i, :inner] = (sr * orr + si * oi).astype(bf16)
                save_ref[i, inner:] = (si * orr - sr * oi).astype(bf16)
                zr, zi = sr * kr + si * ki, si * kr - sr * ki
            else:
                save_ref[i] = s.astype(bf16)
                zr, zi = sr * kr - si * ki, sr * ki + si * kr
            z = jnp.concatenate([zr, zi], 0).astype(bf16)
            w = mm_tn(table_ref[i], z)
            w_ref[at] = w.astype(bf16).reshape(2, inner, ch)

        @pl.when(step == pl.num_programs(0) - 1)
        def _():
            outer_back(w_ref, last_ref, x_ref)
            take_pieces(me_ref, x_ref, out_refs, kern)

    args = [me, *pieces, kernel_spec, tabs["inner"], tabs["first"], tabs["last"]]
    in_specs = [smem()] + [whole(piece.shape) for piece in pieces] + [
        slab(2 * inner, ch),
        slab(2 * inner, 2 * inner),
        whole(tabs["first"].shape),
        whole(tabs["last"].shape),
    ]
    if flip:
        args.append(other_spec)
        in_specs.append(slab(2 * inner, ch))
    outs = pl.pallas_call(
        kernel,
        grid=(outer // wide,),
        in_specs=in_specs,
        out_specs=[whole(shape) for shape in shapes] + [slab(2 * inner, ch)],
        out_shape=[jax.ShapeDtypeStruct(shape, bf16) for shape in shapes]
        + [jax.ShapeDtypeStruct((outer, 2 * inner, ch), bf16)],
        scratch_shapes=[
            pltpu.VMEM((outer, inner, ch), bf16),
            pltpu.VMEM((outer, 2, inner, ch), bf16),
            pltpu.VMEM((outer, 2, inner, ch), bf16),
        ],
        compiler_params=params(56),
        cost_estimate=cost(8),
        name="correlate" if flip else "convolve",
    )(*args)
    return list(outs[:-1]), outs[-1]


def tap_gradient(words, products, limits, tabs, out_shapes, write):
    outer, _, ch = products[0].shape
    length = outer * inner

    def kernel(word_ref, limit_ref, *refs):
        spec_refs, refs = refs[: len(products)], refs[len(products) :]
        table_ref, last_ref, refs = refs[0], refs[1], refs[2:]
        out_refs, (w_ref, x_ref, t_ref) = refs[: len(out_shapes)], refs[len(out_shapes) :]
        step = pl.program_id(0)
        for i in range(wide):
            z = spec_refs[0][i].astype(f32)
            for spec_ref in spec_refs[1:]:
                z = z + spec_ref[i].astype(f32)
            w = mm_tn(table_ref[i], (z * (1.0 / length)).astype(bf16))
            w_ref[step * wide + i] = w.astype(bf16).reshape(2, inner, ch)

        @pl.when(step == pl.num_programs(0) - 1)
        def _():
            outer_back(w_ref, last_ref, x_ref)
            taps = x_ref[...].reshape(length, ch)
            index = lax.broadcasted_iota(jnp.int32, (length, ch), 0)
            taps = jnp.where(index < limit_ref[...], taps, 0.0)
            edge = jnp.zeros((1, ch), f32)
            below = jnp.concatenate([edge, taps[:-1]], 0)
            above = jnp.concatenate([taps[1:], edge], 0)
            t_ref[...] = ((below + taps + above) / 3.0).astype(bf16)
            write(word_ref, t_ref, out_refs)

    return pl.pallas_call(
        kernel,
        grid=(outer // wide,),
        in_specs=[smem(), whole((1, ch))]
        + [slab(2 * inner, ch)] * len(products)
        + [slab(2 * inner, 2 * inner), whole(tabs["last"].shape)],
        out_specs=[whole(shape) for shape in out_shapes],
        out_shape=[jax.ShapeDtypeStruct(shape, bf16) for shape in out_shapes],
        scratch_shapes=[
            pltpu.VMEM((outer, 2, inner, ch), bf16),
            pltpu.VMEM((outer, inner, ch), f32),
            pltpu.VMEM((length, ch), bf16),
        ],
        compiler_params=params(56),
        cost_estimate=cost(5),
        name="tap_gradient",
    )(words, limits, *products, tabs["inner"], tabs["last"])


def exchange(pieces, sign):
    count = len(pieces)
    moved = [pieces[0]]
    for k in range(1, count):
        route = [(i, (i + sign * k) % count) for i in range(count)]
        moved.append(lax.ppermute(pieces[k], "kern", route))
    return moved


def spread_out(block, axis_name, groups=None):
    return lax.all_to_all(
        block, axis_name, split_axis=0, concat_axis=0, tiled=True, axis_index_groups=groups
    )


def sum_all(row):
    for axis_name in ("dp", "kern"):
        count = lax.axis_size(axis_name)
        for bit in range(count.bit_length() - 1):
            route = [(i, i ^ (1 << bit)) for i in range(count)]
            row = row + lax.ppermute(row, axis_name, route)
    return row


def padded_rows(block):
    count = lax.axis_size("kern")
    forward = [(i, i + 1) for i in range(count - 1)]
    backward = [(target, source) for source, target in forward]
    low = lax.ppermute(block[-1:], "kern", forward)
    high = lax.ppermute(block[:1], "kern", backward)
    return jnp.concatenate([low, block, high], axis=0)


def layer_norm(values, norm_gain):
    center = values - jnp.mean(values, axis=-1, keepdims=True)
    spread = jnp.mean(center * center, axis=-1, keepdims=True)
    return center * lax.rsqrt(spread + norm_eps) * norm_gain


def shrink(tap_values):
    return tap_values - shrink_level * tap_values / jnp.sqrt(
        tap_values * tap_values + shrink_level * shrink_level
    )


def shrink_slope(tap_values):
    return 1.0 - shrink_level**3 / (tap_values * tap_values + shrink_level * shrink_level) ** 1.5


def pool_three(padded):
    return (padded[:-2] + padded[1:-1] + padded[2:]) / 3.0


def dot(left, right, dims):
    return lax.dot_general(left, right, (dims, ((), ())), preferred_element_type=f32)


def shards_general(
    tokens,
    cotangent,
    in_weight,
    out_weight,
    up_weight,
    down_weight,
    first_gain,
    second_gain,
    raw_taps,
    pad_lengths,
):
    seq_count, row_count, feat = tokens.shape
    kern = lax.axis_size("kern")
    me = lax.axis_index("kern")
    me_word = me.astype(jnp.int32).reshape(1)
    groups = lax.axis_size("dp")
    local_taps = raw_taps.shape[0]
    total_taps = local_taps * kern
    chan = feat // kern
    outer = row_count * kern // inner
    blocks = row_count // inner
    tabs = all_tables(outer)

    limits = total_taps - lax.dynamic_slice_in_dim(pad_lengths, me * chan, chan, 0)[None]
    my_raw = lax.all_to_all(raw_taps, "kern", split_axis=1, concat_axis=0, tiled=True)
    kernel_spec = tap_spectrum(me_word, shrink(my_raw)[None, None], limits, tabs)

    def apart(values):
        values = values.reshape(blocks, inner, kern, chan).transpose(2, 0, 1, 3)
        return [values[(me - k) % kern] for k in range(kern)]

    def joined(pieces):
        stack = jnp.stack(pieces)
        stack = jnp.stack([stack[(me - k) % kern] for k in range(kern)])
        return stack.transpose(1, 2, 0, 3).reshape(row_count, feat)

    def one(x, cot):
        inputs = x.astype(f32)
        first_norm, first_pull = jax.vjp(layer_norm, inputs, first_gain)
        normed = first_norm.astype(bf16)
        projected = dot(normed, in_weight, ((1,), (0,)))
        gate = projected[:, feat:]
        pieces = exchange(apart(projected[:, :feat].astype(bf16)), -1)
        pieces, spectrum = convolve(me_word, pieces, kern, kernel_spec, tabs, False)
        convolved = joined(exchange(pieces, 1)).astype(f32)
        mixed = (gate * convolved).astype(bf16)
        middle = inputs + dot(mixed, out_weight, ((1,), (0,)))
        second_norm, second_pull = jax.vjp(layer_norm, middle, second_gain)
        normed_two = second_norm.astype(bf16)
        raised = dot(normed_two, up_weight, ((1,), (0,)))
        activated, gelu_pull = jax.vjp(jax.nn.gelu, raised)
        hidden = activated.astype(bf16)
        out = (middle + dot(hidden, down_weight, ((1,), (0,)))).astype(bf16)
        grad_raised = gelu_pull(dot(cot, down_weight, ((1,), (1,))))[0].astype(bf16)
        grad_mid, second_row = second_pull(dot(grad_raised, up_weight, ((1,), (1,))))
        grad_mid = cot.astype(f32) + grad_mid
        branch = grad_mid.astype(bf16)
        grad_mixed = dot(branch, out_weight, ((1,), (1,)))
        grad_gate = (grad_mixed * convolved).astype(bf16)
        pieces = exchange(apart((grad_mixed * gate).astype(bf16)), -1)
        pieces, product = convolve(me_word, pieces, kern, kernel_spec, tabs, True, spectrum)
        grad_signal = joined(exchange(pieces, 1))
        grad_projected = jnp.concatenate([grad_signal, grad_gate], axis=-1)
        grad_first, first_row = first_pull(dot(grad_projected, in_weight, ((1,), (1,))))
        weights = (
            dot(normed, grad_projected, ((0,), (0,))),
            dot(mixed, branch, ((0,), (0,))),
            dot(normed_two, grad_raised, ((0,), (0,))),
            dot(hidden, cot, ((0,), (0,))),
        )
        return out, (grad_mid + grad_first).astype(bf16), product, (first_row, second_row), weights

    ones = [one(tokens[b], cotangent[b]) for b in range(seq_count)]
    rows, weights = ones[0][3:]
    for other in ones[1:]:
        rows, weights = jax.tree.map(jnp.add, (rows, weights), other[3:])
    def write(_, taps_ref, out_refs):
        out_refs[0][...] = taps_ref[...]

    products = [item[2] for item in ones]
    shapes = [(total_taps, chan)]
    grad_taps = tap_gradient(me_word, products, limits, tabs, shapes, write)[0]
    grad_taps = lax.all_to_all(grad_taps, "kern", split_axis=0, concat_axis=1, tiled=True)
    grad_raw = lax.psum(grad_taps, "dp").astype(f32) * shrink_slope(raw_taps)
    sums = []
    for weight in weights:
        weight = lax.psum_scatter(weight.astype(bf16), "dp", scatter_dimension=1, tiled=True)
        weight = lax.psum_scatter(weight, "kern", scatter_dimension=0, tiled=True)
        sums.append(weight.astype(f32))
    gains = sum_all(jnp.stack(rows))
    gains = lax.dynamic_slice_in_dim(gains, me * chan, chan, 1)
    return (
        jnp.stack([item[0] for item in ones]),
        jnp.stack([item[1] for item in ones]),
        *sums,
        gains[0],
        gains[1],
        grad_raw,
    )


def row_mean(values):
    return jnp.mean(values, axis=-1, keepdims=True)


def centered(values):
    center = values - row_mean(values)
    inverse = lax.rsqrt(row_mean(center * center) + norm_eps)
    return center * inverse, inverse


def norm_back(grad, normed, inverse, gain):
    scaled = grad * gain
    return inverse * (scaled - row_mean(scaled) - normed * row_mean(scaled * normed))


def mm(left, right):
    return jnp.dot(left, right, preferred_element_type=f32)


def mm_nt(left, right):
    return lax.dot_general(left, right, (((1,), (1,)), ((), ())), preferred_element_type=f32)


def mm_tn(left, right):
    return lax.dot_general(left, right, (((0,), (0,)), ((), ())), preferred_element_type=f32)


def fixed(shape):
    return pl.BlockSpec(shape, lambda *_: (0,) * len(shape))


def once(shape):
    return pl.BlockSpec(
        shape, lambda *_: (0,) * len(shape), pipeline_mode=pl.Buffered(1)
    )


def along(seq, rows, feat):
    return pl.BlockSpec((1, rows, feat), lambda i: (seq, i, 0))


def cut(me_ref, values, piece_refs, stack_ref, part=0, parts=1):
    kern, rows, ch = stack_ref.shape
    if len(piece_refs) > 1:
        for k in range(kern):
            stack_ref[k] = values[:, k * ch : (k + 1) * ch]
    for ref, lead, owner in owners(me_ref, piece_refs, kern, -1):
        block = stack_ref[owner] if len(piece_refs) > 1 else values[:, owner * ch : (owner + 1) * ch]
        pack(ref, lead, block, part, parts)


def join(me_ref, piece_refs, stack_ref, out_ref, part=0, parts=1):
    kern, rows, ch = stack_ref.shape
    blocks = rows // inner
    for ref, lead, owner in owners(me_ref, piece_refs, kern, -1):
        for at, block in unpack(ref, lead, part, parts, ch, blocks):
            width = block.shape[2]
            block = block.reshape(rows, width)
            if len(piece_refs) > 1:
                stack_ref[owner, :, at : at + width] = block
            else:
                out_ref[:, owner * ch + at : owner * ch + at + width] = block
    if len(piece_refs) > 1:
        for k in range(kern):
            out_ref[:, k * ch : (k + 1) * ch] = stack_ref[k]


def project(me, seq, tokens, gain, weight, kern, stacked, turn=False):
    _, rows, feat = tokens.shape
    chan = feat // kern
    parts = 1
    tile = rows // parts
    shapes = piece_shapes(kern, rows, chan, stacked)
    turned_shape = [weight.shape[::-1]] if turn else []

    def kernel(me_ref, x_ref, gain_ref, weight_ref, *refs):
        normed_ref, gate_ref = refs[:2]
        piece_refs, stack_ref = refs[2 : 2 + len(shapes)], refs[-1]
        if turn:
            pl.when(pl.program_id(0) == 0)(lambda: put_turned(weight_ref, refs[-2]))
        hat, _ = centered(x_ref[0].astype(f32))
        normed = (hat * gain_ref[...]).astype(bf16)
        normed_ref[...] = normed
        projected = mm(normed, weight_ref[...])
        gate_ref[...] = projected[:, feat:]
        signal = projected[:, :feat].astype(bf16)
        for part in range(parts):
            pl.when(pl.program_id(0) == part)(
                lambda: cut(me_ref, signal, piece_refs, stack_ref, part, parts)
            )

    outs = pl.pallas_call(
        kernel,
        grid=(parts,),
        in_specs=[smem(), along(seq, tile, feat), fixed((feat,)), fixed(weight.shape)],
        out_specs=[
            pl.BlockSpec((tile, feat), lambda i: (i, 0)),
            pl.BlockSpec((tile, feat), lambda i: (i, 0)),
        ]
        + [fixed(shape) for shape in shapes + turned_shape],
        out_shape=[
            jax.ShapeDtypeStruct((rows, feat), bf16),
            jax.ShapeDtypeStruct((rows, feat), f32),
        ]
        + [jax.ShapeDtypeStruct(shape, bf16) for shape in shapes + turned_shape],
        scratch_shapes=[pltpu.VMEM((kern, tile, chan), bf16)],
        compiler_params=params(56),
        cost_estimate=cost(4),
        name="project",
    )(me, tokens, gain, weight)
    return outs[0], outs[1], list(outs[2 : 2 + len(shapes)]), outs[-1]


def put_turned(from_ref, to_ref):
    to_ref[...] = from_ref[...].T


def gelu_pair(raised):
    root = math.sqrt(2.0 / math.pi)
    square = raised * raised
    t = jnp.tanh(raised * (root + (root * 0.044715) * square))
    half = 0.5 + 0.5 * t
    slope = half + (0.5 * raised) * (1.0 - t * t) * (root + (3.0 * root * 0.044715) * square)
    return raised * half, slope


def own_pair(words):
    return 2 * words[3] + words[2]


def grad_hidden(words, cots, down_weight):
    seqs, rows, feat = cots.shape
    width = down_weight.shape[0]
    chunk = feat

    def kernel(_, cot_ref, down_ref, out_ref):
        out = mm_nt(cot_ref[...].reshape(seqs * rows, feat), down_ref[...])
        out_ref[...] = out.astype(bf16).reshape(seqs, rows, chunk)

    return pl.pallas_call(
        kernel,
        grid=(width // chunk,),
        in_specs=[smem(), fixed(cots.shape), pl.BlockSpec((chunk, feat), lambda i: (i, 0))],
        out_specs=pl.BlockSpec((seqs, rows, chunk), lambda i: (0, 0, i)),
        out_shape=jax.ShapeDtypeStruct((seqs, rows, width), bf16),
        compiler_params=params(56),
        cost_estimate=cost(6),
        name="grad_hidden",
    )(words, cots, down_weight)


def flipped(place):
    return 2 * (place & 1) + (place >> 1)


def feed_forward(words, seq, tokens, cots, grads, gate, conv, normed, out_weight, up_weight, down_weight, gain, kern, groups, stacked, earlier, out_before):
    seqs, rows, feat = tokens.shape
    width = up_weight.shape[1]
    count = len(conv)
    shapes = piece_shapes(kern, rows, feat // kern, stacked)
    chan = feat // kern
    pairs = groups // 2
    chunk = width // pairs
    deep = feat // groups
    half = chunk // 2
    add = earlier is not None

    def kernel(word_ref, x_ref, cot_ref, gh_ref, gate_ref, ow_ref, up_ref, down_ref, gain_ref, *refs):
        conv_refs, refs = refs[:count], refs[count:]
        if add:
            old, refs = refs[:5], refs[5:]
        far_refs, refs = refs[: len(far)], refs[len(far) :]
        ggain_ref, out_ref, mid_ref, ggate_ref = refs[:4]
        u_keep, u_give, d_keep, d_give, o_ref, g_ref = refs[4:10]
        piece_refs, refs = refs[10 : 10 + len(shapes)], refs[10 + len(shapes) :]
        stack_s, cv, mixed_s, middle_s, n2_s, acc_s, back_s, o_s, g_s = refs[:9]
        piece_s, refs = refs[9 : 9 + len(shapes)], refs[9 + len(shapes) :]
        near_refs, in_sem, out_sem = refs[: len(loaded)], refs[-2], refs[-1]
        f = pl.program_id(0)
        loads = [
            pltpu.make_async_copy(far_ref, near_ref, in_sem.at[i])
            for i, (far_ref, near_ref) in enumerate(zip(far_refs, near_refs))
        ]
        cot = cot_ref.at[0]

        @pl.when(f == 0)
        def _():
            for load in loads:
                load.start()
            join(word_ref, conv_refs, stack_s, cv)
            mixed = (gate_ref[...] * cv[...].astype(f32)).astype(bf16)
            mixed_s[...] = mixed
            middle = x_ref[0].astype(f32) + mm(mixed, ow_ref[...])
            middle_s[...] = middle
            hat, _ = centered(middle)
            n2_s[...] = (hat * gain_ref[...]).astype(bf16)
            acc_s[...] = middle
            back_s[...] = jnp.zeros_like(back_s)

        hidden, grad_raised = [], []
        for at in range(0, rows, rows // 2):
            part = slice(at, at + rows // 2)
            act, slope = gelu_pair(mm(n2_s[part], up_ref[...]))
            hidden.append(act.astype(bf16))
            grad_raised.append((gh_ref[0, part].astype(f32) * slope).astype(bf16))
        hidden = jnp.concatenate(hidden, 0)
        grad_raised = jnp.concatenate(grad_raised, 0)
        acc_s[...] += mm(hidden, down_ref[...])
        back_s[...] += mm_nt(grad_raised, up_ref[...])
        u = mm_tn(n2_s[...], grad_raised).astype(bf16)
        d = mm_tn(cot[...], hidden).astype(bf16).reshape(pairs, 2, deep, chunk)
        even = word_ref[1] == 0
        for to, u_ref, d_ref, u_old, d_old in (
            (0, u_keep, d_keep, 0, 2),
            (1, u_give, d_give, 1, 3),
        ):
            for pair in range(pairs):
                at = pair ^ own_pair(word_ref)
                part = jnp.where(even, d[pair, to], d[pair, 1 - to])
                d_ref[at, 0] = part + old[d_old][at, 0] if add else part
            uu = jnp.where(
                even,
                u[:, to * half : (to + 1) * half],
                u[:, (1 - to) * half : (2 - to) * half],
            ).reshape(kern, 2, deep, half)
            for z in range(kern):
                at = flipped(z ^ word_ref[0])
                part = jnp.concatenate([uu[z, 0], uu[z, 1]], axis=1)
                u_ref[0, at] = part + old[u_old][0, at] if add else part

        @pl.when(f == pairs - 1)
        def _():
            stores = []

            def store(near_ref, far_ref):
                stores.append(pltpu.make_async_copy(near_ref, far_ref, out_sem.at[len(stores)]))
                stores[-1].start()

            n2_s[...] = acc_s[...].astype(bf16)
            store(n2_s, out_ref.at[seq])
            hat, inverse = centered(middle_s[...])
            back = back_s[...]
            ggain = jnp.sum(back * hat, axis=0, keepdims=True)
            ggain_ref[...] = ggain + old[4][...] if add else ggain
            grad_mid = cot[...].astype(f32) + norm_back(back, hat, inverse, gain_ref[...])
            back_s[...] = grad_mid
            store(back_s, mid_ref)
            branch = grad_mid.astype(bf16)
            grad_mixed = mm_nt(branch, ow_ref[...])
            cut(word_ref, (grad_mixed * gate_ref[...]).astype(bf16), piece_s, stack_s)
            for near_ref, far_ref in zip(piece_s, piece_refs):
                store(near_ref, far_ref)
            ggate = (grad_mixed * cv[...].astype(f32)).astype(bf16)
            cv[...] = ggate
            store(cv, ggate_ref)
            for load in loads:
                load.wait()
            o = mm_tn(branch, mixed_s[...])
            o_s[...] = (o + near_refs[1][...].astype(f32) if add else o).astype(bf16)
            store(o_s, o_ref)
            g = mm_tn(ggate, near_refs[0][...])
            g_s[...] = (g + near_refs[2][...].astype(f32) if add else g).astype(bf16)
            store(g_s, g_ref)
            for item in stores:
                item.wait()

    u_spec = pl.BlockSpec((1, kern, deep, chunk), lambda f, w: (flipped(f ^ own_pair(w)), 0, 0, 0))
    d_spec = pl.BlockSpec((pairs, 1, deep, chunk), lambda f, w: (0, flipped(f ^ w[0]), 0, 0))
    anywhere = pl.BlockSpec(memory_space=pl.ANY)
    one = pl.BlockSpec((1, rows, feat), lambda f, w: (seq, 0, 0))
    args = [words, tokens, cots, grads, gate, out_weight, up_weight, down_weight, gain, *conv]
    in_specs = [
        one,
        one,
        pl.BlockSpec((1, rows, chunk), lambda f, w: (seq, 0, f)),
        once((rows, feat)),
        once(out_weight.shape),
        pl.BlockSpec((feat, chunk), lambda f, w: (0, f)),
        pl.BlockSpec((chunk, feat), lambda f, w: (f, 0)),
        fixed((feat,)),
    ] + [fixed(piece.shape) for piece in conv]
    grad_specs = [u_spec, u_spec, d_spec, d_spec]
    loaded = [normed]
    aliases = {}
    if add:
        *big_before, o_before, g_before, row_before = earlier
        args += [*big_before, row_before]
        in_specs += [*grad_specs, fixed((1, feat))]
        loaded += [o_before, g_before]
    far = list(loaded)
    if add:
        far.append(out_before)
        aliases = {len(args) + len(loaded): 1}
    args += far
    in_specs += [anywhere] * len(far)
    big = jax.ShapeDtypeStruct((pairs, kern, deep, chunk), bf16)
    outs = pl.pallas_call(
        kernel,
        grid_spec=pltpu.PrefetchScalarGridSpec(
            num_scalar_prefetch=1,
            grid=(pairs,),
            in_specs=in_specs,
            out_specs=[fixed((1, feat))]
            + [anywhere] * 3
            + grad_specs
            + [anywhere] * (2 + len(shapes)),
            scratch_shapes=[
                pltpu.VMEM((kern, rows, feat // kern), bf16),
                pltpu.VMEM((rows, feat), bf16),
                pltpu.VMEM((rows, feat), bf16),
                pltpu.VMEM((rows, feat), f32),
                pltpu.VMEM((rows, feat), bf16),
                pltpu.VMEM((rows, feat), f32),
                pltpu.VMEM((rows, feat), f32),
                pltpu.VMEM((feat, feat), bf16),
                pltpu.VMEM((feat, feat), bf16),
            ]
            + [pltpu.VMEM(shape, bf16) for shape in shapes]
            + [pltpu.VMEM(block.shape, bf16) for block in loaded]
            + [
                pltpu.SemaphoreType.DMA((len(loaded),)),
                pltpu.SemaphoreType.DMA((5 + len(shapes),)),
            ],
        ),
        out_shape=[
            jax.ShapeDtypeStruct((1, feat), f32),
            jax.ShapeDtypeStruct(tokens.shape, bf16),
            jax.ShapeDtypeStruct((rows, feat), f32),
            jax.ShapeDtypeStruct((rows, feat), bf16),
            big,
            big,
            big,
            big,
            jax.ShapeDtypeStruct((feat, feat), bf16),
            jax.ShapeDtypeStruct((feat, feat), bf16),
        ]
        + [jax.ShapeDtypeStruct(shape, bf16) for shape in shapes],
        input_output_aliases=aliases,
        compiler_params=params(56),
        cost_estimate=cost(24),
        name="feed_forward",
    )(*args)
    row, out, mid, ggate = outs[:4]
    return (out, mid, ggate, row), list(outs[4:10]), list(outs[10:])


late_rows = 144
late_packed = 224
late_free = slice(208, 224)


def finish(words, seq, tokens, grad_mid, grad_gate, signal, weight, gain, kern, out_before):
    seqs, rows, feat = tokens.shape
    count = len(signal)
    chan = feat // kern
    part = rows // 2
    add = out_before is not None

    def kernel(word_ref, x_ref, mid_ref, gate_ref, weight_ref, gain_ref, *refs):
        signal_refs, refs = refs[:count], refs[count:]
        out_ref, stack_s, gs = refs[1:] if add else refs
        i = pl.program_id(0)
        for p in range(2):
            pl.when(i == p)(lambda: join(word_ref, signal_refs, stack_s, gs, p, 2))
        back = mm_nt(gs[...], weight_ref[:, :feat]) + mm_nt(gate_ref[...], weight_ref[:, feat:])
        hat, inverse = centered(x_ref[0].astype(f32))
        grad = mid_ref[...] + norm_back(back, hat, inverse, gain_ref[...])
        out_ref[0] = grad.astype(bf16)

    tiled = pl.BlockSpec((part, feat), lambda i: (i, 0))
    args = [words, tokens, grad_mid, grad_gate, weight, gain, *signal]
    in_specs = [
        smem(),
        along(seq, part, feat),
        tiled,
        tiled,
        fixed(weight.shape),
        fixed((feat,)),
    ] + [fixed(piece.shape) for piece in signal]
    aliases = {}
    if add:
        args.append(out_before)
        in_specs.append(pl.BlockSpec(memory_space=pl.ANY))
        aliases = {len(args) - 1: 0}
    return pl.pallas_call(
        kernel,
        grid=(2,),
        in_specs=in_specs,
        out_specs=along(seq, part, feat),
        out_shape=jax.ShapeDtypeStruct(tokens.shape, bf16),
        scratch_shapes=[
            pltpu.VMEM((kern, part, chan), bf16),
            pltpu.VMEM((part, feat), bf16),
        ],
        input_output_aliases=aliases,
        compiler_params=params(56),
        cost_estimate=cost(6),
        name="finish",
    )(*args)


def late_gradients(words, signals, normeds, gate_t, out_t, weight_t, gain, second_row, taps, kern, groups):
    rows, feat = normeds[0].shape
    counts = [len(signal) for signal in signals]
    chan = feat // kern
    pairs = groups // 2
    in_rows, out_rows = 2 * feat // groups, feat // groups
    late = (pairs, kern, late_packed + taps[0].shape[2], 128)

    def kernel(word_ref, *refs):
        signal_refs = []
        for count in counts:
            signal_refs.append(refs[:count])
            refs = refs[count:]
        normed_refs, refs = refs[: len(normeds)], refs[len(normeds) :]
        gain_ref, row_ref, refs = refs[0], refs[1], refs[2:]
        far_refs, late_refs, refs = refs[:7], refs[7:11], refs[11:]
        (stack_s, gs, s_ref), near_refs, refs = refs[:3], refs[3:10], refs[10:]
        late_s, in_sem, out_sem = refs[:4], refs[4], refs[5]
        loads = [
            pltpu.make_async_copy(far, near, in_sem.at[i])
            for i, (far, near) in enumerate(zip(far_refs, near_refs))
        ]
        for load in loads:
            load.start()
        gt_ref, ot_ref, wt_ref, tap_refs = *near_refs[:3], near_refs[3:]
        for seq, piece_refs in enumerate(signal_refs):
            join(word_ref, piece_refs, stack_s, gs)
            s = mm_tn(gs[...], normed_refs[seq][...])
            s_ref[...] = s if seq == 0 else s_ref[...] + s
        for load in loads:
            load.wait()
        first = jnp.sum(s_ref[...] * wt_ref[:feat].astype(f32), axis=0, keepdims=True)
        first += jnp.sum(
            gt_ref[...].astype(f32) * wt_ref[feat:].astype(f32), axis=0, keepdims=True
        )
        rows_gain = (first / gain_ref[...], row_ref[...])
        gains = []
        for z in range(kern):
            lanes = [
                row[:, at : at + 64]
                for row in rows_gain
                for at in range(z * chan, (z + 1) * chan, 64)
            ]
            lanes.append(jnp.zeros((16 - len(lanes), 64), f32))
            gains.append(jnp.concatenate(lanes, 0).astype(bf16))
        stores = []
        for to, side in ((0, word_ref[1]), (1, 1 - word_ref[1])):
            for pair in range(pairs):
                from_ref = s_ref if pair < pairs // 2 else gt_ref
                at_in = (2 * (pair % (pairs // 2)) + side) * in_rows
                at_in = pl.multiple_of(at_in, in_rows)
                at_out = pl.multiple_of((2 * pair + side) * out_rows, out_rows)
                columns = from_ref[pl.ds(at_in, in_rows), :].astype(bf16)
                values = [
                    columns[:late_rows],
                    jnp.concatenate(
                        [columns[late_rows:], ot_ref[pl.ds(at_out, out_rows), :]], 0
                    ),
                ]
                at = pair ^ own_pair(word_ref)
                for h in range(2):
                    place = flipped(at) if h == 0 else at
                    which = 2 * h + to
                    for z in range(kern):
                        late_pack(
                            late_s[which],
                            (place, flipped(z ^ word_ref[0])),
                            values[h][:, z * chan : (z + 1) * chan],
                        )
                        near = flipped(z ^ word_ref[0])
                        late_s[which][place, near, late_free, 64:] = gains[z]
                    late_s[which][place, :, late_packed:] = tap_refs[which][place]
                    stores.append(
                        pltpu.make_async_copy(
                            late_s[which].at[place],
                            late_refs[which].at[place],
                            out_sem.at[which, pair],
                        )
                    )
                    stores[-1].start()
        for store in stores:
            store.wait()

    args = [words]
    for signal in signals:
        args += signal
    args += [*normeds, gain, second_row]
    far = [gate_t, out_t, weight_t, *taps]
    return pl.pallas_call(
        kernel,
        in_specs=[smem()]
        + [pl.BlockSpec(memory_space=pltpu.VMEM)] * (len(args) - 1)
        + [pl.BlockSpec(memory_space=pl.ANY)] * len(far),
        out_specs=[pl.BlockSpec(memory_space=pl.ANY)] * 4,
        out_shape=[jax.ShapeDtypeStruct(late, bf16)] * 4,
        scratch_shapes=[
            pltpu.VMEM((kern, rows, chan), bf16),
            pltpu.VMEM((rows, feat), bf16),
            pltpu.VMEM((feat, feat), f32),
        ]
        + [pltpu.VMEM(block.shape, block.dtype) for block in far]
        + [pltpu.VMEM(late, bf16)] * 4
        + [pltpu.SemaphoreType.DMA((len(far),)), pltpu.SemaphoreType.DMA((4, pairs))],
        compiler_params=pltpu.CompilerParams(vmem_limit_bytes=56 * 2**20),
        cost_estimate=cost(6),
        name="late_gradients",
    )(*args, *far)


def late_pack(ref, lead, values):
    rows = values.shape[0]
    half = (rows // 2 + 15) // 16 * 16
    ref[(*lead, slice(0, rows))] = values[:, :128]
    ref[(*lead, slice(rows, rows + half), slice(0, 64))] = values[:half, 128:]
    ref[(*lead, slice(rows, 2 * rows - half), slice(64, 128))] = values[half:, 128:]


def late_unpack(block, rows):
    half = (rows // 2 + 15) // 16 * 16
    rest = block[..., rows : rows + half, :]
    rest = jnp.concatenate([rest[..., :64], rest[..., : rows - half, 64:]], axis=-2)
    return jnp.concatenate([block[..., :rows, :], rest], axis=-1)


def swap(block, axis_name, bit):
    route = [(i, i ^ (1 << bit)) for i in range(lax.axis_size(axis_name))]
    return lax.ppermute(block, axis_name, route)


def added(block):
    return jnp.sum(block.astype(f32), axis=0)


class Folding:
    bits = ((("dp", 1), ("dp", 2)), (("dp", 2), ("dp", 1)))

    def __init__(self, first, second):
        self.rows = first[0].shape[2]
        self.rest = first[0].shape[2:]
        self.mine = [first[0], second[0]]
        self.got = [swap(first[1], "dp", 0), swap(second[1], "dp", 0)]
        self.stage = 0

    def half(self, which, side):
        left = 3 - self.stage
        shape = (2, 2**left) + self.rest
        mine = self.mine[which].reshape(shape)
        got = self.got[which].reshape(shape)
        return mine[side].astype(f32) + got[side].astype(f32)

    def step(self):
        gives = [self.half(which, 1).astype(bf16) for which in range(len(self.mine))]
        self.mine = [self.half(which, 0).astype(bf16) for which in range(len(self.mine))]
        if self.stage < 2:
            self.got = [swap(give, *self.bits[which][self.stage]) for which, give in enumerate(gives)]
        else:
            if len(gives) > 1:
                gives = [jnp.concatenate(gives, axis=-2)]
                self.mine = [jnp.concatenate(self.mine, axis=-2)]
                self.rest = (2 * self.rows, self.rest[1])
            self.got = [swap(gives[0], "kern", self.stage - 2)]
        self.stage += 1
        return gives

    def take(self, rows):
        taken = []
        for which in range(2):
            shape = (2 ** (4 - self.stage),) + self.rest
            mine, got = self.mine[which].reshape(shape), self.got[which].reshape(shape)
            taken.append(mine[:, rows:].astype(f32) + got[:, rows:].astype(f32))
            self.mine[which], self.got[which] = mine[:, :rows], got[:, :rows]
        self.rows, self.rest = rows, (rows, self.rest[1])
        return [block.astype(bf16) for block in taken]

    def hold(self, anchor):
        self.mine = after(anchor, self.mine)

    def totals(self):
        block = self.mine[0].reshape(self.rest).astype(f32) + self.got[0].reshape(self.rest).astype(f32)
        return block[: self.rows], block[self.rows :]


def after(anchor, values):
    return lax.optimization_barrier((anchor, values))[1]


def shards(
    tokens,
    cotangent,
    in_weight,
    out_weight,
    up_weight,
    down_weight,
    first_gain,
    second_gain,
    raw_taps,
    pad_lengths,
):
    seq_count, row_count, feat = tokens.shape
    width = up_weight.shape[1]
    kern = lax.axis_size("kern")
    groups = lax.axis_size("dp")
    me = lax.axis_index("kern").astype(jnp.int32)
    my_group = lax.axis_index("dp").astype(jnp.int32)
    words = jnp.stack([me, my_group % 2, my_group // 2 % 2, my_group // 4])
    local_taps = raw_taps.shape[0]
    total_taps = local_taps * kern
    chan = feat // kern
    outer = row_count * kern // inner
    share = local_taps // groups
    deep = feat // groups
    in_rows = 2 * deep
    tabs = all_tables(outer)
    seqs = range(seq_count)

    def across(pieces, sign, *anchors):
        if anchors:
            pieces = after(anchors, pieces)
        if len(pieces) == 1:
            return [spread_out(pieces[0], "kern")]
        return exchange(pieces, sign)

    def copies(block):
        return jnp.broadcast_to(block[None], (groups, *block.shape))

    def to_all(block):
        return spread_out(copies(block), "dp")

    my_taps = lax.dynamic_slice_in_dim(raw_taps, my_group * share, share, 0)
    my_taps = shrink(my_taps).astype(bf16).reshape(share, kern, chan).transpose(1, 0, 2)
    limits = total_taps - lax.dynamic_slice_in_dim(pad_lengths, me * chan, chan, 0)[None]

    my_taps = spread_out(my_taps, "kern")

    heads, arrived = [], []
    for b in seqs:
        head = project(words, b, tokens, first_gain, in_weight, kern, b > 0, b == seq_count - 1)
        words = after(head[0], words)
        heads.append(head)
        if b == 0:
            all_taps = to_all(after(head[0], my_taps))
            arrived.append(across(head[2], -1))
        else:
            hidden_back = grad_hidden(words, cotangent, down_weight)
            words = after(hidden_back, words)
            arrived.append(across(head[2], -1, *arrived, all_taps, hidden_back))

    kernel_spec = tap_spectrum(words, all_taps, limits, tabs)
    words = after(kernel_spec, words)

    convs, returned = [], []
    for b in seqs:
        conv = convolve(words, arrived[b], kern, kernel_spec, tabs, False, None, b > 0)
        words = after(conv[1], words)
        convs.append(conv)
        returned.append(across(conv[0], 1, *returned))

    slope = lax.optimization_barrier(shrink_slope(raw_taps))
    words = after(slope, words)

    mids, arrived_back = [], []
    earlier, out_tokens = None, None
    for b in seqs:
        mid, grads, pieces = feed_forward(
            words,
            b,
            tokens,
            cotangent,
            hidden_back,
            heads[b][1],
            returned[b],
            heads[b][0],
            out_weight,
            up_weight,
            down_weight,
            second_gain,
            kern,
            groups,
            True,
            earlier,
            out_tokens,
        )
        words = after(mid[3], words)
        out_tokens, second_row = mid[0], mid[3]
        earlier = [*grads, second_row]
        mids.append(mid)
        arrived_back.append(across(pieces, -1, returned[-1], *arrived_back))
    u_keep, u_give, d_keep, d_give, out_t, gate_t = grads
    u_give, d_give = after(arrived_back[:-1], (u_give, d_give))
    wide_sums = Folding((u_keep, u_give), (d_keep, d_give))

    corrs, signal_back = [], []
    for b in seqs:
        corr = convolve(
            words, arrived_back[b], kern, kernel_spec, tabs, True, convs[b][1], b > 0
        )
        words = after(corr[1], words)
        corrs.append(corr)
        if b == 0:
            steps = wide_sums.step()
            words = after(steps, words)
            signal_back.append(across(corr[0], 1, steps))
        else:
            signal_back.append(across(corr[0], 1))

    wide_sums.hold(signal_back[0])
    words = after(wide_sums.step(), words)

    def write(word_ref, taps_ref, out_refs):
        for to, side in ((0, word_ref[1]), (1, 1 - word_ref[1])):
            for pair in range(groups // 2):
                for z in range(kern):
                    start = (z * groups + 2 * pair + side) * share
                    block = taps_ref[pl.ds(pl.multiple_of(start, share), share), :]
                    at = pair ^ own_pair(word_ref)
                    for h in range(2):
                        place = (flipped(at) if h == 0 else at, flipped(z ^ word_ref[0]))
                        half = block[h * share // 2 : (h + 1) * share // 2]
                        late_pack(out_refs[2 * h + to], place, half)

    shapes = [(groups // 2, kern, share // 4 * 3, 128)] * 4
    products = [corr[1] for corr in corrs]
    grad_taps = tap_gradient(words, products, limits, tabs, shapes, write)
    words = after(grad_taps, words)
    words = after(wide_sums.step(), words)

    late = late_gradients(
        words,
        signal_back,
        [head[0] for head in heads],
        gate_t,
        out_t,
        heads[-1][3],
        first_gain,
        second_row,
        grad_taps,
        kern,
        groups,
    )

    late_sums = Folding(late[:2], late[2:])
    grad_tokens = None
    for b in seqs:
        steps = late_sums.step()
        if b == 0:
            wide_sums.hold(steps)
            wide_sums.step()
        grad_tokens = finish(
            after(steps, words),
            b,
            tokens,
            mids[b][1],
            mids[b][2],
            signal_back[b],
            in_weight,
            first_gain,
            kern,
            grad_tokens,
        )
        late_sums.hold(grad_tokens)
    taps = jnp.stack(late_sums.take(late_packed), axis=1)
    steps = late_sums.step()
    taps = [taps[flipped(r)] for r in range(kern)]
    for r in range(1, kern):
        taps[r] = lax.ppermute(taps[r], "kern", [(i, i ^ r) for i in range(kern)])
    taps = late_unpack(jnp.stack(taps), share // 2).reshape(kern, share, chan)
    taps = jnp.concatenate(
        [lax.dynamic_index_in_dim(taps, me ^ z, 0, keepdims=False) for z in range(kern)], axis=1
    )
    taps = copies(taps)
    late_sums.hold(taps)
    wide_sums.hold(late_sums.step())
    up, down = wide_sums.totals()
    grad_taps = spread_out(taps, "dp").reshape(local_taps, feat)
    grad_raw = grad_taps.astype(f32) * slope

    sum_up = jnp.concatenate(jnp.split(up, 2, axis=1), axis=0)
    sum_down = down.T
    late = late_sums.totals()
    gains = late[1][late_free, 64:][: 2 * chan // 64].reshape(2, chan)
    late = jnp.concatenate([late_unpack(block, late_rows) for block in late], axis=0)
    sum_in = late[:in_rows].T
    sum_out = late[in_rows : in_rows + deep].T
    return (
        out_tokens,
        grad_tokens,
        sum_in,
        sum_out,
        sum_up,
        sum_down,
        gains[0],
        gains[1],
        grad_raw,
    )


def solution(mesh):
    placed = (
        P("dp", "kern", None),
        P("dp", "kern", None),
        P(),
        P(),
        P(),
        P(),
        P(),
        P(),
        P("kern", None),
        P(),
    )
    placed_out = (
        P("dp", "kern", None),
        P("dp", "kern", None),
        P("kern", "dp"),
        P("kern", "dp"),
        P("kern", "dp"),
        P("kern", "dp"),
        P("kern"),
        P("kern"),
        P("kern", None),
    )
    groups, kern = mesh.shape["dp"], mesh.shape["kern"]

    def layer(*arrays):
        seq_count, length, feat = arrays[0].shape
        seq_count = seq_count // groups
        width = arrays[4].shape[1]
        rows = length // kern
        tiles = (
            feat % (16 * groups) == 0
            and width % (128 * groups) == 0
            and width == groups // 2 * feat
            and groups == 8
            and kern == 4
            and rows % (2 * inner) == 0
            and 3 * feat // groups == 2 * late_rows
            and seq_count == 2
            and feat // kern == 192
            and arrays[8].shape[0] == 64 * groups * kern
        )
        return run(shards if tiles else shards_general)(*arrays)

    def run(body):
        return jax.shard_map(
            body,
            mesh=mesh,
            in_specs=placed,
            out_specs=placed_out,
            check_vma=False,
        )

    return layer
```

```python
import math

import jax
import jax.numpy as jnp
import ml_dtypes
import numpy as np
from jax import lax
from jax.experimental import pallas as pl
from jax.experimental.pallas import tpu as pltpu
from jax.sharding import PartitionSpec as P

shrink_level = 0.003
norm_eps = 1e-05
bf16 = jnp.bfloat16
f32 = jnp.float32
inner = 128
group = 16
wide = 8


def inner_tables(outer):
    length = outer * inner
    k1 = np.arange(outer)[:, None, None]
    k2 = np.arange(inner)[None, :, None]
    n2 = np.arange(inner)[None, None, :]
    turns = (n2 * (4 * (outer * k2 + k1) + 1)) % (4 * length)
    angle = turns * (2 * math.pi / (4 * length))
    c, s = np.cos(angle), np.sin(angle)
    table = np.concatenate([np.concatenate([c, s], 2), np.concatenate([-s, c], 2)], 1)
    return table.astype(ml_dtypes.bfloat16)


def outer_tables(outer):
    k1 = np.arange(outer)[:, None]
    n1 = np.arange(outer)[None, :]
    angle = (n1 * (4 * k1 + 1)) % (4 * outer) * (2 * math.pi / (4 * outer))
    parts = np.stack([np.cos(angle), -np.sin(angle)], 1)
    table = np.einsum("kcn,ij->kcinj", parts, np.eye(group))
    table = table.reshape(outer * 2 * group, outer * group)
    return table.astype(ml_dtypes.bfloat16), table.T.astype(ml_dtypes.bfloat16)


def all_tables(outer):
    first, last = outer_tables(outer)
    tabs = {"inner": inner_tables(outer), "first": first, "last": last}
    return {key: jnp.asarray(value) for key, value in tabs.items()}


def outer_forward(x_ref, table_ref, y_ref):
    outer, _, ch = x_ref.shape

    def step(j, carry):
        rows = pl.ds(pl.multiple_of(j * group, group), group)
        x = x_ref[:, rows, :].reshape(outer * group, ch)
        y = jnp.dot(table_ref[...], x, preferred_element_type=f32).astype(bf16)
        y = y.reshape(outer, 2, group, ch)
        y_ref[:, 0, rows, :] = y[:, 0]
        y_ref[:, 1, rows, :] = y[:, 1]
        return carry

    lax.fori_loop(0, inner // group, step, 0, unroll=8)


def outer_back(w_ref, table_ref, x_ref):
    outer, _, _, ch = w_ref.shape

    def step(j, carry):
        rows = pl.ds(pl.multiple_of(j * group, group), group)
        w = w_ref[:, :, rows, :].reshape(outer * 2 * group, ch)
        x = jnp.dot(table_ref[...], w, preferred_element_type=f32)
        x_ref[:, rows, :] = x.astype(x_ref.dtype).reshape(outer, group, ch)
        return carry

    lax.fori_loop(0, inner // group, step, 0, unroll=8)


def whole(shape):
    return pl.BlockSpec(shape, lambda i: (0,) * len(shape))


def slab(*shape):
    return pl.BlockSpec((wide,) + shape, lambda i: (i,) + (0,) * len(shape))


def smem():
    return pl.BlockSpec(memory_space=pltpu.SMEM)


def params(mib):
    return pltpu.CompilerParams(
        vmem_limit_bytes=mib * 2**20, dimension_semantics=("arbitrary",)
    )


def cost(micros):
    return pl.CostEstimate(
        flops=int(micros * 8e8), bytes_accessed=int(micros * 1e6), transcendentals=0
    )


def tap_spectrum(words, taps, limits, tabs):
    groups, kern, share, ch = taps.shape
    length = groups * kern * share
    outer = length // inner

    def kernel(_, taps_ref, limit_ref, table_ref, first_ref, out_ref, x_ref, y_ref, flat_ref):
        @pl.when(pl.program_id(0) == 0)
        def _():
            for z in range(kern):
                for p in range(groups):
                    at = (z * groups + p) * share
                    flat_ref[at : at + share] = taps_ref[p, z].astype(f32)
            values = flat_ref[...]
            edge = jnp.zeros((1, ch), f32)
            below = jnp.concatenate([edge, values[:-1]], 0)
            above = jnp.concatenate([values[1:], edge], 0)
            index = lax.broadcasted_iota(jnp.int32, (length, ch), 0)
            values = jnp.where(index < limit_ref[...], (below + values + above) / 3.0, 0.0)
            x_ref[...] = values.astype(bf16).reshape(outer, inner, ch)
            outer_forward(x_ref, first_ref, y_ref)

        for i in range(wide):
            y = y_ref[pl.program_id(0) * wide + i].reshape(2 * inner, ch)
            s = jnp.dot(table_ref[i], y, preferred_element_type=f32)
            out_ref[i] = (s * (1.0 / length)).astype(bf16)

    return pl.pallas_call(
        kernel,
        grid=(outer // wide,),
        in_specs=[
            smem(),
            whole(taps.shape),
            whole((1, ch)),
            slab(2 * inner, 2 * inner),
            whole(tabs["first"].shape),
        ],
        out_specs=slab(2 * inner, ch),
        out_shape=jax.ShapeDtypeStruct((outer, 2 * inner, ch), bf16),
        scratch_shapes=[
            pltpu.VMEM((outer, inner, ch), bf16),
            pltpu.VMEM((outer, 2, inner, ch), bf16),
            pltpu.VMEM((length, ch), f32),
        ],
        compiler_params=params(56),
        cost_estimate=cost(6),
        name="tap_spectrum",
    )(words, taps, limits, tabs["inner"], tabs["first"])


def packed(rows, ch):
    if ch % 128 == 64 and rows % (2 * inner) == 0:
        return (rows // inner * (2 * ch // 128) // 2, inner, 128)
    return (rows // inner, inner, ch)


def pack(ref, lead, values, part, parts):
    rows, ch = values.shape
    blocks = rows // inner
    if ref.shape[-1] == ch:
        ref[(*lead, pl.ds(part * blocks, blocks))] = values.reshape(blocks, inner, ch)
        return
    full = ch // 128
    for j in range(full):
        at = (j * parts + part) * blocks
        lanes = values[:, j * 128 : (j + 1) * 128]
        ref[(*lead, pl.ds(at, blocks))] = lanes.reshape(blocks, inner, 128)
    rest = values[:, full * 128 :]
    half = parts * blocks // 2
    for t in range(blocks):
        at = part * blocks + t
        side, row = at // half, at % half
        ref[(*lead, full * parts * blocks + row, slice(None), slice(side * 64, side * 64 + 64))] = (
            rest[t * inner : (t + 1) * inner]
        )


def unpack(ref, lead, part, parts, ch, blocks):
    if ref.shape[-1] == ch:
        return [(0, ref[(*lead, pl.ds(part * blocks, blocks))])]
    full = ch // 128
    out = []
    for j in range(full):
        at = (j * parts + part) * blocks
        out.append((j * 128, ref[(*lead, pl.ds(at, blocks))]))
    half = parts * blocks // 2
    rest = []
    for t in range(blocks):
        at = part * blocks + t
        side, row = at // half, at % half
        rest.append(
            ref[(*lead, full * parts * blocks + row, slice(None), slice(side * 64, side * 64 + 64))]
        )
    out.append((full * 128, jnp.stack(rest)))
    return out


def owners(me_ref, refs, kern, sign):
    if len(refs) == 1 and kern > 1:
        return [(refs[0], (k,), k) for k in range(kern)]
    return [
        (ref, (), lax.rem(me_ref[0] + (k if sign > 0 else kern - k), kern))
        for k, ref in enumerate(refs)
    ]


def piece_shapes(kern, rows, ch, stacked):
    shape = packed(rows, ch)
    return [(kern, *shape)] if stacked else [shape] * kern


def place_pieces(me_ref, piece_refs, x_ref, kern):
    outer, _, ch = x_ref.shape
    blocks = outer // kern
    for ref, lead, owner in owners(me_ref, piece_refs, kern, 1):
        for at, block in unpack(ref, lead, 0, 1, ch, blocks):
            x_ref[pl.ds(owner * blocks, blocks), :, at : at + block.shape[2]] = block


def take_pieces(me_ref, x_ref, piece_refs, kern):
    outer, _, ch = x_ref.shape
    blocks = outer // kern
    for ref, lead, owner in owners(me_ref, piece_refs, kern, 1):
        pack(ref, lead, x_ref[pl.ds(owner * blocks, blocks)].reshape(blocks * inner, ch), 0, 1)


def convolve(me, pieces, kern, kernel_spec, tabs, flip, other_spec=None, stacked=False):
    count = len(pieces)
    outer, _, ch = kernel_spec.shape
    shapes = piece_shapes(kern, outer * inner // kern, ch, stacked)

    far = [kernel_spec, tabs["inner"]] + ([other_spec] if flip else [])
    chunks = outer // wide

    def kernel(me_ref, *refs):
        piece_refs, refs = refs[:count], refs[count:]
        first_ref, last_ref, refs = refs[0], refs[1], refs[2:]
        far_refs, refs = refs[: len(far)], refs[len(far) :]
        out_refs, refs = refs[: len(shapes)], refs[len(shapes) :]
        save_ref, x_ref, y_ref, w_ref, saved = refs[:5]
        near_refs, in_sem, out_sem = refs[5 : 5 + len(far)], refs[-2], refs[-1]

        def loads(c):
            part = pl.ds(c * wide, wide)
            return [
                pltpu.make_async_copy(from_ref.at[part], to_ref.at[part], in_sem.at[c, i])
                for i, (from_ref, to_ref) in enumerate(zip(far_refs, near_refs))
            ]

        def store(c):
            part = pl.ds(c * wide, wide)
            return pltpu.make_async_copy(saved.at[part], save_ref.at[part], out_sem.at[c])

        for c in range(chunks):
            for load in loads(c):
                load.start()
        place_pieces(me_ref, piece_refs, x_ref, kern)
        outer_forward(x_ref, first_ref, y_ref)
        spec_ref, table_ref = near_refs[:2]

        def some(c, carry):
            for load in loads(c):
                load.wait()
            for i in range(wide):
                at = c * wide + i
                y = y_ref[at].reshape(2 * inner, ch)
                s = jnp.dot(table_ref[at], y, preferred_element_type=f32)
                sr, si = s[:inner], s[inner:]
                kr = spec_ref[at, :inner].astype(f32)
                ki = spec_ref[at, inner:].astype(f32)
                if flip:
                    orr = near_refs[2][at, :inner].astype(f32)
                    oi = near_refs[2][at, inner:].astype(f32)
                    saved[at, :inner] = (sr * orr + si * oi).astype(bf16)
                    saved[at, inner:] = (si * orr - sr * oi).astype(bf16)
                    zr, zi = sr * kr + si * ki, si * kr - sr * ki
                else:
                    saved[at] = s.astype(bf16)
                    zr, zi = sr * kr - si * ki, sr * ki + si * kr
                z = jnp.concatenate([zr, zi], 0).astype(bf16)
                w = mm_tn(table_ref[at], z)
                w_ref[at] = w.astype(bf16).reshape(2, inner, ch)
            store(c).start()
            return carry

        lax.fori_loop(0, chunks, some, 0, unroll=True)
        outer_back(w_ref, last_ref, x_ref)
        take_pieces(me_ref, x_ref, out_refs, kern)
        for c in range(chunks):
            store(c).wait()

    vmem, anywhere = pl.BlockSpec(memory_space=pltpu.VMEM), pl.BlockSpec(memory_space=pl.ANY)
    spectrum = (outer, 2 * inner, ch)
    outs = pl.pallas_call(
        kernel,
        in_specs=[smem()] + [vmem] * (count + 2) + [anywhere] * len(far),
        out_specs=[vmem] * len(shapes) + [anywhere],
        out_shape=[jax.ShapeDtypeStruct(shape, bf16) for shape in shapes]
        + [jax.ShapeDtypeStruct(spectrum, bf16)],
        scratch_shapes=[
            pltpu.VMEM((outer, inner, ch), bf16),
            pltpu.VMEM((outer, 2, inner, ch), bf16),
            pltpu.VMEM((outer, 2, inner, ch), bf16),
            pltpu.VMEM(spectrum, bf16),
        ]
        + [pltpu.VMEM(block.shape, bf16) for block in far]
        + [pltpu.SemaphoreType.DMA((chunks, len(far))), pltpu.SemaphoreType.DMA((chunks,))],
        compiler_params=pltpu.CompilerParams(vmem_limit_bytes=56 * 2**20),
        cost_estimate=cost(8),
        name="correlate" if flip else "convolve",
    )(me, *pieces, tabs["first"], tabs["last"], *far)
    return list(outs[:-1]), outs[-1]


def tap_gradient(words, products, limits, tabs, out_shapes, write):
    outer, _, ch = products[0].shape
    length = outer * inner

    def kernel(word_ref, limit_ref, *refs):
        spec_refs, refs = refs[: len(products)], refs[len(products) :]
        table_ref, last_ref, refs = refs[0], refs[1], refs[2:]
        out_refs, (w_ref, x_ref, t_ref) = refs[: len(out_shapes)], refs[len(out_shapes) :]
        step = pl.program_id(0)
        for i in range(wide):
            z = spec_refs[0][i].astype(f32)
            for spec_ref in spec_refs[1:]:
                z = z + spec_ref[i].astype(f32)
            w = mm_tn(table_ref[i], (z * (1.0 / length)).astype(bf16))
            w_ref[step * wide + i] = w.astype(bf16).reshape(2, inner, ch)

        @pl.when(step == pl.num_programs(0) - 1)
        def _():
            outer_back(w_ref, last_ref, x_ref)
            taps = x_ref[...].reshape(length, ch)
            index = lax.broadcasted_iota(jnp.int32, (length, ch), 0)
            taps = jnp.where(index < limit_ref[...], taps, 0.0)
            edge = jnp.zeros((1, ch), f32)
            below = jnp.concatenate([edge, taps[:-1]], 0)
            above = jnp.concatenate([taps[1:], edge], 0)
            t_ref[...] = ((below + taps + above) / 3.0).astype(bf16)
            write(word_ref, t_ref, out_refs)

    return pl.pallas_call(
        kernel,
        grid=(outer // wide,),
        in_specs=[smem(), whole((1, ch))]
        + [slab(2 * inner, ch)] * len(products)
        + [slab(2 * inner, 2 * inner), whole(tabs["last"].shape)],
        out_specs=[whole(shape) for shape in out_shapes],
        out_shape=[jax.ShapeDtypeStruct(shape, bf16) for shape in out_shapes],
        scratch_shapes=[
            pltpu.VMEM((outer, 2, inner, ch), bf16),
            pltpu.VMEM((outer, inner, ch), f32),
            pltpu.VMEM((length, ch), bf16),
        ],
        compiler_params=params(56),
        cost_estimate=cost(5),
        name="tap_gradient",
    )(words, limits, *products, tabs["inner"], tabs["last"])


def exchange(pieces, sign):
    count = len(pieces)
    moved = [pieces[0]]
    for k in range(1, count):
        route = [(i, (i + sign * k) % count) for i in range(count)]
        moved.append(lax.ppermute(pieces[k], "kern", route))
    return moved


def spread_out(block, axis_name, groups=None):
    return lax.all_to_all(
        block, axis_name, split_axis=0, concat_axis=0, tiled=True, axis_index_groups=groups
    )


def sum_all(row):
    for axis_name in ("dp", "kern"):
        count = lax.axis_size(axis_name)
        for bit in range(count.bit_length() - 1):
            route = [(i, i ^ (1 << bit)) for i in range(count)]
            row = row + lax.ppermute(row, axis_name, route)
    return row


def padded_rows(block):
    count = lax.axis_size("kern")
    forward = [(i, i + 1) for i in range(count - 1)]
    backward = [(target, source) for source, target in forward]
    low = lax.ppermute(block[-1:], "kern", forward)
    high = lax.ppermute(block[:1], "kern", backward)
    return jnp.concatenate([low, block, high], axis=0)


def layer_norm(values, norm_gain):
    center = values - jnp.mean(values, axis=-1, keepdims=True)
    spread = jnp.mean(center * center, axis=-1, keepdims=True)
    return center * lax.rsqrt(spread + norm_eps) * norm_gain


def shrink(tap_values):
    return tap_values - shrink_level * tap_values / jnp.sqrt(
        tap_values * tap_values + shrink_level * shrink_level
    )


def shrink_slope(tap_values):
    return 1.0 - shrink_level**3 / (tap_values * tap_values + shrink_level * shrink_level) ** 1.5


def pool_three(padded):
    return (padded[:-2] + padded[1:-1] + padded[2:]) / 3.0


def dot(left, right, dims):
    return lax.dot_general(left, right, (dims, ((), ())), preferred_element_type=f32)


def shards_general(
    tokens,
    cotangent,
    in_weight,
    out_weight,
    up_weight,
    down_weight,
    first_gain,
    second_gain,
    raw_taps,
    pad_lengths,
):
    seq_count, row_count, feat = tokens.shape
    kern = lax.axis_size("kern")
    me = lax.axis_index("kern")
    me_word = me.astype(jnp.int32).reshape(1)
    groups = lax.axis_size("dp")
    local_taps = raw_taps.shape[0]
    total_taps = local_taps * kern
    chan = feat // kern
    outer = row_count * kern // inner
    blocks = row_count // inner
    tabs = all_tables(outer)

    limits = total_taps - lax.dynamic_slice_in_dim(pad_lengths, me * chan, chan, 0)[None]
    my_raw = lax.all_to_all(raw_taps, "kern", split_axis=1, concat_axis=0, tiled=True)
    kernel_spec = tap_spectrum(me_word, shrink(my_raw)[None, None], limits, tabs)

    def apart(values):
        values = values.reshape(blocks, inner, kern, chan).transpose(2, 0, 1, 3)
        return [values[(me - k) % kern] for k in range(kern)]

    def joined(pieces):
        stack = jnp.stack(pieces)
        stack = jnp.stack([stack[(me - k) % kern] for k in range(kern)])
        return stack.transpose(1, 2, 0, 3).reshape(row_count, feat)

    def one(x, cot):
        inputs = x.astype(f32)
        first_norm, first_pull = jax.vjp(layer_norm, inputs, first_gain)
        normed = first_norm.astype(bf16)
        projected = dot(normed, in_weight, ((1,), (0,)))
        gate = projected[:, feat:]
        pieces = exchange(apart(projected[:, :feat].astype(bf16)), -1)
        pieces, spectrum = convolve(me_word, pieces, kern, kernel_spec, tabs, False)
        convolved = joined(exchange(pieces, 1)).astype(f32)
        mixed = (gate * convolved).astype(bf16)
        middle = inputs + dot(mixed, out_weight, ((1,), (0,)))
        second_norm, second_pull = jax.vjp(layer_norm, middle, second_gain)
        normed_two = second_norm.astype(bf16)
        raised = dot(normed_two, up_weight, ((1,), (0,)))
        activated, gelu_pull = jax.vjp(jax.nn.gelu, raised)
        hidden = activated.astype(bf16)
        out = (middle + dot(hidden, down_weight, ((1,), (0,)))).astype(bf16)
        grad_raised = gelu_pull(dot(cot, down_weight, ((1,), (1,))))[0].astype(bf16)
        grad_mid, second_row = second_pull(dot(grad_raised, up_weight, ((1,), (1,))))
        grad_mid = cot.astype(f32) + grad_mid
        branch = grad_mid.astype(bf16)
        grad_mixed = dot(branch, out_weight, ((1,), (1,)))
        grad_gate = (grad_mixed * convolved).astype(bf16)
        pieces = exchange(apart((grad_mixed * gate).astype(bf16)), -1)
        pieces, product = convolve(me_word, pieces, kern, kernel_spec, tabs, True, spectrum)
        grad_signal = joined(exchange(pieces, 1))
        grad_projected = jnp.concatenate([grad_signal, grad_gate], axis=-1)
        grad_first, first_row = first_pull(dot(grad_projected, in_weight, ((1,), (1,))))
        weights = (
            dot(normed, grad_projected, ((0,), (0,))),
            dot(mixed, branch, ((0,), (0,))),
            dot(normed_two, grad_raised, ((0,), (0,))),
            dot(hidden, cot, ((0,), (0,))),
        )
        return out, (grad_mid + grad_first).astype(bf16), product, (first_row, second_row), weights

    ones = [one(tokens[b], cotangent[b]) for b in range(seq_count)]
    rows, weights = ones[0][3:]
    for other in ones[1:]:
        rows, weights = jax.tree.map(jnp.add, (rows, weights), other[3:])
    def write(_, taps_ref, out_refs):
        out_refs[0][...] = taps_ref[...]

    products = [item[2] for item in ones]
    shapes = [(total_taps, chan)]
    grad_taps = tap_gradient(me_word, products, limits, tabs, shapes, write)[0]
    grad_taps = lax.all_to_all(grad_taps, "kern", split_axis=0, concat_axis=1, tiled=True)
    grad_raw = lax.psum(grad_taps, "dp").astype(f32) * shrink_slope(raw_taps)
    sums = []
    for weight in weights:
        weight = lax.psum_scatter(weight.astype(bf16), "dp", scatter_dimension=1, tiled=True)
        weight = lax.psum_scatter(weight, "kern", scatter_dimension=0, tiled=True)
        sums.append(weight.astype(f32))
    gains = sum_all(jnp.stack(rows))
    gains = lax.dynamic_slice_in_dim(gains, me * chan, chan, 1)
    return (
        jnp.stack([item[0] for item in ones]),
        jnp.stack([item[1] for item in ones]),
        *sums,
        gains[0],
        gains[1],
        grad_raw,
    )


def row_mean(values):
    return jnp.mean(values, axis=-1, keepdims=True)


def centered(values):
    center = values - row_mean(values)
    inverse = lax.rsqrt(row_mean(center * center) + norm_eps)
    return center * inverse, inverse


def norm_back(grad, normed, inverse, gain):
    scaled = grad * gain
    return inverse * (scaled - row_mean(scaled) - normed * row_mean(scaled * normed))


def mm(left, right):
    return jnp.dot(left, right, preferred_element_type=f32)


def mm_nt(left, right):
    return lax.dot_general(left, right, (((1,), (1,)), ((), ())), preferred_element_type=f32)


def mm_tn(left, right):
    return lax.dot_general(left, right, (((0,), (0,)), ((), ())), preferred_element_type=f32)


def fixed(shape):
    return pl.BlockSpec(shape, lambda *_: (0,) * len(shape))


def once(shape):
    return pl.BlockSpec(
        shape, lambda *_: (0,) * len(shape), pipeline_mode=pl.Buffered(1)
    )


def along(seq, rows, feat):
    return pl.BlockSpec((1, rows, feat), lambda i: (seq, i, 0))


def cut(me_ref, values, piece_refs, stack_ref, part=0, parts=1):
    kern, rows, ch = stack_ref.shape
    if len(piece_refs) > 1:
        for k in range(kern):
            stack_ref[k] = values[:, k * ch : (k + 1) * ch]
    for ref, lead, owner in owners(me_ref, piece_refs, kern, -1):
        block = stack_ref[owner] if len(piece_refs) > 1 else values[:, owner * ch : (owner + 1) * ch]
        pack(ref, lead, block, part, parts)


def join(me_ref, piece_refs, stack_ref, out_ref, part=0, parts=1):
    kern, rows, ch = stack_ref.shape
    blocks = rows // inner
    for ref, lead, owner in owners(me_ref, piece_refs, kern, -1):
        for at, block in unpack(ref, lead, part, parts, ch, blocks):
            width = block.shape[2]
            block = block.reshape(rows, width)
            if len(piece_refs) > 1:
                stack_ref[owner, :, at : at + width] = block
            else:
                out_ref[:, owner * ch + at : owner * ch + at + width] = block
    if len(piece_refs) > 1:
        for k in range(kern):
            out_ref[:, k * ch : (k + 1) * ch] = stack_ref[k]


def project(me, seq, tokens, gain, weight, kern, stacked, turn=False):
    _, rows, feat = tokens.shape
    chan = feat // kern
    parts = 1
    tile = rows // parts
    shapes = piece_shapes(kern, rows, chan, stacked)
    turned_shape = [weight.shape[::-1]] if turn else []

    def kernel(me_ref, x_ref, gain_ref, weight_ref, *refs):
        normed_ref, gate_ref = refs[:2]
        piece_refs, stack_ref = refs[2 : 2 + len(shapes)], refs[-1]
        if turn:
            pl.when(pl.program_id(0) == 0)(lambda: put_turned(weight_ref, refs[-2]))
        hat, _ = centered(x_ref[0].astype(f32))
        normed = (hat * gain_ref[...]).astype(bf16)
        normed_ref[...] = normed
        projected = mm(normed, weight_ref[...])
        gate_ref[...] = projected[:, feat:]
        signal = projected[:, :feat].astype(bf16)
        for part in range(parts):
            pl.when(pl.program_id(0) == part)(
                lambda: cut(me_ref, signal, piece_refs, stack_ref, part, parts)
            )

    outs = pl.pallas_call(
        kernel,
        grid=(parts,),
        in_specs=[smem(), along(seq, tile, feat), fixed((feat,)), fixed(weight.shape)],
        out_specs=[
            pl.BlockSpec((tile, feat), lambda i: (i, 0)),
            pl.BlockSpec((tile, feat), lambda i: (i, 0)),
        ]
        + [fixed(shape) for shape in shapes + turned_shape],
        out_shape=[
            jax.ShapeDtypeStruct((rows, feat), bf16),
            jax.ShapeDtypeStruct((rows, feat), f32),
        ]
        + [jax.ShapeDtypeStruct(shape, bf16) for shape in shapes + turned_shape],
        scratch_shapes=[pltpu.VMEM((kern, tile, chan), bf16)],
        compiler_params=params(56),
        cost_estimate=cost(4),
        name="project",
    )(me, tokens, gain, weight)
    return outs[0], outs[1], list(outs[2 : 2 + len(shapes)]), outs[-1]


def put_turned(from_ref, to_ref):
    to_ref[...] = from_ref[...].T


def gelu_pair(raised):
    root = math.sqrt(2.0 / math.pi)
    square = raised * raised
    t = jnp.tanh(raised * (root + (root * 0.044715) * square))
    half = 0.5 + 0.5 * t
    slope = half + (0.5 * raised) * (1.0 - t * t) * (root + (3.0 * root * 0.044715) * square)
    return raised * half, slope


def own_pair(words):
    return 2 * words[3] + words[2]


def grad_hidden(words, cots, down_weight):
    seqs, rows, feat = cots.shape
    width = down_weight.shape[0]
    chunk = feat

    def kernel(_, cot_ref, down_ref, out_ref):
        out = mm_nt(cot_ref[...].reshape(seqs * rows, feat), down_ref[...])
        out_ref[...] = out.astype(bf16).reshape(seqs, rows, chunk)

    return pl.pallas_call(
        kernel,
        grid=(width // chunk,),
        in_specs=[smem(), fixed(cots.shape), pl.BlockSpec((chunk, feat), lambda i: (i, 0))],
        out_specs=pl.BlockSpec((seqs, rows, chunk), lambda i: (0, 0, i)),
        out_shape=jax.ShapeDtypeStruct((seqs, rows, width), bf16),
        compiler_params=params(56),
        cost_estimate=cost(6),
        name="grad_hidden",
    )(words, cots, down_weight)


def flipped(place):
    return 2 * (place & 1) + (place >> 1)


def feed_forward(words, seq, tokens, cots, grads, gate, conv, normed, out_weight, up_weight, down_weight, gain, kern, groups, stacked, earlier, out_before):
    seqs, rows, feat = tokens.shape
    width = up_weight.shape[1]
    count = len(conv)
    shapes = piece_shapes(kern, rows, feat // kern, stacked)
    chan = feat // kern
    pairs = groups // 2
    chunk = width // pairs
    deep = feat // groups
    half = chunk // 2
    add = earlier is not None

    def kernel(word_ref, x_ref, cot_ref, gh_ref, gate_ref, ow_ref, up_ref, down_ref, gain_ref, *refs):
        conv_refs, refs = refs[:count], refs[count:]
        if add:
            old, refs = refs[:5], refs[5:]
        far_refs, refs = refs[: len(far)], refs[len(far) :]
        ggain_ref, out_ref, mid_ref, ggate_ref = refs[:4]
        u_keep, u_give, d_keep, d_give, o_ref, g_ref = refs[4:10]
        piece_refs, refs = refs[10 : 10 + len(shapes)], refs[10 + len(shapes) :]
        stack_s, cv, mixed_s, middle_s, n2_s, acc_s, back_s, o_s, g_s = refs[:9]
        piece_s, refs = refs[9 : 9 + len(shapes)], refs[9 + len(shapes) :]
        near_refs, in_sem, out_sem = refs[: len(loaded)], refs[-2], refs[-1]
        f = pl.program_id(0)
        loads = [
            pltpu.make_async_copy(far_ref, near_ref, in_sem.at[i])
            for i, (far_ref, near_ref) in enumerate(zip(far_refs, near_refs))
        ]
        cot = cot_ref.at[0]

        @pl.when(f == 0)
        def _():
            for load in loads:
                load.start()
            join(word_ref, conv_refs, stack_s, cv)
            mixed = (gate_ref[...] * cv[...].astype(f32)).astype(bf16)
            mixed_s[...] = mixed
            middle = x_ref[0].astype(f32) + mm(mixed, ow_ref[...])
            middle_s[...] = middle
            hat, _ = centered(middle)
            n2_s[...] = (hat * gain_ref[...]).astype(bf16)
            acc_s[...] = middle
            back_s[...] = jnp.zeros_like(back_s)

        hidden, grad_raised = [], []
        for at in range(0, rows, rows // 2):
            part = slice(at, at + rows // 2)
            act, slope = gelu_pair(mm(n2_s[part], up_ref[...]))
            hidden.append(act.astype(bf16))
            grad_raised.append((gh_ref[0, part].astype(f32) * slope).astype(bf16))
        hidden = jnp.concatenate(hidden, 0)
        grad_raised = jnp.concatenate(grad_raised, 0)
        acc_s[...] += mm(hidden, down_ref[...])
        back_s[...] += mm_nt(grad_raised, up_ref[...])
        u = mm_tn(n2_s[...], grad_raised).astype(bf16)
        d = mm_tn(cot[...], hidden).astype(bf16).reshape(pairs, 2, deep, chunk)
        even = word_ref[1] == 0
        for to, u_ref, d_ref, u_old, d_old in (
            (0, u_keep, d_keep, 0, 2),
            (1, u_give, d_give, 1, 3),
        ):
            for pair in range(pairs):
                at = pair ^ own_pair(word_ref)
                part = jnp.where(even, d[pair, to], d[pair, 1 - to])
                d_ref[at, 0] = part + old[d_old][at, 0] if add else part
            uu = jnp.where(
                even,
                u[:, to * half : (to + 1) * half],
                u[:, (1 - to) * half : (2 - to) * half],
            ).reshape(kern, 2, deep, half)
            for z in range(kern):
                at = flipped(z ^ word_ref[0])
                part = jnp.concatenate([uu[z, 0], uu[z, 1]], axis=1)
                u_ref[0, at] = part + old[u_old][0, at] if add else part

        @pl.when(f == pairs - 1)
        def _():
            stores = []

            def store(near_ref, far_ref):
                stores.append(pltpu.make_async_copy(near_ref, far_ref, out_sem.at[len(stores)]))
                stores[-1].start()

            n2_s[...] = acc_s[...].astype(bf16)
            store(n2_s, out_ref.at[seq])
            hat, inverse = centered(middle_s[...])
            back = back_s[...]
            ggain = jnp.sum(back * hat, axis=0, keepdims=True)
            ggain_ref[...] = ggain + old[4][...] if add else ggain
            grad_mid = cot[...].astype(f32) + norm_back(back, hat, inverse, gain_ref[...])
            back_s[...] = grad_mid
            store(back_s, mid_ref)
            branch = grad_mid.astype(bf16)
            grad_mixed = mm_nt(branch, ow_ref[...])
            cut(word_ref, (grad_mixed * gate_ref[...]).astype(bf16), piece_s, stack_s)
            for near_ref, far_ref in zip(piece_s, piece_refs):
                store(near_ref, far_ref)
            ggate = (grad_mixed * cv[...].astype(f32)).astype(bf16)
            cv[...] = ggate
            store(cv, ggate_ref)
            for load in loads:
                load.wait()
            o = mm_tn(branch, mixed_s[...])
            o_s[...] = (o + near_refs[1][...].astype(f32) if add else o).astype(bf16)
            store(o_s, o_ref)
            g = mm_tn(ggate, near_refs[0][...])
            g_s[...] = (g + near_refs[2][...].astype(f32) if add else g).astype(bf16)
            store(g_s, g_ref)
            for item in stores:
                item.wait()

    u_spec = pl.BlockSpec((1, kern, deep, chunk), lambda f, w: (flipped(f ^ own_pair(w)), 0, 0, 0))
    d_spec = pl.BlockSpec((pairs, 1, deep, chunk), lambda f, w: (0, flipped(f ^ w[0]), 0, 0))
    anywhere = pl.BlockSpec(memory_space=pl.ANY)
    one = pl.BlockSpec((1, rows, feat), lambda f, w: (seq, 0, 0))
    args = [words, tokens, cots, grads, gate, out_weight, up_weight, down_weight, gain, *conv]
    in_specs = [
        one,
        one,
        pl.BlockSpec((1, rows, chunk), lambda f, w: (seq, 0, f)),
        once((rows, feat)),
        once(out_weight.shape),
        pl.BlockSpec((feat, chunk), lambda f, w: (0, f)),
        pl.BlockSpec((chunk, feat), lambda f, w: (f, 0)),
        fixed((feat,)),
    ] + [fixed(piece.shape) for piece in conv]
    grad_specs = [u_spec, u_spec, d_spec, d_spec]
    loaded = [normed]
    aliases = {}
    if add:
        *big_before, o_before, g_before, row_before = earlier
        args += [*big_before, row_before]
        in_specs += [*grad_specs, fixed((1, feat))]
        loaded += [o_before, g_before]
    far = list(loaded)
    if add:
        far.append(out_before)
        aliases = {len(args) + len(loaded): 1}
    args += far
    in_specs += [anywhere] * len(far)
    big = jax.ShapeDtypeStruct((pairs, kern, deep, chunk), bf16)
    outs = pl.pallas_call(
        kernel,
        grid_spec=pltpu.PrefetchScalarGridSpec(
            num_scalar_prefetch=1,
            grid=(pairs,),
            in_specs=in_specs,
            out_specs=[fixed((1, feat))]
            + [anywhere] * 3
            + grad_specs
            + [anywhere] * (2 + len(shapes)),
            scratch_shapes=[
                pltpu.VMEM((kern, rows, feat // kern), bf16),
                pltpu.VMEM((rows, feat), bf16),
                pltpu.VMEM((rows, feat), bf16),
                pltpu.VMEM((rows, feat), f32),
                pltpu.VMEM((rows, feat), bf16),
                pltpu.VMEM((rows, feat), f32),
                pltpu.VMEM((rows, feat), f32),
                pltpu.VMEM((feat, feat), bf16),
                pltpu.VMEM((feat, feat), bf16),
            ]
            + [pltpu.VMEM(shape, bf16) for shape in shapes]
            + [pltpu.VMEM(block.shape, bf16) for block in loaded]
            + [
                pltpu.SemaphoreType.DMA((len(loaded),)),
                pltpu.SemaphoreType.DMA((5 + len(shapes),)),
            ],
        ),
        out_shape=[
            jax.ShapeDtypeStruct((1, feat), f32),
            jax.ShapeDtypeStruct(tokens.shape, bf16),
            jax.ShapeDtypeStruct((rows, feat), f32),
            jax.ShapeDtypeStruct((rows, feat), bf16),
            big,
            big,
            big,
            big,
            jax.ShapeDtypeStruct((feat, feat), bf16),
            jax.ShapeDtypeStruct((feat, feat), bf16),
        ]
        + [jax.ShapeDtypeStruct(shape, bf16) for shape in shapes],
        input_output_aliases=aliases,
        compiler_params=params(56),
        cost_estimate=cost(24),
        name="feed_forward",
    )(*args)
    row, out, mid, ggate = outs[:4]
    return (out, mid, ggate, row), list(outs[4:10]), list(outs[10:])


late_rows = 144
late_packed = 224
late_free = slice(208, 224)


def finish(words, seq, tokens, grad_mid, grad_gate, signal, weight, gain, kern, out_before):
    seqs, rows, feat = tokens.shape
    count = len(signal)
    chan = feat // kern
    part = rows // 2
    add = out_before is not None

    def kernel(word_ref, x_ref, mid_ref, gate_ref, weight_ref, gain_ref, *refs):
        signal_refs, refs = refs[:count], refs[count:]
        out_ref, stack_s, gs = refs[1:] if add else refs
        i = pl.program_id(0)
        for p in range(2):
            pl.when(i == p)(lambda: join(word_ref, signal_refs, stack_s, gs, p, 2))
        back = mm_nt(gs[...], weight_ref[:, :feat]) + mm_nt(gate_ref[...], weight_ref[:, feat:])
        hat, inverse = centered(x_ref[0].astype(f32))
        grad = mid_ref[...] + norm_back(back, hat, inverse, gain_ref[...])
        out_ref[0] = grad.astype(bf16)

    tiled = pl.BlockSpec((part, feat), lambda i: (i, 0))
    args = [words, tokens, grad_mid, grad_gate, weight, gain, *signal]
    in_specs = [
        smem(),
        along(seq, part, feat),
        tiled,
        tiled,
        fixed(weight.shape),
        fixed((feat,)),
    ] + [fixed(piece.shape) for piece in signal]
    aliases = {}
    if add:
        args.append(out_before)
        in_specs.append(pl.BlockSpec(memory_space=pl.ANY))
        aliases = {len(args) - 1: 0}
    return pl.pallas_call(
        kernel,
        grid=(2,),
        in_specs=in_specs,
        out_specs=along(seq, part, feat),
        out_shape=jax.ShapeDtypeStruct(tokens.shape, bf16),
        scratch_shapes=[
            pltpu.VMEM((kern, part, chan), bf16),
            pltpu.VMEM((part, feat), bf16),
        ],
        input_output_aliases=aliases,
        compiler_params=params(56),
        cost_estimate=cost(6),
        name="finish",
    )(*args)


def late_gradients(words, signals, normeds, gate_t, out_t, weight_t, gain, second_row, taps, kern, groups):
    rows, feat = normeds[0].shape
    counts = [len(signal) for signal in signals]
    chan = feat // kern
    pairs = groups // 2
    in_rows, out_rows = 2 * feat // groups, feat // groups
    late = (pairs, kern, late_packed + taps[0].shape[2], 128)

    def kernel(word_ref, *refs):
        signal_refs = []
        for count in counts:
            signal_refs.append(refs[:count])
            refs = refs[count:]
        normed_refs, refs = refs[: len(normeds)], refs[len(normeds) :]
        gain_ref, row_ref, refs = refs[0], refs[1], refs[2:]
        far_refs, late_refs, refs = refs[:7], refs[7:11], refs[11:]
        (stack_s, gs, s_ref), near_refs, refs = refs[:3], refs[3:10], refs[10:]
        late_s, in_sem, out_sem = refs[:4], refs[4], refs[5]
        loads = [
            pltpu.make_async_copy(far, near, in_sem.at[i])
            for i, (far, near) in enumerate(zip(far_refs, near_refs))
        ]
        for load in loads:
            load.start()
        gt_ref, ot_ref, wt_ref, tap_refs = *near_refs[:3], near_refs[3:]
        for seq, piece_refs in enumerate(signal_refs):
            join(word_ref, piece_refs, stack_s, gs)
            s = mm_tn(gs[...], normed_refs[seq][...])
            s_ref[...] = s if seq == 0 else s_ref[...] + s
        for load in loads:
            load.wait()
        first = jnp.sum(s_ref[...] * wt_ref[:feat].astype(f32), axis=0, keepdims=True)
        first += jnp.sum(
            gt_ref[...].astype(f32) * wt_ref[feat:].astype(f32), axis=0, keepdims=True
        )
        rows_gain = (first / gain_ref[...], row_ref[...])
        gains = []
        for z in range(kern):
            lanes = [
                row[:, at : at + 64]
                for row in rows_gain
                for at in range(z * chan, (z + 1) * chan, 64)
            ]
            lanes.append(jnp.zeros((16 - len(lanes), 64), f32))
            gains.append(jnp.concatenate(lanes, 0).astype(bf16))
        stores = []
        for to, side in ((0, word_ref[1]), (1, 1 - word_ref[1])):
            for pair in range(pairs):
                from_ref = s_ref if pair < pairs // 2 else gt_ref
                at_in = (2 * (pair % (pairs // 2)) + side) * in_rows
                at_in = pl.multiple_of(at_in, in_rows)
                at_out = pl.multiple_of((2 * pair + side) * out_rows, out_rows)
                columns = from_ref[pl.ds(at_in, in_rows), :].astype(bf16)
                values = [
                    columns[:late_rows],
                    jnp.concatenate(
                        [columns[late_rows:], ot_ref[pl.ds(at_out, out_rows), :]], 0
                    ),
                ]
                at = pair ^ own_pair(word_ref)
                for h in range(2):
                    place = flipped(at) if h == 0 else at
                    which = 2 * h + to
                    for z in range(kern):
                        late_pack(
                            late_s[which],
                            (place, flipped(z ^ word_ref[0])),
                            values[h][:, z * chan : (z + 1) * chan],
                        )
                        near = flipped(z ^ word_ref[0])
                        late_s[which][place, near, late_free, 64:] = gains[z]
                    late_s[which][place, :, late_packed:] = tap_refs[which][place]
                    stores.append(
                        pltpu.make_async_copy(
                            late_s[which].at[place],
                            late_refs[which].at[place],
                            out_sem.at[which, pair],
                        )
                    )
                    stores[-1].start()
        for store in stores:
            store.wait()

    args = [words]
    for signal in signals:
        args += signal
    args += [*normeds, gain, second_row]
    far = [gate_t, out_t, weight_t, *taps]
    return pl.pallas_call(
        kernel,
        in_specs=[smem()]
        + [pl.BlockSpec(memory_space=pltpu.VMEM)] * (len(args) - 1)
        + [pl.BlockSpec(memory_space=pl.ANY)] * len(far),
        out_specs=[pl.BlockSpec(memory_space=pl.ANY)] * 4,
        out_shape=[jax.ShapeDtypeStruct(late, bf16)] * 4,
        scratch_shapes=[
            pltpu.VMEM((kern, rows, chan), bf16),
            pltpu.VMEM((rows, feat), bf16),
            pltpu.VMEM((feat, feat), f32),
        ]
        + [pltpu.VMEM(block.shape, block.dtype) for block in far]
        + [pltpu.VMEM(late, bf16)] * 4
        + [pltpu.SemaphoreType.DMA((len(far),)), pltpu.SemaphoreType.DMA((4, pairs))],
        compiler_params=pltpu.CompilerParams(vmem_limit_bytes=56 * 2**20),
        cost_estimate=cost(6),
        name="late_gradients",
    )(*args, *far)


def late_pack(ref, lead, values):
    rows = values.shape[0]
    half = (rows // 2 + 15) // 16 * 16
    ref[(*lead, slice(0, rows))] = values[:, :128]
    ref[(*lead, slice(rows, rows + half), slice(0, 64))] = values[:half, 128:]
    ref[(*lead, slice(rows, 2 * rows - half), slice(64, 128))] = values[half:, 128:]


def late_unpack(block, rows):
    half = (rows // 2 + 15) // 16 * 16
    rest = block[..., rows : rows + half, :]
    rest = jnp.concatenate([rest[..., :64], rest[..., : rows - half, 64:]], axis=-2)
    return jnp.concatenate([block[..., :rows, :], rest], axis=-1)


def swap(block, axis_name, bit):
    route = [(i, i ^ (1 << bit)) for i in range(lax.axis_size(axis_name))]
    return lax.ppermute(block, axis_name, route)


def added(block):
    return jnp.sum(block.astype(f32), axis=0)


class Folding:
    bits = ((("dp", 1), ("dp", 2)), (("dp", 2), ("dp", 1)))

    def __init__(self, first, second):
        self.rows = first[0].shape[2]
        self.rest = first[0].shape[2:]
        self.mine = [first[0], second[0]]
        self.got = [swap(first[1], "dp", 0), swap(second[1], "dp", 0)]
        self.stage = 0

    def half(self, which, side):
        left = 3 - self.stage
        shape = (2, 2**left) + self.rest
        mine = self.mine[which].reshape(shape)
        got = self.got[which].reshape(shape)
        return mine[side].astype(f32) + got[side].astype(f32)

    def step(self):
        gives = [self.half(which, 1).astype(bf16) for which in range(len(self.mine))]
        self.mine = [self.half(which, 0).astype(bf16) for which in range(len(self.mine))]
        if self.stage < 2:
            self.got = [swap(give, *self.bits[which][self.stage]) for which, give in enumerate(gives)]
        else:
            if len(gives) > 1:
                gives = [jnp.concatenate(gives, axis=-2)]
                self.mine = [jnp.concatenate(self.mine, axis=-2)]
                self.rest = (2 * self.rows, self.rest[1])
            self.got = [swap(gives[0], "kern", self.stage - 2)]
        self.stage += 1
        return gives

    def take(self, rows):
        taken = []
        for which in range(2):
            shape = (2 ** (4 - self.stage),) + self.rest
            mine, got = self.mine[which].reshape(shape), self.got[which].reshape(shape)
            taken.append(mine[:, rows:].astype(f32) + got[:, rows:].astype(f32))
            self.mine[which], self.got[which] = mine[:, :rows], got[:, :rows]
        self.rows, self.rest = rows, (rows, self.rest[1])
        return [block.astype(bf16) for block in taken]

    def hold(self, anchor):
        self.mine = after(anchor, self.mine)

    def totals(self):
        block = self.mine[0].reshape(self.rest).astype(f32) + self.got[0].reshape(self.rest).astype(f32)
        return block[: self.rows], block[self.rows :]


def after(anchor, values):
    return lax.optimization_barrier((anchor, values))[1]


def shards(
    tokens,
    cotangent,
    in_weight,
    out_weight,
    up_weight,
    down_weight,
    first_gain,
    second_gain,
    raw_taps,
    pad_lengths,
):
    seq_count, row_count, feat = tokens.shape
    width = up_weight.shape[1]
    kern = lax.axis_size("kern")
    groups = lax.axis_size("dp")
    me = lax.axis_index("kern").astype(jnp.int32)
    my_group = lax.axis_index("dp").astype(jnp.int32)
    words = jnp.stack([me, my_group % 2, my_group // 2 % 2, my_group // 4])
    local_taps = raw_taps.shape[0]
    total_taps = local_taps * kern
    chan = feat // kern
    outer = row_count * kern // inner
    share = local_taps // groups
    deep = feat // groups
    in_rows = 2 * deep
    tabs = all_tables(outer)
    seqs = range(seq_count)

    def across(pieces, sign, *anchors):
        if anchors:
            pieces = after(anchors, pieces)
        if len(pieces) == 1:
            return [spread_out(pieces[0], "kern")]
        return exchange(pieces, sign)

    def copies(block):
        return jnp.broadcast_to(block[None], (groups, *block.shape))

    def to_all(block):
        return spread_out(copies(block), "dp")

    my_taps = lax.dynamic_slice_in_dim(raw_taps, my_group * share, share, 0)
    my_taps = shrink(my_taps).astype(bf16).reshape(share, kern, chan).transpose(1, 0, 2)
    limits = total_taps - lax.dynamic_slice_in_dim(pad_lengths, me * chan, chan, 0)[None]

    my_taps = spread_out(my_taps, "kern")

    heads, arrived = [], []
    for b in seqs:
        head = project(words, b, tokens, first_gain, in_weight, kern, b > 0, b == seq_count - 1)
        words = after(head[0], words)
        heads.append(head)
        if b == 0:
            all_taps = to_all(after(head[0], my_taps))
            arrived.append(across(head[2], -1))
        else:
            hidden_back = grad_hidden(words, cotangent, down_weight)
            words = after(hidden_back, words)
            arrived.append(across(head[2], -1, *arrived, all_taps, hidden_back))

    kernel_spec = tap_spectrum(words, all_taps, limits, tabs)
    words = after(kernel_spec, words)

    convs, returned = [], []
    for b in seqs:
        conv = convolve(words, arrived[b], kern, kernel_spec, tabs, False, None, b > 0)
        words = after(conv[1], words)
        convs.append(conv)
        returned.append(across(conv[0], 1, *returned))

    slope = lax.optimization_barrier(shrink_slope(raw_taps))
    words = after(slope, words)

    mids, arrived_back = [], []
    earlier, out_tokens = None, None
    for b in seqs:
        mid, grads, pieces = feed_forward(
            words,
            b,
            tokens,
            cotangent,
            hidden_back,
            heads[b][1],
            returned[b],
            heads[b][0],
            out_weight,
            up_weight,
            down_weight,
            second_gain,
            kern,
            groups,
            True,
            earlier,
            out_tokens,
        )
        words = after(mid[3], words)
        out_tokens, second_row = mid[0], mid[3]
        earlier = [*grads, second_row]
        mids.append(mid)
        arrived_back.append(across(pieces, -1, returned[-1], *arrived_back))
    u_keep, u_give, d_keep, d_give, out_t, gate_t = grads
    u_give, d_give = after(arrived_back[:-1], (u_give, d_give))
    wide_sums = Folding((u_keep, u_give), (d_keep, d_give))

    corrs, signal_back = [], []
    for b in seqs:
        corr = convolve(
            words, arrived_back[b], kern, kernel_spec, tabs, True, convs[b][1], b > 0
        )
        words = after(corr[1], words)
        corrs.append(corr)
        if b == 0:
            steps = wide_sums.step()
            words = after(steps, words)
            signal_back.append(across(corr[0], 1, steps))
        else:
            signal_back.append(across(corr[0], 1))

    wide_sums.hold(signal_back[0])
    words = after(wide_sums.step(), words)

    def write(word_ref, taps_ref, out_refs):
        for to, side in ((0, word_ref[1]), (1, 1 - word_ref[1])):
            for pair in range(groups // 2):
                for z in range(kern):
                    start = (z * groups + 2 * pair + side) * share
                    block = taps_ref[pl.ds(pl.multiple_of(start, share), share), :]
                    at = pair ^ own_pair(word_ref)
                    for h in range(2):
                        place = (flipped(at) if h == 0 else at, flipped(z ^ word_ref[0]))
                        half = block[h * share // 2 : (h + 1) * share // 2]
                        late_pack(out_refs[2 * h + to], place, half)

    shapes = [(groups // 2, kern, share // 4 * 3, 128)] * 4
    products = [corr[1] for corr in corrs]
    grad_taps = tap_gradient(words, products, limits, tabs, shapes, write)
    words = after(grad_taps, words)
    words = after(wide_sums.step(), words)

    late = late_gradients(
        words,
        signal_back,
        [head[0] for head in heads],
        gate_t,
        out_t,
        heads[-1][3],
        first_gain,
        second_row,
        grad_taps,
        kern,
        groups,
    )

    late_sums = Folding(late[:2], late[2:])
    grad_tokens = None
    for b in seqs:
        steps = late_sums.step()
        if b == 0:
            wide_sums.hold(steps)
            wide_sums.step()
        grad_tokens = finish(
            after(steps, words),
            b,
            tokens,
            mids[b][1],
            mids[b][2],
            signal_back[b],
            in_weight,
            first_gain,
            kern,
            grad_tokens,
        )
        late_sums.hold(grad_tokens)
    taps = jnp.stack(late_sums.take(late_packed), axis=1)
    steps = late_sums.step()
    taps = [taps[flipped(r)] for r in range(kern)]
    for r in range(1, kern):
        taps[r] = lax.ppermute(taps[r], "kern", [(i, i ^ r) for i in range(kern)])
    taps = late_unpack(jnp.stack(taps), share // 2).reshape(kern, share, chan)
    taps = jnp.concatenate(
        [lax.dynamic_index_in_dim(taps, me ^ z, 0, keepdims=False) for z in range(kern)], axis=1
    )
    taps = copies(taps)
    late_sums.hold(taps)
    wide_sums.hold(late_sums.step())
    up, down = wide_sums.totals()
    grad_taps = spread_out(taps, "dp").reshape(local_taps, feat)
    grad_raw = grad_taps.astype(f32) * slope

    sum_up = jnp.concatenate(jnp.split(up, 2, axis=1), axis=0)
    sum_down = down.T
    late = late_sums.totals()
    gains = late[1][late_free, 64:][: 2 * chan // 64].reshape(2, chan)
    late = jnp.concatenate([late_unpack(block, late_rows) for block in late], axis=0)
    sum_in = late[:in_rows].T
    sum_out = late[in_rows : in_rows + deep].T
    return (
        out_tokens,
        grad_tokens,
        sum_in,
        sum_out,
        sum_up,
        sum_down,
        gains[0],
        gains[1],
        grad_raw,
    )


def solution(mesh):
    placed = (
        P("dp", "kern", None),
        P("dp", "kern", None),
        P(),
        P(),
        P(),
        P(),
        P(),
        P(),
        P("kern", None),
        P(),
    )
    placed_out = (
        P("dp", "kern", None),
        P("dp", "kern", None),
        P("kern", "dp"),
        P("kern", "dp"),
        P("kern", "dp"),
        P("kern", "dp"),
        P("kern"),
        P("kern"),
        P("kern", None),
    )
    groups, kern = mesh.shape["dp"], mesh.shape["kern"]

    def layer(*arrays):
        seq_count, length, feat = arrays[0].shape
        seq_count = seq_count // groups
        width = arrays[4].shape[1]
        rows = length // kern
        tiles = (
            feat % (16 * groups) == 0
            and width % (128 * groups) == 0
            and width == groups // 2 * feat
            and groups == 8
            and kern == 4
            and rows % (2 * inner) == 0
            and 3 * feat // groups == 2 * late_rows
            and seq_count == 2
            and feat // kern == 192
            and arrays[8].shape[0] == 64 * groups * kern
        )
        return run(shards if tiles else shards_general)(*arrays)

    def run(body):
        return jax.shard_map(
            body,
            mesh=mesh,
            in_specs=placed,
            out_specs=placed_out,
            check_vma=False,
        )

    return layer
```
